32 devices in a mesh: row: 8 (over z, x), col: 4 (over y, core).
Axes of the slice: x: 2, y: 2, z: 4, core: 2. Of those that a mesh axis runs over, the one named last changes fastest.
Arguments:
- sources: float32 [128, 16384], P('col', 'row'), may hold values from -6 to 6
- tiles: bfloat16 [8, 4, 48, 256, 256], P('row', 'col')
- tile_row: int32 [8, 4, 48], P('row', 'col'), may hold values from 0 to 7
- tile_col: int32 [8, 4, 48], P('row', 'col'), may hold values from 0 to 15
- tile_count: int32 [8, 4], P('row', 'col'), may hold values from 1 to 48, as said below
Outputs:
- potential: float32 [128, 16384], P('col', 'row')
The draws below stay inside these ranges and needn't reach their ends.
Inputs may be any that keep to these rules, and one draw needn't show every extreme that they name: `tile_count`: slots at or past a device's count hold no part of the operator; some device holds exactly 48 live slots; tile pairs may repeat and then add.
All inputs are finite; a program needn't handle non-finite values.
Results may differ from the reference program's by a relative error of at most 0.0029.
Values may be sent and summed in bfloat16 or wider, within the bound.
No kernel may reach another device: no remote copies, remote signals or barrier semaphores. Data moves between devices by JAX's collectives and lax.ppermute only.
A program may use at most 128 MiB of HBM per device.

```python
import math
import jax
import jax.numpy as jnp
import numpy as np
from jax import lax

TILE = 256
R = 128
RB = 8
TPD = 48
NB = 64
CB = 16
NP = 16384
N_ROW = 8
N_COL = 4


def draw_tiles(key, part):
    base_key = jax.random.fold_in(key, 11)
    tile_shape = (N_ROW, N_COL, TPD, TILE, TILE)
    entries = jax.random.normal(base_key, tile_shape, jnp.float32)
    first_index = jnp.arange(TILE) == 0
    coarse_mask = first_index[:, None] | first_index[None, :]
    factor = jnp.where(coarse_mask, 4.0, 1.0).astype(jnp.float32)
    spread = 1.0 / math.sqrt(TILE * N_COL * TPD / RB)
    return (entries * factor * spread).astype(jnp.bfloat16)


def draw_tile_count(key, part):
    first_key = jax.random.fold_in(key, 21)
    second_key = jax.random.fold_in(key, 22)
    third_key = jax.random.fold_in(key, 23)
    first_draw = jax.random.randint(first_key, (N_ROW * N_COL,), 1, TPD + 1)
    second_draw = jax.random.randint(second_key, (N_ROW * N_COL,), 1, TPD + 1)
    lesser = jnp.minimum(first_draw, second_draw)
    chosen = jax.random.randint(third_key, (), 0, N_ROW * N_COL)
    filled = jnp.where(jnp.arange(N_ROW * N_COL) == chosen, TPD, lesser)
    return filled.reshape(N_ROW, N_COL).astype(jnp.int32)


def touch_ends(values, rng, smallest, high):
    spot = [jax.random.randint(jax.random.fold_in(rng, axis), (), 0, length) for axis, length in enumerate(values.shape)]
    widest = values.shape.index(max(values.shape))
    next_to = spot[:widest] + [(spot[widest] + 1) % values.shape[widest]] + spot[widest + 1:]
    return values.at[tuple(spot)].set(smallest).at[tuple(next_to)].set(high)


def shard_levels(stream_key, dims, shards, low, top_value):
    factor_of, own = 1.0, jax.random.fold_in(stream_key, 6)
    for dim, parts in shards:
        steps = jnp.exp(jax.random.uniform(jax.random.fold_in(own, dim), (parts,), jnp.float32, low / len(shards), top_value / len(shards)))
        factor_of = factor_of * jnp.repeat(steps, dims[dim] // parts).reshape([-1 if axis == dim else 1 for axis in range(len(dims))])
    return factor_of


def normal_values(own_key, dims, width, reach, shards=(), kind=jnp.bfloat16):
    array = jax.random.normal(own_key, dims, jnp.float32) * width
    if len(shards) > 0:
        array = shard_levels(own_key, dims, shards, -0.22, 0.18) * array
    return jnp.clip(array, min=-reach, max=reach).astype(kind)


def setup_inputs(seed: int = 0) -> dict:
    key_list = jax.random.split(jax.random.key(seed), 6)
    sources = normal_values(key_list[0], (R, NP), 1.0, 6.0, ((0, 4), (1, 8)), jnp.float32)
    tiles = draw_tiles(jax.random.fold_in(key_list[5], 71), 0)
    tile_row = touch_ends(jax.random.randint(key_list[2], (N_ROW, N_COL, TPD), 0, RB), jax.random.fold_in(key_list[2], 1), 0, RB - 1).astype(jnp.int32)
    tile_col = touch_ends(jax.random.randint(key_list[3], (N_ROW, N_COL, TPD), 0, CB), jax.random.fold_in(key_list[3], 1), 0, CB - 1).astype(jnp.int32)
    tile_count = draw_tile_count(jax.random.fold_in(key_list[5], 71), 0)
    return {"sources": sources, "tiles": tiles, "tile_row": tile_row, "tile_col": tile_col, "tile_count": tile_count}


ROOT_HALF = 1.0 / math.sqrt(2.0)

def haar_table(extent):
    matrix = np.eye(extent)
    stride = 1
    while stride < extent:
        for position in range(0, extent, 2 * stride):
            first_row = matrix[position].copy()
            second_row = matrix[position + stride].copy()
            matrix[position] = (first_row + second_row) * ROOT_HALF
            matrix[position + stride] = (first_row - second_row) * ROOT_HALF
        stride = stride * 2
    return matrix

def pair_step(values, stride):
    height, extent = values.shape
    shaped = values.reshape(height, extent // (2 * stride), 2, stride)
    first_part = shaped[:, :, 0, 0]
    second_part = shaped[:, :, 1, 0]
    shaped = shaped.at[:, :, 0, 0].set((first_part + second_part) * ROOT_HALF)
    shaped = shaped.at[:, :, 1, 0].set((first_part - second_part) * ROOT_HALF)
    return shaped.reshape(height, extent)

def haar_forward(values):
    stride = 1
    while stride < values.shape[1]:
        values = pair_step(values, stride)
        stride = stride * 2
    return values

def haar_inverse(values):
    stride = values.shape[1] // 2
    while stride >= 1:
        values = pair_step(values, stride)
        stride = stride // 2
    return values

def reference(sources, tiles, tile_row, tile_col, tile_count):
    haar_matrix = jnp.asarray(haar_table(TILE), jnp.float32)
    shaped = sources.reshape(R, NB, TILE)
    local_coef = jnp.einsum('rbk,nk->rbn', shaped, haar_matrix, precision=lax.Precision.HIGHEST)
    scaling = haar_forward(local_coef[:, :, 0])
    wavelet = local_coef.at[:, :, 0].set(scaling).astype(jnp.bfloat16)
    group_offsets = (jnp.arange(N_COL, dtype=jnp.int32) * CB)[:, None]

    def one_row(carried, inputs):
        row_tiles, row_rows, row_cols, row_counts = inputs
        global_cols = (row_cols + group_offsets).reshape(-1)
        side_blocks = jnp.take(wavelet, global_cols, axis=1).astype(jnp.float32)
        stack = row_tiles.reshape(N_COL * TPD, TILE, TILE).astype(jnp.float32)
        product = jnp.einsum('rtk,tkn->rtn', side_blocks, stack, precision=lax.Precision.HIGHEST)
        usable = (jnp.arange(TPD, dtype=jnp.int32)[None, :] < row_counts[:, None]).reshape(-1)
        select = ((row_rows.reshape(-1)[:, None] == jnp.arange(RB, dtype=jnp.int32)[None, :]) & usable[:, None]).astype(jnp.float32)
        return (carried, jnp.einsum('ti,rtn->rin', select, product, precision=lax.Precision.HIGHEST))
    ignored, stacked = lax.scan(one_row, jnp.zeros((), jnp.float32), (tiles, tile_row, tile_col, tile_count))
    image_coef = jnp.transpose(stacked, (1, 0, 2, 3)).reshape(R, NB, TILE)
    back_scaling = haar_inverse(image_coef[:, :, 0])
    image_coef = image_coef.at[:, :, 0].set(back_scaling)
    result = jnp.einsum('rbn,nk->rbk', image_coef, haar_matrix, precision=lax.Precision.HIGHEST)
    return result.reshape(R, NP)
```

```python
import functools
import math

import jax
import jax.numpy as jnp
import numpy as np
from jax import lax
from jax.experimental import pallas as pl
from jax.experimental.pallas import tpu as pltpu
from jax.sharding import PartitionSpec as P

ROOT_HALF = 1.0 / math.sqrt(2.0)
SIDE_ROWS = 16
SLOT_GROUP = 8
MIB = 2**20


def haar_table(extent):
    matrix = np.eye(extent)
    stride = 1
    while stride < extent:
        for position in range(0, extent, 2 * stride):
            first_row = matrix[position].copy()
            second_row = matrix[position + stride].copy()
            matrix[position] = (first_row + second_row) * ROOT_HALF
            matrix[position + stride] = (first_row - second_row) * ROOT_HALF
        stride = stride * 2
    return matrix


def haar_parts(extent):
    matrix = haar_table(extent)
    scale = np.max(np.abs(matrix), axis=1)
    signs = np.round(matrix / scale[:, None])
    return signs.T, scale[None, :]


def three_terms(value):
    high = value.astype(jnp.bfloat16)
    rest = value - high.astype(jnp.float32)
    middle = rest.astype(jnp.bfloat16)
    low = (rest - middle.astype(jnp.float32)).astype(jnp.bfloat16)
    return high, middle, low


def exact_dot(value, signs):
    return sum(jnp.dot(term, signs, preferred_element_type=jnp.float32) for term in three_terms(value))


def block_forward(columns):
    columns = list(columns)
    stride = 1
    while stride < len(columns):
        for p in range(0, len(columns), 2 * stride):
            u, v = columns[p], columns[p + stride]
            columns[p], columns[p + stride] = (u + v) * ROOT_HALF, (u - v) * ROOT_HALF
        stride *= 2
    return columns


def block_inverse(columns):
    columns = list(columns)
    stride = len(columns) // 2
    while stride >= 1:
        for p in range(0, len(columns), 2 * stride):
            u, v = columns[p], columns[p + stride]
            columns[p], columns[p + stride] = (u + v) * ROOT_HALF, (u - v) * ROOT_HALF
        stride //= 2
    return columns


def front_kernel(core_ref, mine_ref, other_ref, signs_ref, scale_ref, out_ref, *, blocks, extent):
    height = mine_ref.shape[0]
    pair = 2 * height
    mine, other = mine_ref[...], other_ref[...]
    first_core = core_ref[0] == 0
    both = jnp.concatenate([jnp.where(first_core, mine, other), jnp.where(first_core, other, mine)], axis=0)
    parts = [both[:, b * extent : (b + 1) * extent] for b in range(blocks)]
    coef = exact_dot(jnp.concatenate(parts, axis=0), signs_ref[...]) * scale_ref[...]
    columns = block_forward([coef[b * pair : (b + 1) * pair, 0:1] for b in range(blocks)])
    lane = lax.broadcasted_iota(jnp.int32, (pair, extent), 1)
    for b in range(blocks):
        column = jnp.zeros_like(columns[0]) if b == 0 else columns[b]
        block = jnp.where(lane == 0, column, coef[b * pair : (b + 1) * pair, :])
        out_ref[b * pair : (b + 1) * pair, :] = block.astype(jnp.bfloat16)
    total = functools.reduce(jnp.add, parts)
    ones = jnp.ones((SIDE_ROWS, extent), jnp.bfloat16)
    first = sum(
        lax.dot_general(ones, term, (((1,), (1,)), ((), ())), preferred_element_type=jnp.float32)
        for term in three_terms(total)
    ) * (1.0 / math.sqrt(blocks * extent))
    high, middle, low = (term.astype(jnp.float32) for term in three_terms(first))
    row = lax.broadcasted_iota(jnp.int32, first.shape, 0)
    side = jnp.where(row == 0, high, jnp.where(row == 1, middle, jnp.where(row == 2, low, 0.0)))
    out_ref[blocks * pair :, :] = jnp.zeros((SIDE_ROWS, extent), jnp.bfloat16)
    out_ref[blocks * pair :, 0:pair] = side.astype(jnp.bfloat16)


def edge_kernel(rows_ref, cols_ref, count_ref, tiles_ref, first_cols_ref, first_row_ref, *, blocks):
    step = pl.program_id(0)
    extent = tiles_ref.shape[-1]

    @pl.when(step == 0)
    def _():
        first_cols_ref[...] = jnp.zeros_like(first_cols_ref)
        first_row_ref[...] = jnp.zeros_like(first_row_ref)

    pick = (lax.broadcasted_iota(jnp.int32, (SIDE_ROWS, extent), 1) == 0).astype(jnp.bfloat16)
    for s in range(SLOT_GROUP):
        slot = step * SLOT_GROUP + s
        live = slot < count_ref[0]
        row, col = rows_ref[slot], cols_ref[slot]

        @pl.when(live & (lax.rem(col, blocks) == 0))
        def _():
            at = pl.ds(col + row, 1)
            first_cols_ref[at, :] += tiles_ref[s, 0:SIDE_ROWS, :].astype(jnp.float32)[0:1, :]

        @pl.when(live & (row == 0))
        def _():
            column = lax.dot_general(
                pick, tiles_ref[s], (((1,), (1,)), ((), ())), preferred_element_type=jnp.float32
            )
            first_row_ref[pl.ds(col, 1), :] += column[0:1, :]


def product_kernel(
    rows_ref, cols_ref, count_ref, place_ref, tiles_ref, first_cols_ref, first_row_ref, *refs, blocks, owners, spans
):
    messages = refs[: owners * spans]
    keep_ref, send_ref, sides, acc, firsts = refs[owners * spans :]
    step = pl.program_id(0)
    extent = tiles_ref.shape[-1]
    pair = sides.shape[1] // spans
    height = pair // 2

    @pl.when(step == 0)
    def _():
        for index, message in enumerate(messages):
            owner, at = place_ref[2 * index + 1], place_ref[2 * index + 2]
            rows = pl.ds(pl.multiple_of(at * pair, pair), pair)
            for b in range(blocks):
                sides[owner * blocks + b, rows, :] = message[b * pair : (b + 1) * pair, :]
            side = jnp.transpose(message[blocks * pair :, :].astype(jnp.float32))
            column = side[0:pair, 0:1] + side[0:pair, 1:2] + side[0:pair, 2:3]
            firsts[owner, rows, :] = jnp.broadcast_to(column, (pair, firsts.shape[2]))
        lane = lax.broadcasted_iota(jnp.int32, (1, extent), 1)
        for i in range(blocks):
            total = jnp.zeros(acc.shape[1:], jnp.float32)
            for owner in range(owners):
                line = first_cols_ref[owner * blocks + i : owner * blocks + i + 1, :]
                if i == 0:
                    line = jnp.where(lane == 0, 0.0, line)
                total += firsts[owner][:, 0:1] * line
            acc[i] = total

    count = count_ref[0]
    for s in range(SLOT_GROUP):
        slot = step * SLOT_GROUP + s

        @pl.when(slot < count)
        def _():
            row, col = rows_ref[slot], cols_ref[slot]
            acc[row] += jnp.dot(sides[col], tiles_ref[s], preferred_element_type=jnp.float32)

    @pl.when(step == pl.num_programs(0) - 1)
    def _():
        total = jnp.zeros(acc.shape[1:], jnp.float32)
        for b in range(blocks * owners):
            total += sides[b].astype(jnp.float32) * first_row_ref[b : b + 1, :]
        top = jnp.sum(total, axis=1, keepdims=True)
        for owner in range(owners):
            top += firsts[owner][:, 0:1] * first_row_ref[owner * blocks : owner * blocks + 1, 0:1]
        lane = lax.broadcasted_iota(jnp.int32, acc.shape[1:], 1)
        acc[0] = jnp.where(lane == 0, top, acc[0])
        first_core = place_ref[0] == 0
        for i in range(blocks):
            value = acc[i]
            for y in range(spans):
                one = value[y * pair : y * pair + height, :]
                two = value[y * pair + height : (y + 1) * pair, :]
                keep_ref[y, i] = jnp.where(first_core, one, two)
                send_ref[y, i] = jnp.where(first_core, two, one)


def combine_kernel(span_ref, keep_ref, arrived_ref, own_ref, *out_refs):
    spans = keep_ref.shape[0]
    span = span_ref[0]
    own_ref[...] = keep_ref[span] + arrived_ref[span]
    for j, out_ref in enumerate(out_refs, 1):
        at = lax.rem(span + j, spans)
        out_ref[...] = (keep_ref[at] + arrived_ref[at]).astype(jnp.bfloat16)


def back_kernel(own_ref, *refs):
    *arrived, signs_ref, scale_ref, out_ref = refs
    blocks, height, extent = own_ref.shape
    total = own_ref[...]
    for part in arrived:
        total = total + part[...].astype(jnp.float32)
    columns = block_inverse([total[b][:, 0:1] for b in range(blocks)])
    lane = lax.broadcasted_iota(jnp.int32, (height, extent), 1)
    fixed = jnp.concatenate([jnp.where(lane == 0, columns[b], total[b]) for b in range(blocks)], axis=0)
    result = exact_dot(fixed * scale_ref[...], signs_ref[...])
    for b in range(blocks):
        out_ref[:, b * extent : (b + 1) * extent] = result[b * height : (b + 1) * height, :]


def butterfly(value, partner, index, bit):
    active = index % 2**bit == 0
    upper = index // 2**bit % 2 == 1
    combined = jnp.where(upper, partner - value, partner + value) * ROOT_HALF
    return jnp.where(active, combined, value)


def inverse_cross(value, axis):
    size = lax.axis_size(axis)
    index = lax.axis_index(axis)
    for bit in reversed(range(size.bit_length() - 1)):
        pairs = [(source, source ^ 2**bit) for source in range(size)]
        value = butterfly(value, lax.ppermute(value, axis, pairs), index, bit)
    return value


def local(sources, tiles, tile_row, tile_col, tile_count):
    n_row, n_col = lax.axis_size("row"), lax.axis_size("col")
    owners = n_row // n_col
    spans = n_col // 2
    extent = tiles.shape[-1]
    slots = tiles.shape[2]
    height = sources.shape[0]
    blocks = sources.shape[1] // extent
    pair = 2 * height
    row_index, col_index = lax.axis_index("row"), lax.axis_index("col")
    z, x = row_index // owners, row_index % owners
    span, core = col_index // 2, col_index % 2
    signs, scale = haar_parts(extent)

    def moved(value, to):
        pairs = []
        for a in range(n_row):
            for b in range(n_col):
                zz, xx, yy, cc = to(a // owners, a % owners, b // 2, b % 2)
                pairs.append((a * n_col + b, (zz * owners + xx) * n_col + yy * 2 + cc))
        return lax.ppermute(value, ("row", "col"), pairs)

    def other_core(value):
        return moved(value, lambda zz, xx, yy, cc: (zz, xx, yy, 1 - cc))

    smem = pl.BlockSpec(memory_space=pltpu.SMEM)
    vmem = pl.BlockSpec(memory_space=pltpu.VMEM)

    message = pl.pallas_call(
        functools.partial(front_kernel, blocks=blocks, extent=extent),
        out_shape=jax.ShapeDtypeStruct((blocks * pair + SIDE_ROWS, extent), jnp.bfloat16),
        in_specs=[smem, vmem, vmem, vmem, vmem],
        out_specs=vmem,
        name="front",
        compiler_params=pltpu.CompilerParams(vmem_limit_bytes=16 * MIB),
        cost_estimate=pl.CostEstimate(flops=6 * blocks * pair * extent * extent, bytes_accessed=MIB, transcendentals=0),
    )(
        core.astype(jnp.int32).reshape(1),
        sources,
        other_core(sources),
        jnp.asarray(signs, jnp.bfloat16),
        jnp.asarray(scale, jnp.float32),
    )

    pieces, places = [], [core]
    direct = [
        moved(message, lambda zz, xx, yy, cc, m=m: (cc * spans + (yy + m) % spans, xx, zz // 2, zz % 2))
        for m in range(spans)
    ]
    for m in range(spans):
        came_from = (z % spans - m) % spans
        pieces.append(direct[m])
        places += [x, came_from]
        for j in range(1, owners):
            pieces.append(moved(direct[m], lambda zz, xx, yy, cc, j=j: (zz, (xx + j) % owners, yy, cc)))
            places += [(x - j) % owners, came_from]

    stack = tiles.reshape(slots, extent, extent)
    rows_flat, cols_flat = tile_row.reshape(-1), tile_col.reshape(-1)
    count = tile_count.reshape(1)
    steps = slots // SLOT_GROUP

    def tile_block(step, rows_ref, cols_ref, count_ref, *_):
        return jnp.minimum(step, (count_ref[0] - 1) // SLOT_GROUP), 0, 0

    first_cols, first_row = pl.pallas_call(
        functools.partial(edge_kernel, blocks=blocks),
        out_shape=[
            jax.ShapeDtypeStruct((owners * blocks, extent), jnp.float32),
            jax.ShapeDtypeStruct((owners * blocks, extent), jnp.float32),
        ],
        grid_spec=pltpu.PrefetchScalarGridSpec(
            num_scalar_prefetch=3,
            grid=(steps,),
            in_specs=[pl.BlockSpec((SLOT_GROUP, extent, extent), tile_block)],
            out_specs=[pl.BlockSpec((owners * blocks, extent), lambda *_: (0, 0))] * 2,
        ),
        name="edges",
        compiler_params=pltpu.CompilerParams(vmem_limit_bytes=16 * MIB),
        cost_estimate=pl.CostEstimate(flops=0, bytes_accessed=stack.size * 2, transcendentals=0),
    )(rows_flat, cols_flat, count, stack)

    by_owner = first_cols.reshape(owners, blocks, extent)
    by_owner = block_inverse([inverse_cross(by_owner[0], "col")] + [by_owner[i] for i in range(1, owners)])
    first_cols = jnp.concatenate(by_owner, axis=0)
    corner = jnp.stack([part[0, 0] for part in by_owner])
    first_row = inverse_cross(first_row.at[::blocks, 0].set(corner), "row")

    shape = (spans, blocks, height, extent)
    whole = lambda *dims: pl.BlockSpec(dims, lambda *_: (0,) * len(dims))
    keep, send = pl.pallas_call(
        functools.partial(product_kernel, blocks=blocks, owners=owners, spans=spans),
        out_shape=[jax.ShapeDtypeStruct(shape, jnp.float32)] * 2,
        grid_spec=pltpu.PrefetchScalarGridSpec(
            num_scalar_prefetch=4,
            grid=(steps,),
            in_specs=[
                pl.BlockSpec((SLOT_GROUP, extent, extent), tile_block),
                whole(owners * blocks, extent),
                whole(owners * blocks, extent),
            ]
            + [whole(blocks * pair + SIDE_ROWS, extent)] * (owners * spans),
            out_specs=[whole(*shape)] * 2,
            scratch_shapes=[
                pltpu.VMEM((owners * blocks, spans * pair, extent), jnp.bfloat16),
                pltpu.VMEM((blocks, spans * pair, extent), jnp.float32),
                pltpu.VMEM((owners, spans * pair, 128), jnp.float32),
            ],
        ),
        name="products",
        compiler_params=pltpu.CompilerParams(vmem_limit_bytes=32 * MIB),
        cost_estimate=pl.CostEstimate(
            flops=2 * slots * spans * pair * extent * extent, bytes_accessed=stack.size * 2, transcendentals=0
        ),
    )(rows_flat, cols_flat, count, jnp.stack(places).astype(jnp.int32), stack, first_cols, first_row, *pieces)

    part = jax.ShapeDtypeStruct(shape[1:], jnp.bfloat16)
    own, *outgoing = pl.pallas_call(
        combine_kernel,
        out_shape=[jax.ShapeDtypeStruct(shape[1:], jnp.float32)] + [part] * (spans - 1),
        in_specs=[smem, vmem, vmem],
        out_specs=[vmem] * spans,
        name="combine",
        compiler_params=pltpu.CompilerParams(vmem_limit_bytes=16 * MIB),
    )(span.astype(jnp.int32).reshape(1), keep, other_core(send))
    arrived = [
        moved(value, lambda zz, xx, yy, cc, j=j: (zz, xx, (yy + j) % spans, cc)) for j, value in enumerate(outgoing, 1)
    ]
    return pl.pallas_call(
        back_kernel,
        out_shape=jax.ShapeDtypeStruct(sources.shape, jnp.float32),
        in_specs=[vmem] * (spans + 2),
        out_specs=vmem,
        name="back",
        compiler_params=pltpu.CompilerParams(vmem_limit_bytes=16 * MIB),
    )(own, *arrived, jnp.asarray(signs.T, jnp.bfloat16), jnp.asarray(scale, jnp.float32))


def solution(mesh):
    return jax.shard_map(
        local,
        mesh=mesh,
        in_specs=(
            P("col", "row"),
            P("row", "col", None, None, None),
            P("row", "col", None),
            P("row", "col", None),
            P("row", "col"),
        ),
        out_specs=P("col", "row"),
        check_vma=False,
    )
```

```python
import functools
import math

import jax
import jax.numpy as jnp
import numpy as np
from jax import lax
from jax.experimental import pallas as pl
from jax.experimental.pallas import tpu as pltpu
from jax.sharding import PartitionSpec as P

ROOT_HALF = 1.0 / math.sqrt(2.0)
SIDE_ROWS = 16
CHUNKS = 2
UNROLL = 4
MIB = 2**20


def haar_table(extent):
    matrix = np.eye(extent)
    stride = 1
    while stride < extent:
        for position in range(0, extent, 2 * stride):
            first_row = matrix[position].copy()
            second_row = matrix[position + stride].copy()
            matrix[position] = (first_row + second_row) * ROOT_HALF
            matrix[position + stride] = (first_row - second_row) * ROOT_HALF
        stride = stride * 2
    return matrix


def haar_parts(extent):
    matrix = haar_table(extent)
    scale = np.max(np.abs(matrix), axis=1)
    signs = np.round(matrix / scale[:, None])
    return signs.T, scale[None, :]


def three_terms(value):
    high = value.astype(jnp.bfloat16)
    rest = value - high.astype(jnp.float32)
    middle = rest.astype(jnp.bfloat16)
    low = (rest - middle.astype(jnp.float32)).astype(jnp.bfloat16)
    return high, middle, low


def exact_dot(value, signs):
    return sum(jnp.dot(term, signs, preferred_element_type=jnp.float32) for term in three_terms(value))


def block_forward(columns):
    columns = list(columns)
    stride = 1
    while stride < len(columns):
        for p in range(0, len(columns), 2 * stride):
            u, v = columns[p], columns[p + stride]
            columns[p], columns[p + stride] = (u + v) * ROOT_HALF, (u - v) * ROOT_HALF
        stride *= 2
    return columns


def block_inverse(columns):
    columns = list(columns)
    stride = len(columns) // 2
    while stride >= 1:
        for p in range(0, len(columns), 2 * stride):
            u, v = columns[p], columns[p + stride]
            columns[p], columns[p + stride] = (u + v) * ROOT_HALF, (u - v) * ROOT_HALF
        stride //= 2
    return columns


def front_kernel(core_ref, mine_ref, other_ref, signs_ref, scale_ref, *out_refs, blocks, extent):
    height = mine_ref.shape[0]
    pair = 2 * height
    mine, other = mine_ref[...], other_ref[...]
    first_core = core_ref[0] == 0
    both = jnp.concatenate([jnp.where(first_core, mine, other), jnp.where(first_core, other, mine)], axis=0)
    parts = [both[:, b * extent : (b + 1) * extent] for b in range(blocks)]
    coef = exact_dot(jnp.concatenate(parts, axis=0), signs_ref[...]) * scale_ref[...]
    columns = block_forward([coef[b * pair : (b + 1) * pair, 0:1] for b in range(blocks)])
    lane = lax.broadcasted_iota(jnp.int32, (pair, extent), 1)
    held = blocks // len(out_refs)
    for b in range(blocks):
        column = jnp.zeros_like(columns[0]) if b == 0 else columns[b]
        block = jnp.where(lane == 0, column, coef[b * pair : (b + 1) * pair, :])
        at = b % held * pair
        out_refs[b // held][at : at + pair, :] = block.astype(jnp.bfloat16)
    total = functools.reduce(jnp.add, parts)
    ones = jnp.ones((SIDE_ROWS, extent), jnp.bfloat16)
    first = sum(
        lax.dot_general(ones, term, (((1,), (1,)), ((), ())), preferred_element_type=jnp.float32)
        for term in three_terms(total)
    ) * (1.0 / math.sqrt(blocks * extent))
    high, middle, low = (term.astype(jnp.float32) for term in three_terms(first))
    row = lax.broadcasted_iota(jnp.int32, first.shape, 0)
    side = jnp.where(row == 0, high, jnp.where(row == 1, middle, jnp.where(row == 2, low, 0.0)))
    out_refs[-1][held * pair :, :] = jnp.zeros((SIDE_ROWS, extent), jnp.bfloat16)
    out_refs[-1][held * pair :, 0:pair] = side.astype(jnp.bfloat16)


def edge_kernel(
    place_ref, rows_ref, cols_ref, count_ref, tiles_ref, _, lead_ref, rest_ref, row_ref, order_ref, sizes_ref, *, blocks, owners
):
    extent = tiles_ref.shape[-1]
    lead_ref[...] = jnp.zeros_like(lead_ref)
    rest_ref[...] = jnp.zeros_like(rest_ref)
    row_ref[...] = jnp.zeros_like(row_ref)
    pick = (lax.broadcasted_iota(jnp.int32, (SIDE_ROWS, extent), 1) == 0).astype(jnp.bfloat16)
    x = place_ref[2]

    def visit(slot, sizes):
        row, col = rows_ref[slot], cols_ref[slot]
        owner, block = col // blocks, lax.rem(col, blocks)

        @pl.when((block == 0) & (owner == 0))
        def _():
            lead_ref[pl.ds(row, 1), :] += tiles_ref[slot, 0:SIDE_ROWS, :].astype(jnp.float32)[0:1, :]

        @pl.when((block == 0) & (owner > 0))
        def _():
            at = pl.ds((owner - 1) * blocks + row, 1)
            rest_ref[at, :] += tiles_ref[slot, 0:SIDE_ROWS, :].astype(jnp.float32)[0:1, :]

        @pl.when(row == 0)
        def _():
            column = lax.dot_general(
                pick, tiles_ref[slot], (((1,), (1,)), ((), ())), preferred_element_type=jnp.float32
            )
            row_ref[pl.ds(col, 1), :] += column[0:1, :]

        behind = lax.rem(x - owner + owners, owners)
        side = jnp.where(behind == 0, block, (behind - 1) * blocks + block)
        entry = (slot * 256 + side) * 256 + row
        own = (behind == 0).astype(jnp.int32)
        order_ref[1 - own, jnp.where(own == 1, sizes[0], sizes[1])] = entry
        return sizes[0] + own, sizes[1] + 1 - own

    sizes = lax.fori_loop(0, count_ref[0], visit, (jnp.int32(0), jnp.int32(0)))
    for which in range(2):
        sizes_ref[which] = sizes[which]
        for k in range(UNROLL - 1):
            order_ref[which, sizes[which] + k] = blocks


def corner_kernel(place_ref, lead_ref, partner_ref, rest_ref, row_ref, cols_ref, fixed_ref, *, blocks, owners):
    lead, partner = lead_ref[...], partner_ref[...]
    combined = jnp.where(place_ref[0] == 1, partner - lead, partner + lead) * ROOT_HALF
    lines = [combined] + [rest_ref[i * blocks : (i + 1) * blocks, :] for i in range(owners - 1)]
    lines = block_inverse(lines)
    fixed = row_ref[...]
    index = lax.broadcasted_iota(jnp.int32, fixed.shape, 0)
    lane = lax.broadcasted_iota(jnp.int32, fixed.shape, 1)
    for i, line in enumerate(lines):
        cols_ref[i * blocks : (i + 1) * blocks, :] = line
        fixed = jnp.where((index == i * blocks) & (lane == 0), line[0:1, 0:1], fixed)
    fixed_ref[...] = fixed


def fill_sides(sides, messages, place_ref, chunks, blocks, spans):
    pair = sides.shape[1] // spans
    held = blocks // chunks
    for index, message in enumerate(messages):
        behind, m, chunk = index // (spans * chunks), index // chunks % spans, index % chunks
        rows = pl.ds(pl.multiple_of(place_ref[3 + m] * pair, pair), pair)
        for b in range(held):
            sides[behind * blocks + chunk * held + b, rows, :] = message[b * pair : (b + 1) * pair, :]


def add_products(order_ref, sizes_ref, which, tiles_ref, sides, acc):
    def group(index, _):
        for k in range(UNROLL):
            entry = order_ref[which, index * UNROLL + k]
            slot, side, row = entry >> 16, (entry >> 8) & 255, entry & 255
            acc[row] += jnp.dot(sides[side], tiles_ref[slot], preferred_element_type=jnp.float32)
        return 0

    lax.fori_loop(0, (sizes_ref[which] + UNROLL - 1) // UNROLL, group, 0)


def near_kernel(place_ref, order_ref, sizes_ref, tiles_ref, *refs, blocks, spans, chunks):
    *messages, acc_ref, sides = refs
    fill_sides(sides, messages, place_ref, chunks, blocks, spans)
    acc_ref[...] = jnp.zeros_like(acc_ref)
    add_products(order_ref, sizes_ref, 0, tiles_ref, sides, acc_ref)


def far_kernel(
    place_ref, order_ref, sizes_ref, tiles_ref, near_ref, cols_ref, row_ref, *refs, blocks, owners, spans, chunks
):
    direct, swapped = refs[: spans * chunks], refs[spans * chunks : owners * spans * chunks]
    keep_ref, send_ref, sides, acc, firsts = refs[owners * spans * chunks :]
    extent = tiles_ref.shape[-1]
    pair = sides.shape[1] // spans
    height = pair // 2
    held = blocks // chunks
    x = place_ref[2]
    fill_sides(sides, swapped, place_ref, chunks, blocks, spans)
    messages = (*direct, *swapped)
    for behind in range(owners):
        owner = lax.rem(x - behind + owners, owners)
        for m in range(spans):
            message = messages[(behind * spans + m) * chunks + chunks - 1]
            side = jnp.transpose(message[held * pair :, :].astype(jnp.float32))
            column = side[0:pair, 0:1] + side[0:pair, 1:2] + side[0:pair, 2:3]
            rows = pl.ds(pl.multiple_of(place_ref[3 + m] * pair, pair), pair)
            firsts[owner, rows, :] = jnp.broadcast_to(column, (pair, firsts.shape[2]))
    for i in range(blocks):
        total = near_ref[i]
        for owner in range(owners):
            total += firsts[owner][:, 0:1] * cols_ref[owner * blocks + i : owner * blocks + i + 1, :]
        acc[i] = total
    add_products(order_ref, sizes_ref, 1, tiles_ref, sides, acc)

    lane = lax.broadcasted_iota(jnp.int32, (pair, extent), 1)
    for m in range(spans):
        rows = pl.ds(pl.multiple_of(place_ref[3 + m] * pair, pair), pair)
        total = jnp.zeros((pair, extent), jnp.float32)
        top = jnp.zeros((pair, 1), jnp.float32)
        for behind in range(owners):
            owner = lax.rem(x - behind + owners, owners)
            for b in range(blocks):
                message = messages[(behind * spans + m) * chunks + b // held]
                at = b % held * pair
                line = row_ref[pl.ds(owner * blocks + b, 1), :]
                total += message[at : at + pair, :].astype(jnp.float32) * line
                if b == 0:
                    top += firsts[owner, rows, :][:, 0:1] * line[:, 0:1]
        top += jnp.sum(total, axis=1, keepdims=True)
        acc[0, rows, :] = jnp.where(lane == 0, top, acc[0, rows, :])
    first_core = place_ref[0] == 0
    for i in range(blocks):
        value = acc[i]
        for y in range(spans):
            one = value[y * pair : y * pair + height, :]
            two = value[y * pair + height : (y + 1) * pair, :]
            keep_ref[y, i] = jnp.where(first_core, one, two)
            send_ref[y, i] = jnp.where(first_core, two, one)


def combine_kernel(place_ref, keep_ref, arrived_ref, own_ref, *out_refs):
    spans = keep_ref.shape[0]
    span = place_ref[1]
    own_ref[...] = keep_ref[span] + arrived_ref[span]
    for j, out_ref in enumerate(out_refs, 1):
        at = lax.rem(span + j, spans)
        out_ref[...] = (keep_ref[at] + arrived_ref[at]).astype(jnp.bfloat16)


def back_kernel(own_ref, *refs):
    *arrived, signs_ref, scale_ref, out_ref = refs
    blocks, height, extent = own_ref.shape
    total = own_ref[...]
    for part in arrived:
        total = total + part[...].astype(jnp.float32)
    columns = block_inverse([total[b][:, 0:1] for b in range(blocks)])
    lane = lax.broadcasted_iota(jnp.int32, (height, extent), 1)
    fixed = jnp.concatenate([jnp.where(lane == 0, columns[b], total[b]) for b in range(blocks)], axis=0)
    result = exact_dot(fixed * scale_ref[...], signs_ref[...])
    for b in range(blocks):
        out_ref[:, b * extent : (b + 1) * extent] = result[b * height : (b + 1) * height, :]


def butterfly(value, partner, index, bit):
    active = index % 2**bit == 0
    upper = index // 2**bit % 2 == 1
    combined = jnp.where(upper, partner - value, partner + value) * ROOT_HALF
    return jnp.where(active, combined, value)


def local(sources, tiles, tile_row, tile_col, tile_count):
    n_row, n_col = lax.axis_size("row"), lax.axis_size("col")
    owners = n_row // n_col
    spans = n_col // 2
    extent = tiles.shape[-1]
    slots = tiles.shape[2]
    height = sources.shape[0]
    blocks = sources.shape[1] // extent
    pair = 2 * height
    held = blocks // CHUNKS
    row_index, col_index = lax.axis_index("row"), lax.axis_index("col")
    z, x = row_index // owners, row_index % owners
    span, core = col_index // 2, col_index % 2
    signs, scale = haar_parts(extent)

    def moved(value, to):
        pairs = []
        for a in range(n_row):
            for b in range(n_col):
                zz, xx, yy, cc = to(a // owners, a % owners, b // 2, b % 2)
                pairs.append((a * n_col + b, (zz * owners + xx) * n_col + yy * 2 + cc))
        return lax.ppermute(value, ("row", "col"), pairs)

    def other_core(value):
        return moved(value, lambda zz, xx, yy, cc: (zz, xx, yy, 1 - cc))

    def along_x(value, j):
        return moved(value, lambda zz, xx, yy, cc: (zz, (xx + j) % owners, yy, cc))

    smem = pl.BlockSpec(memory_space=pltpu.SMEM)
    vmem = pl.BlockSpec(memory_space=pltpu.VMEM)

    def call(kernel, name, out_shape, in_specs, out_specs, limit=16, scratch=(), flops=0, moved_bytes=MIB, **sizes):
        return pl.pallas_call(
            functools.partial(kernel, **sizes) if sizes else kernel,
            out_shape=out_shape,
            in_specs=in_specs,
            out_specs=out_specs,
            scratch_shapes=scratch,
            name=name,
            compiler_params=pltpu.CompilerParams(vmem_limit_bytes=limit * MIB),
            cost_estimate=pl.CostEstimate(flops=flops, bytes_accessed=moved_bytes, transcendentals=0),
        )

    def f32(*dims):
        return jax.ShapeDtypeStruct(dims, jnp.float32)

    def bf16(*dims):
        return jax.ShapeDtypeStruct(dims, jnp.bfloat16)

    place = jnp.stack([core, span, x] + [(z - m) % spans for m in range(spans)]).astype(jnp.int32)

    messages = call(
        front_kernel,
        "front",
        [bf16(held * pair + (SIDE_ROWS if q == CHUNKS - 1 else 0), extent) for q in range(CHUNKS)],
        [smem, vmem, vmem, vmem, vmem],
        [vmem] * CHUNKS,
        blocks=blocks,
        extent=extent,
    )(place, sources, other_core(sources), jnp.asarray(signs, jnp.bfloat16), jnp.asarray(scale, jnp.float32))

    direct = [
        moved(messages[q], lambda zz, xx, yy, cc, m=m: (cc * spans + (yy + m) % spans, xx, zz // 2, zz % 2))
        for m in range(spans)
        for q in range(CHUNKS)
    ]
    swapped = [along_x(piece, j) for j in range(1, owners) for piece in direct]

    stack = tiles.reshape(slots, extent, extent)
    rows_flat, cols_flat = tile_row.reshape(-1), tile_col.reshape(-1)
    lead, rest, first_row, order, sizes = call(
        edge_kernel,
        "edges",
        [
            f32(blocks, extent),
            f32((owners - 1) * blocks, extent),
            f32(owners * blocks, extent),
            jax.ShapeDtypeStruct((2, slots + UNROLL), jnp.int32),
            jax.ShapeDtypeStruct((2,), jnp.int32),
        ],
        [smem] * 4 + [vmem, pl.BlockSpec(memory_space=pl.ANY)],
        [vmem] * 3 + [smem] * 2,
        blocks=blocks,
        owners=owners,
    )(place, rows_flat, cols_flat, tile_count.reshape(1), stack, messages[0])

    for bit in reversed(range(1, n_col.bit_length() - 1)):
        step = 2 ** (bit - 1)
        partner = moved(lead, lambda zz, xx, yy, cc, step=step: (zz, xx, yy ^ step, cc))
        lead = butterfly(lead, partner, col_index, bit)
    first_cols, first_row = call(
        corner_kernel,
        "corner",
        [f32(owners * blocks, extent)] * 2,
        [smem] + [vmem] * 4,
        [vmem] * 2,
        blocks=blocks,
        owners=owners,
    )(place, lead, other_core(lead), rest, first_row)
    behind = [first_row] + [along_x(first_row, j) for j in range(1, owners)]
    by_x = []
    for i in range(owners):
        line = behind[0]
        for j in range(1, owners):
            line = jnp.where((x - i) % owners == j, behind[j], line)
        by_x.append(line)
    for bit in reversed(range((n_row // owners).bit_length() - 1)):
        partner = moved(by_x[0], lambda zz, xx, yy, cc, bit=bit: (zz ^ 2**bit, xx, yy, cc))
        by_x[0] = butterfly(by_x[0], partner, z, bit)
    by_x = block_inverse(by_x)
    first_row = by_x[0]
    for i in range(1, owners):
        first_row = jnp.where(x == i, by_x[i], first_row)

    every = (spans * pair, extent)
    work = 2 * slots * spans * pair * extent * extent
    near = call(
        near_kernel,
        "near",
        f32(blocks + 1, *every),
        [smem] * 3 + [vmem] * (1 + len(direct)),
        vmem,
        limit=24,
        scratch=[pltpu.VMEM((blocks, *every), jnp.bfloat16)],
        flops=work // owners,
        moved_bytes=stack.size * 2,
        blocks=blocks,
        spans=spans,
        chunks=CHUNKS,
    )(place, order, sizes, stack, *direct)

    shape = (spans, blocks, height, extent)
    keep, send = call(
        far_kernel,
        "far",
        [f32(*shape)] * 2,
        [smem] * 3 + [vmem] * (4 + len(direct) + len(swapped)),
        [vmem] * 2,
        limit=32,
        scratch=[
            pltpu.VMEM(((owners - 1) * blocks, *every), jnp.bfloat16),
            pltpu.VMEM((blocks + 1, *every), jnp.float32),
            pltpu.VMEM((owners, spans * pair, 128), jnp.float32),
        ],
        flops=work,
        moved_bytes=stack.size * 2,
        blocks=blocks,
        owners=owners,
        spans=spans,
        chunks=CHUNKS,
    )(place, order, sizes, stack, near, first_cols, first_row, *direct, *swapped)

    own, *outgoing = call(
        combine_kernel,
        "combine",
        [f32(*shape[1:])] + [bf16(*shape[1:])] * (spans - 1),
        [smem, vmem, vmem],
        [vmem] * spans,
    )(place, keep, other_core(send))
    arrived = [
        moved(value, lambda zz, xx, yy, cc, j=j: (zz, xx, (yy + j) % spans, cc)) for j, value in enumerate(outgoing, 1)
    ]
    return call(back_kernel, "back", f32(*sources.shape), [vmem] * (spans + 2), vmem)(
        own, *arrived, jnp.asarray(signs.T, jnp.bfloat16), jnp.asarray(scale, jnp.float32)
    )


def solution(mesh):
    return jax.shard_map(
        local,
        mesh=mesh,
        in_specs=(
            P("col", "row"),
            P("row", "col", None, None, None),
            P("row", "col", None),
            P("row", "col", None),
            P("row", "col"),
        ),
        out_specs=P("col", "row"),
        check_vma=False,
    )
```

```python
import functools
import math

import jax
import jax.numpy as jnp
from jax import lax
from jax.experimental import pallas as pl
from jax.experimental.pallas import tpu as pltpu
from jax.sharding import PartitionSpec as P

ROOT_HALF = 1.0 / math.sqrt(2.0)
SIDE_ROWS = 16
CHUNKS = 2
UNROLL = 4
MIB = 2**20


def haar_parts(extent, transposed):
    k = lax.broadcasted_iota(jnp.int32, (extent, extent), 1 if transposed else 0)
    n = lax.broadcasted_iota(jnp.int32, (extent, extent), 0 if transposed else 1)
    stride = jnp.where(n == 0, extent, n & -n)
    signs = jnp.where((k ^ n) < 2 * stride, jnp.where((k & stride) == 0, 1.0, -1.0), 0.0)
    n = lax.broadcasted_iota(jnp.int32, (1, extent), 1)
    scale = jnp.full((1, extent), 1.0 / math.sqrt(extent), jnp.float32)
    level = 1
    while level < extent:
        scale = jnp.where((n & -n) == level, 1.0 / math.sqrt(2 * level), scale)
        level *= 2
    return signs.astype(jnp.bfloat16), scale


def three_terms(value):
    high = value.astype(jnp.bfloat16)
    rest = value - high.astype(jnp.float32)
    middle = rest.astype(jnp.bfloat16)
    low = (rest - middle.astype(jnp.float32)).astype(jnp.bfloat16)
    return high, middle, low


def exact_dot(value, signs):
    return sum(jnp.dot(term, signs, preferred_element_type=jnp.float32) for term in three_terms(value))


def block_forward(columns):
    columns = list(columns)
    stride = 1
    while stride < len(columns):
        for p in range(0, len(columns), 2 * stride):
            u, v = columns[p], columns[p + stride]
            columns[p], columns[p + stride] = (u + v) * ROOT_HALF, (u - v) * ROOT_HALF
        stride *= 2
    return columns


def block_inverse(columns):
    columns = list(columns)
    stride = len(columns) // 2
    while stride >= 1:
        for p in range(0, len(columns), 2 * stride):
            u, v = columns[p], columns[p + stride]
            columns[p], columns[p + stride] = (u + v) * ROOT_HALF, (u - v) * ROOT_HALF
        stride //= 2
    return columns


def front_kernel(core_ref, sources_ref, other_ref, *refs, blocks, extent):
    *out_refs, mine_ref, sem = refs
    copy = pltpu.make_async_copy(sources_ref, mine_ref, sem)
    copy.start()
    height = mine_ref.shape[0]
    pair = 2 * height
    signs, scale = haar_parts(extent, False)
    copy.wait()
    mine, other = mine_ref[...], other_ref[...]
    first_core = core_ref[0] == 0
    both = jnp.concatenate([jnp.where(first_core, mine, other), jnp.where(first_core, other, mine)], axis=0)
    parts = [both[:, b * extent : (b + 1) * extent] for b in range(blocks)]
    coef = exact_dot(jnp.concatenate(parts, axis=0), signs) * scale
    columns = block_forward([coef[b * pair : (b + 1) * pair, 0:1] for b in range(blocks)])
    lane = lax.broadcasted_iota(jnp.int32, (pair, extent), 1)
    held = blocks // len(out_refs)
    for b in range(blocks):
        column = jnp.zeros_like(columns[0]) if b == 0 else columns[b]
        block = jnp.where(lane == 0, column, coef[b * pair : (b + 1) * pair, :])
        at = b % held * pair
        out_refs[b // held][at : at + pair, :] = block.astype(jnp.bfloat16)
    total = functools.reduce(jnp.add, parts)
    ones = jnp.ones((SIDE_ROWS, extent), jnp.bfloat16)
    first = sum(
        lax.dot_general(ones, term, (((1,), (1,)), ((), ())), preferred_element_type=jnp.float32)
        for term in three_terms(total)
    ) * (1.0 / math.sqrt(blocks * extent))
    high, middle, low = (term.astype(jnp.float32) for term in three_terms(first))
    row = lax.broadcasted_iota(jnp.int32, first.shape, 0)
    side = jnp.where(row == 0, high, jnp.where(row == 1, middle, jnp.where(row == 2, low, 0.0)))
    out_refs[-1][held * pair :, :] = jnp.zeros((SIDE_ROWS, extent), jnp.bfloat16)
    out_refs[-1][held * pair :, 0:pair] = side.astype(jnp.bfloat16)


def edge_kernel(
    place_ref,
    rows_ref,
    cols_ref,
    count_ref,
    tiles_ref,
    lead_ref,
    rest_ref,
    row_ref,
    order_ref,
    sizes_ref,
    strips,
    held,
    strip_sem,
    held_sems,
    *,
    blocks,
    owners,
):
    extent = tiles_ref.shape[-1]
    count = count_ref[0]
    x = place_ref[2]
    strip_copy = pltpu.make_async_copy(tiles_ref.at[:, 0:SIDE_ROWS, :], strips, strip_sem)
    strip_copy.start()
    lead_ref[...] = jnp.zeros_like(lead_ref)
    rest_ref[...] = jnp.zeros_like(rest_ref)
    row_ref[...] = jnp.zeros_like(row_ref)
    pick = (lax.broadcasted_iota(jnp.int32, (SIDE_ROWS, extent), 1) == 0).astype(jnp.bfloat16)

    def tile_copy(slot):
        return pltpu.make_async_copy(tiles_ref.at[slot], held.at[slot], held_sems.at[slot])

    def visit(slot, sizes):
        row, col = rows_ref[slot], cols_ref[slot]
        owner, block = col // blocks, lax.rem(col, blocks)

        @pl.when(row == 0)
        def _():
            tile_copy(slot).start()

        behind = lax.rem(x - owner + owners, owners)
        own = (behind == 0).astype(jnp.int32)
        side = jnp.where(behind == 0, block, (behind - 1) * blocks + block)
        order_ref[1 - own, jnp.where(own == 1, sizes[0], sizes[1])] = (slot << 16) + (side << 8) + row
        return sizes[0] + own, sizes[1] + 1 - own

    sizes = lax.fori_loop(0, count, visit, (jnp.int32(0), jnp.int32(0)))
    for which in range(2):
        sizes_ref[which] = sizes[which]
        for k in range(UNROLL - 1):
            order_ref[which, sizes[which] + k] = blocks
    strip_copy.wait()

    def add(slot, _):
        row, col = rows_ref[slot], cols_ref[slot]
        owner, block = col // blocks, lax.rem(col, blocks)

        @pl.when((block == 0) & (owner == 0))
        def _():
            lead_ref[pl.ds(row, 1), :] += strips[slot].astype(jnp.float32)[0:1, :]

        @pl.when((block == 0) & (owner > 0))
        def _():
            at = pl.ds((owner - 1) * blocks + row, 1)
            rest_ref[at, :] += strips[slot].astype(jnp.float32)[0:1, :]

        @pl.when(row == 0)
        def _():
            tile_copy(slot).wait()
            column = lax.dot_general(
                pick, held[slot], (((1,), (1,)), ((), ())), preferred_element_type=jnp.float32
            )
            row_ref[pl.ds(col, 1), :] += column[0:1, :]

        return 0

    lax.fori_loop(0, count, add, 0)


def corner_kernel(place_ref, lead_ref, partner_ref, rest_ref, row_ref, _, cols_ref, fixed_ref, *, blocks, owners):
    lead, partner = lead_ref[...], partner_ref[...]
    combined = jnp.where(place_ref[0] == 1, partner - lead, partner + lead) * ROOT_HALF
    lines = [combined] + [rest_ref[i * blocks : (i + 1) * blocks, :] for i in range(owners - 1)]
    lines = block_inverse(lines)
    fixed = row_ref[...]
    index = lax.broadcasted_iota(jnp.int32, fixed.shape, 0)
    lane = lax.broadcasted_iota(jnp.int32, fixed.shape, 1)
    for i, line in enumerate(lines):
        cols_ref[i * blocks : (i + 1) * blocks, :] = line
        fixed = jnp.where((index == i * blocks) & (lane == 0), line[0:1, 0:1], fixed)
    fixed_ref[...] = fixed


def fill_sides(sides, messages, place_ref, chunks, blocks, spans):
    pair = sides.shape[1] // spans
    held = blocks // chunks
    for index, message in enumerate(messages):
        behind, m, chunk = index // (spans * chunks), index // chunks % spans, index % chunks
        rows = pl.ds(pl.multiple_of(place_ref[3 + m] * pair, pair), pair)
        for b in range(held):
            sides[behind * blocks + chunk * held + b, rows, :] = message[b * pair : (b + 1) * pair, :]


def add_products(order_ref, sizes_ref, which, tiles_ref, sides, acc):
    def group(index, _):
        for k in range(UNROLL):
            entry = order_ref[which, index * UNROLL + k]
            slot, side, row = entry >> 16, (entry >> 8) & 255, entry & 255
            acc[row] += jnp.dot(sides[side], tiles_ref[slot], preferred_element_type=jnp.float32)
        return 0

    lax.fori_loop(0, (sizes_ref[which] + UNROLL - 1) // UNROLL, group, 0)


def near_kernel(place_ref, order_ref, sizes_ref, tiles_ref, *refs, blocks, spans, chunks):
    *messages, acc_ref, sides = refs
    fill_sides(sides, messages, place_ref, chunks, blocks, spans)
    acc_ref[...] = jnp.zeros_like(acc_ref)
    add_products(order_ref, sizes_ref, 0, tiles_ref, sides, acc_ref)


def far_kernel(
    place_ref, order_ref, sizes_ref, tiles_ref, near_ref, cols_ref, row_ref, *refs, blocks, owners, spans, chunks
):
    direct, swapped = refs[: spans * chunks], refs[spans * chunks : owners * spans * chunks]
    keep_ref, send_ref, sides, acc, firsts = refs[owners * spans * chunks :]
    extent = tiles_ref.shape[-1]
    pair = sides.shape[1] // spans
    height = pair // 2
    held = blocks // chunks
    x = place_ref[2]
    fill_sides(sides, swapped, place_ref, chunks, blocks, spans)
    messages = (*direct, *swapped)
    for behind in range(owners):
        owner = lax.rem(x - behind + owners, owners)
        for m in range(spans):
            message = messages[(behind * spans + m) * chunks + chunks - 1]
            side = jnp.transpose(message[held * pair :, :].astype(jnp.float32))
            column = side[0:pair, 0:1] + side[0:pair, 1:2] + side[0:pair, 2:3]
            rows = pl.ds(pl.multiple_of(place_ref[3 + m] * pair, pair), pair)
            firsts[owner, rows, :] = jnp.broadcast_to(column, (pair, firsts.shape[2]))
    for i in range(blocks):
        total = near_ref[i]
        for owner in range(owners):
            total += firsts[owner][:, 0:1] * cols_ref[owner * blocks + i : owner * blocks + i + 1, :]
        acc[i] = total
    add_products(order_ref, sizes_ref, 1, tiles_ref, sides, acc)

    lane = lax.broadcasted_iota(jnp.int32, (pair, extent), 1)
    for m in range(spans):
        rows = pl.ds(pl.multiple_of(place_ref[3 + m] * pair, pair), pair)
        total = jnp.zeros((pair, extent), jnp.float32)
        top = jnp.zeros((pair, 1), jnp.float32)
        for behind in range(owners):
            owner = lax.rem(x - behind + owners, owners)
            for b in range(blocks):
                message = messages[(behind * spans + m) * chunks + b // held]
                at = b % held * pair
                line = row_ref[pl.ds(owner * blocks + b, 1), :]
                total += message[at : at + pair, :].astype(jnp.float32) * line
                if b == 0:
                    top += firsts[owner, rows, :][:, 0:1] * line[:, 0:1]
        top += jnp.sum(total, axis=1, keepdims=True)
        acc[0, rows, :] = jnp.where(lane == 0, top, acc[0, rows, :])
    first_core = place_ref[0] == 0
    for i in range(blocks):
        value = acc[i]
        for y in range(spans):
            one = value[y * pair : y * pair + height, :]
            two = value[y * pair + height : (y + 1) * pair, :]
            keep_ref[y, i] = jnp.where(first_core, one, two)
            send_ref[y, i] = jnp.where(first_core, two, one)


def combine_kernel(place_ref, keep_ref, arrived_ref, own_ref, *out_refs):
    spans = keep_ref.shape[0]
    span = place_ref[1]
    own_ref[...] = keep_ref[span] + arrived_ref[span]
    for j, out_ref in enumerate(out_refs, 1):
        at = lax.rem(span + j, spans)
        out_ref[...] = (keep_ref[at] + arrived_ref[at]).astype(jnp.bfloat16)


def back_kernel(own_ref, *refs):
    *arrived, out_ref = refs
    blocks, height, extent = own_ref.shape
    total = own_ref[...]
    for part in arrived:
        total = total + part[...].astype(jnp.float32)
    columns = block_inverse([total[b][:, 0:1] for b in range(blocks)])
    lane = lax.broadcasted_iota(jnp.int32, (height, extent), 1)
    fixed = jnp.concatenate([jnp.where(lane == 0, columns[b], total[b]) for b in range(blocks)], axis=0)
    signs, scale = haar_parts(extent, True)
    result = exact_dot(fixed * scale, signs)
    for b in range(blocks):
        out_ref[:, b * extent : (b + 1) * extent] = result[b * height : (b + 1) * height, :]


def butterfly(value, partner, index, bit):
    active = index % 2**bit == 0
    upper = index // 2**bit % 2 == 1
    combined = jnp.where(upper, partner - value, partner + value) * ROOT_HALF
    return jnp.where(active, combined, value)


def local(sources, tiles, tile_row, tile_col, tile_count):
    n_row, n_col = lax.axis_size("row"), lax.axis_size("col")
    owners = n_row // n_col
    spans = n_col // 2
    extent = tiles.shape[-1]
    slots = tiles.shape[2]
    height = sources.shape[0]
    blocks = sources.shape[1] // extent
    pair = 2 * height
    held = blocks // CHUNKS
    row_index, col_index = lax.axis_index("row"), lax.axis_index("col")
    z, x = row_index // owners, row_index % owners
    span, core = col_index // 2, col_index % 2

    def moved(value, to):
        pairs = []
        for a in range(n_row):
            for b in range(n_col):
                zz, xx, yy, cc = to(a // owners, a % owners, b // 2, b % 2)
                pairs.append((a * n_col + b, (zz * owners + xx) * n_col + yy * 2 + cc))
        return lax.ppermute(value, ("row", "col"), pairs)

    def other_core(value):
        return moved(value, lambda zz, xx, yy, cc: (zz, xx, yy, 1 - cc))

    def along_x(value, j):
        return moved(value, lambda zz, xx, yy, cc: (zz, (xx + j) % owners, yy, cc))

    smem = pl.BlockSpec(memory_space=pltpu.SMEM)
    vmem = pl.BlockSpec(memory_space=pltpu.VMEM)
    hbm = pl.BlockSpec(memory_space=pltpu.HBM)
    unread = pl.BlockSpec(memory_space=pl.ANY)

    def call(kernel, name, out_shape, in_specs, out_specs, limit=16, scratch=(), flops=0, moved_bytes=MIB, **sizes):
        return pl.pallas_call(
            functools.partial(kernel, **sizes) if sizes else kernel,
            out_shape=out_shape,
            in_specs=in_specs,
            out_specs=out_specs,
            scratch_shapes=scratch,
            name=name,
            compiler_params=pltpu.CompilerParams(vmem_limit_bytes=limit * MIB),
            cost_estimate=pl.CostEstimate(flops=flops, bytes_accessed=moved_bytes, transcendentals=0),
        )

    def f32(*dims):
        return jax.ShapeDtypeStruct(dims, jnp.float32)

    def bf16(*dims):
        return jax.ShapeDtypeStruct(dims, jnp.bfloat16)

    place = jnp.stack([core, span, x] + [(z - m) % spans for m in range(spans)]).astype(jnp.int32)

    stack = tiles.reshape(slots, extent, extent)
    rows_flat, cols_flat = tile_row.reshape(-1), tile_col.reshape(-1)
    lead, rest, first_row, order, sizes = call(
        edge_kernel,
        "edges",
        [
            f32(blocks, extent),
            f32((owners - 1) * blocks, extent),
            f32(owners * blocks, extent),
            jax.ShapeDtypeStruct((2, slots + UNROLL), jnp.int32),
            jax.ShapeDtypeStruct((2,), jnp.int32),
        ],
        [smem] * 4 + [hbm],
        [vmem] * 3 + [smem] * 2,
        limit=48,
        scratch=[
            pltpu.VMEM((slots, SIDE_ROWS, extent), jnp.bfloat16),
            pltpu.VMEM((slots, extent, extent), jnp.bfloat16),
            pltpu.SemaphoreType.DMA,
            pltpu.SemaphoreType.DMA((slots,)),
        ],
        blocks=blocks,
        owners=owners,
    )(place, rows_flat, cols_flat, tile_count.reshape(1), stack)

    messages = call(
        front_kernel,
        "front",
        [bf16(held * pair + (SIDE_ROWS if q == CHUNKS - 1 else 0), extent) for q in range(CHUNKS)],
        [smem, hbm, vmem],
        [vmem] * CHUNKS,
        limit=48,
        scratch=[pltpu.VMEM(sources.shape, jnp.float32), pltpu.SemaphoreType.DMA],
        blocks=blocks,
        extent=extent,
    )(place, sources, other_core(sources))

    direct = [
        moved(messages[q], lambda zz, xx, yy, cc, m=m: (cc * spans + (yy + m) % spans, xx, zz // 2, zz % 2))
        for m in range(spans)
        for q in range(CHUNKS)
    ]
    swapped = [along_x(piece, j) for j in range(1, owners) for piece in direct]

    def after(value, *others):
        return lax.optimization_barrier((value, *others))[0]


    lead = after(lead, messages[0])
    for bit in reversed(range(1, n_col.bit_length() - 1)):
        step = 2 ** (bit - 1)
        partner = moved(lead, lambda zz, xx, yy, cc, step=step: (zz, xx, yy ^ step, cc))
        lead = butterfly(lead, partner, col_index, bit)
    lead = after(lead, direct[0])
    first_cols, first_row = call(
        corner_kernel,
        "corner",
        [f32(owners * blocks, extent)] * 2,
        [smem] + [vmem] * 4 + [unread],
        [vmem] * 2,
        blocks=blocks,
        owners=owners,
    )(place, lead, other_core(lead), rest, first_row, direct[1])
    behind = [first_row] + [along_x(first_row, j) for j in range(1, owners)]
    by_x = []
    for i in range(owners):
        line = behind[0]
        for j in range(1, owners):
            line = jnp.where((x - i) % owners == j, behind[j], line)
        by_x.append(line)
    by_x[0] = after(by_x[0], direct[2], swapped[0])
    for bit in reversed(range((n_row // owners).bit_length() - 1)):
        partner = moved(by_x[0], lambda zz, xx, yy, cc, bit=bit: (zz ^ 2**bit, xx, yy, cc))
        by_x[0] = butterfly(by_x[0], partner, z, bit)
        by_x[0] = after(by_x[0], direct[-1], *swapped[1 : 2 if bit else 3])
    by_x = block_inverse(by_x)
    first_row = by_x[0]
    for i in range(1, owners):
        first_row = jnp.where(x == i, by_x[i], first_row)

    every = (spans * pair, extent)
    work = 2 * slots * spans * pair * extent * extent
    near = call(
        near_kernel,
        "near",
        f32(blocks + 1, *every),
        [smem] * 3 + [vmem] * (1 + len(direct)),
        vmem,
        limit=24,
        scratch=[pltpu.VMEM((blocks, *every), jnp.bfloat16)],
        flops=work // owners,
        moved_bytes=stack.size * 2,
        blocks=blocks,
        spans=spans,
        chunks=CHUNKS,
    )(place, order, sizes, stack, *direct)

    shape = (spans, blocks, height, extent)
    keep, send = call(
        far_kernel,
        "far",
        [f32(*shape)] * 2,
        [smem] * 3 + [vmem] * (4 + len(direct) + len(swapped)),
        [vmem] * 2,
        limit=32,
        scratch=[
            pltpu.VMEM(((owners - 1) * blocks, *every), jnp.bfloat16),
            pltpu.VMEM((blocks + 1, *every), jnp.float32),
            pltpu.VMEM((owners, spans * pair, 128), jnp.float32),
        ],
        flops=work,
        moved_bytes=stack.size * 2,
        blocks=blocks,
        owners=owners,
        spans=spans,
        chunks=CHUNKS,
    )(place, order, sizes, stack, near, first_cols, first_row, *direct, *swapped)

    own, *outgoing = call(
        combine_kernel,
        "combine",
        [f32(*shape[1:])] + [bf16(*shape[1:])] * (spans - 1),
        [smem, vmem, vmem],
        [vmem] * spans,
    )(place, keep, other_core(send))
    arrived = [
        moved(value, lambda zz, xx, yy, cc, j=j: (zz, xx, (yy + j) % spans, cc)) for j, value in enumerate(outgoing, 1)
    ]
    return call(back_kernel, "back", f32(*sources.shape), [vmem] * spans, vmem)(own, *arrived)


def solution(mesh):
    return jax.shard_map(
        local,
        mesh=mesh,
        in_specs=(
            P("col", "row"),
            P("row", "col", None, None, None),
            P("row", "col", None),
            P("row", "col", None),
            P("row", "col"),
        ),
        out_specs=P("col", "row"),
        check_vma=False,
    )
```

```python
import functools
import math

import jax
import jax.numpy as jnp
from jax import lax
from jax.experimental import pallas as pl
from jax.experimental.pallas import tpu as pltpu
from jax.sharding import PartitionSpec as P

ROOT_HALF = 1.0 / math.sqrt(2.0)
SIDE_ROWS = 16
FIRST_ROWS = 16
CHUNKS = 2
UNROLL = 4
MIB = 2**20


def haar_parts(extent, transposed):
    k = lax.broadcasted_iota(jnp.int32, (extent, extent), 1 if transposed else 0)
    n = lax.broadcasted_iota(jnp.int32, (extent, extent), 0 if transposed else 1)
    stride = jnp.where(n == 0, extent, n & -n)
    signs = jnp.where((k ^ n) < 2 * stride, jnp.where((k & stride) == 0, 1.0, -1.0), 0.0)
    n = lax.broadcasted_iota(jnp.int32, (1, extent), 1)
    scale = jnp.full((1, extent), 1.0 / math.sqrt(extent), jnp.float32)
    level = 1
    while level < extent:
        scale = jnp.where((n & -n) == level, 1.0 / math.sqrt(2 * level), scale)
        level *= 2
    return signs.astype(jnp.bfloat16), scale


def three_terms(value):
    high = value.astype(jnp.bfloat16)
    rest = value - high.astype(jnp.float32)
    middle = rest.astype(jnp.bfloat16)
    low = (rest - middle.astype(jnp.float32)).astype(jnp.bfloat16)
    return high, middle, low


def exact_dot(value, signs):
    return sum(jnp.dot(term, signs, preferred_element_type=jnp.float32) for term in three_terms(value))


def block_forward(columns):
    columns = list(columns)
    stride = 1
    while stride < len(columns):
        for p in range(0, len(columns), 2 * stride):
            u, v = columns[p], columns[p + stride]
            columns[p], columns[p + stride] = (u + v) * ROOT_HALF, (u - v) * ROOT_HALF
        stride *= 2
    return columns


def block_inverse(columns):
    columns = list(columns)
    stride = len(columns) // 2
    while stride >= 1:
        for p in range(0, len(columns), 2 * stride):
            u, v = columns[p], columns[p + stride]
            columns[p], columns[p + stride] = (u + v) * ROOT_HALF, (u - v) * ROOT_HALF
        stride //= 2
    return columns


def front_kernel(place_ref, sources_ref, other_ref, lead_ref, body_ref, first_ref, mine_ref, sem, *, blocks, extent):
    copy = pltpu.make_async_copy(sources_ref, mine_ref, sem)
    copy.start()
    height = mine_ref.shape[0]
    pair = 2 * height
    signs, scale = haar_parts(extent, False)
    copy.wait()
    mine, other = mine_ref[...], other_ref[...]
    first_core = place_ref[0] == 0
    both = jnp.concatenate([jnp.where(first_core, mine, other), jnp.where(first_core, other, mine)], axis=0)
    parts = [both[:, b * extent : (b + 1) * extent] for b in range(blocks)]
    coef = exact_dot(jnp.concatenate(parts, axis=0), signs) * scale
    columns = block_forward([coef[b * pair : (b + 1) * pair, 0:1] for b in range(blocks)])
    lane = lax.broadcasted_iota(jnp.int32, (pair, extent), 1)
    held = blocks // CHUNKS
    for b in range(blocks):
        column = jnp.zeros_like(columns[0]) if b == 0 else columns[b]
        block = jnp.where(lane == 0, column, coef[b * pair : (b + 1) * pair, :])
        at = b % held * pair
        (lead_ref, body_ref)[b // held][at : at + pair, :] = block.astype(jnp.bfloat16)
    total = functools.reduce(jnp.add, parts)
    ones = jnp.ones((FIRST_ROWS, extent), jnp.bfloat16)
    first = sum(
        lax.dot_general(ones, term, (((1,), (1,)), ((), ())), preferred_element_type=jnp.float32)
        for term in three_terms(total)
    )
    first_ref[...] = jnp.zeros_like(first_ref)
    first_ref[:, 0:pair] = first * (1.0 / math.sqrt(blocks * extent))


def edge_kernel(
    place_ref,
    rows_ref,
    cols_ref,
    count_ref,
    tiles_ref,
    first_ref,
    first_cols_ref,
    edge_ref,
    order_ref,
    sizes_ref,
    strips,
    held,
    strip_sem,
    held_sems,
    *,
    blocks,
    owners,
):
    extent = tiles_ref.shape[-1]
    count = count_ref[0]
    x = place_ref[2]
    strip_copy = pltpu.make_async_copy(tiles_ref.at[:, 0:SIDE_ROWS, :], strips, strip_sem)
    strip_copy.start()
    first_cols_ref[...] = jnp.zeros_like(first_cols_ref)
    edge_ref[...] = jnp.zeros_like(edge_ref)
    edge_ref[owners * blocks : owners * blocks + 8, :] = first_ref[0:8, :]
    pick = (lax.broadcasted_iota(jnp.int32, (SIDE_ROWS, extent), 1) == 0).astype(jnp.bfloat16)

    def tile_copy(slot):
        return pltpu.make_async_copy(tiles_ref.at[slot], held.at[slot], held_sems.at[slot])

    def visit(slot, sizes):
        row, col = rows_ref[slot], cols_ref[slot]
        owner, block = col // blocks, lax.rem(col, blocks)

        @pl.when(row == 0)
        def _():
            tile_copy(slot).start()

        behind = lax.rem(x - owner + owners, owners)
        own = (behind == 0).astype(jnp.int32)
        side = jnp.where(behind == 0, block, (behind - 1) * blocks + block)
        order_ref[1 - own, jnp.where(own == 1, sizes[0], sizes[1])] = (slot << 16) + (side << 8) + row
        return sizes[0] + own, sizes[1] + 1 - own

    sizes = lax.fori_loop(0, count, visit, (jnp.int32(0), jnp.int32(0)))
    for which in range(2):
        sizes_ref[which] = sizes[which]
        for k in range(UNROLL - 1):
            order_ref[which, sizes[which] + k] = blocks
    strip_copy.wait()

    def add(slot, _):
        row, col = rows_ref[slot], cols_ref[slot]

        @pl.when(lax.rem(col, blocks) == 0)
        def _():
            first_cols_ref[pl.ds(col + row, 1), :] += strips[slot].astype(jnp.float32)[0:1, :]

        @pl.when(row == 0)
        def _():
            tile_copy(slot).wait()
            column = lax.dot_general(
                pick, held[slot], (((1,), (1,)), ((), ())), preferred_element_type=jnp.float32
            )
            edge_ref[pl.ds(col, 1), :] += column[0:1, :]

        return 0

    lax.fori_loop(0, count, add, 0)


def seal_kernel(place_ref, body_ref, *refs, blocks, owners):
    edges, (out_ref, line_ref, rest_ref) = refs[:owners], refs[owners:]
    x = place_ref[2]
    by_x = []
    for i in range(owners):
        value = edges[0][...]
        for j in range(1, owners):
            value = jnp.where(lax.rem(x - i + owners, owners) == j, edges[j][...], value)
        by_x.append(value)
    length = owners * blocks
    line_ref[...] = by_x[0][0:length, :]
    for i in range(1, owners):
        rest_ref[i - 1] = by_x[i][0:length, :]
    firsts = block_forward([value[length : length + 1, :] for value in by_x])
    row = lax.broadcasted_iota(jnp.int32, (SIDE_ROWS, body_ref.shape[1]), 0)
    side = jnp.zeros(row.shape, jnp.float32)
    for i, first in enumerate(firsts):
        for k, term in enumerate(three_terms(first)):
            side = jnp.where(row == 3 * i + k, term.astype(jnp.float32), side)
    rows = body_ref.shape[0]
    out_ref[0:rows, :] = body_ref[...]
    out_ref[rows:, :] = side.astype(jnp.bfloat16)


def firsts_kernel(place_ref, *refs, owners, spans, pair):
    messages, out_ref = refs[:spans], refs[-1]
    width = messages[0].shape[1]
    total = jnp.zeros(out_ref.shape, jnp.float32)
    row = lax.broadcasted_iota(jnp.int32, out_ref.shape, 0)
    lane = lax.broadcasted_iota(jnp.int32, out_ref.shape, 1)
    for m, message in enumerate(messages):
        side = message[message.shape[0] - SIDE_ROWS :, :].astype(jnp.float32)
        copies = jnp.concatenate([side[:, 0:pair]] * spans, axis=1)
        at = place_ref[3 + m] * pair
        for i in range(owners):
            value = copies[3 * i : 3 * i + 1, :] + copies[3 * i + 1 : 3 * i + 2, :] + copies[3 * i + 2 : 3 * i + 3, :]
            total = jnp.where((row == i) & (lane >= at) & (lane < at + pair), value, total)
    out_ref[...] = total


def fill_sides(sides, messages, place_ref, blocks, spans):
    pair = sides.shape[1] // spans
    held = blocks // CHUNKS
    for index, message in enumerate(messages):
        behind, m, chunk = index // (spans * CHUNKS), index // CHUNKS % spans, index % CHUNKS
        rows = pl.ds(pl.multiple_of(place_ref[3 + m] * pair, pair), pair)
        for b in range(held):
            sides[behind * blocks + chunk * held + b, rows, :] = message[b * pair : (b + 1) * pair, :]


def start_tiles(order_ref, sizes_ref, which, tiles_ref, held, sems):
    def start(index, _):
        slot = order_ref[which, index] >> 16
        pltpu.make_async_copy(tiles_ref.at[slot], held.at[index], sems.at[index]).start()
        return 0

    lax.fori_loop(0, (sizes_ref[which] + UNROLL - 1) // UNROLL * UNROLL, start, 0)


def add_products(order_ref, sizes_ref, which, tiles_ref, held, sems, sides, acc):
    def group(index, _):
        for k in range(UNROLL):
            at = index * UNROLL + k
            pltpu.make_async_copy(tiles_ref.at[0], held.at[at], sems.at[at]).wait()
        for k in range(UNROLL):
            at = index * UNROLL + k
            entry = order_ref[which, at]
            side, row = (entry >> 8) & 255, entry & 255
            acc[row] += jnp.dot(sides[side], held[at], preferred_element_type=jnp.float32)
        return 0

    lax.fori_loop(0, (sizes_ref[which] + UNROLL - 1) // UNROLL, group, 0)


def near_kernel(place_ref, order_ref, sizes_ref, tiles_ref, *refs, blocks, spans):
    *messages, acc_ref, sides, held, sems = refs
    start_tiles(order_ref, sizes_ref, 0, tiles_ref, held, sems)
    fill_sides(sides, messages, place_ref, blocks, spans)
    acc_ref[...] = jnp.zeros_like(acc_ref)
    add_products(order_ref, sizes_ref, 0, tiles_ref, held, sems, sides, acc_ref)


def far_kernel(
    place_ref, order_ref, sizes_ref, tiles_ref, near_ref, firsts_ref, cols_ref, row_ref, *refs, blocks, owners, spans
):
    direct, swapped = refs[: spans * CHUNKS], refs[spans * CHUNKS : owners * spans * CHUNKS]
    keep_ref, send_ref, sides, acc, held_tiles, sems = refs[owners * spans * CHUNKS :]
    start_tiles(order_ref, sizes_ref, 1, tiles_ref, held_tiles, sems)
    extent = tiles_ref.shape[-1]
    pair = sides.shape[1] // spans
    height = pair // 2
    held = blocks // CHUNKS
    x = place_ref[2]
    fill_sides(sides, swapped, place_ref, blocks, spans)
    messages = (*direct, *swapped)
    columns = jnp.transpose(firsts_ref[...])
    for i in range(blocks):
        total = near_ref[i]
        for owner in range(owners):
            total += columns[:, owner : owner + 1] * cols_ref[owner * blocks + i : owner * blocks + i + 1, :]
        acc[i] = total
    add_products(order_ref, sizes_ref, 1, tiles_ref, held_tiles, sems, sides, acc)

    top = jnp.zeros((spans * pair, 1), jnp.float32)
    for owner in range(owners):
        top += columns[:, owner : owner + 1] * row_ref[owner * blocks : owner * blocks + 1, 0:1]
    lane = lax.broadcasted_iota(jnp.int32, (spans * pair, extent), 1)
    acc[0] = jnp.where(lane == 0, top, acc[0])
    lane = lane[0:pair]
    for m in range(spans):
        rows = pl.ds(pl.multiple_of(place_ref[3 + m] * pair, pair), pair)
        total = jnp.zeros((pair, extent), jnp.float32)
        for behind in range(owners):
            owner = lax.rem(x - behind + owners, owners)
            for b in range(blocks):
                message = messages[(behind * spans + m) * CHUNKS + b // held]
                at = b % held * pair
                line = row_ref[pl.ds(owner * blocks + b, 1), :]
                total += message[at : at + pair, :].astype(jnp.float32) * line
        part = jnp.sum(total, axis=1, keepdims=True)
        acc[0, rows, :] = acc[0, rows, :] + jnp.where(lane == 0, part, 0.0)
    first_core = place_ref[0] == 0
    for i in range(blocks):
        value = acc[i]
        for y in range(spans):
            one = value[y * pair : y * pair + height, :]
            two = value[y * pair + height : (y + 1) * pair, :]
            keep_ref[y, i] = jnp.where(first_core, one, two)
            send_ref[y, i] = jnp.where(first_core, two, one)


def combine_kernel(place_ref, keep_ref, arrived_ref, own_ref, *out_refs):
    spans = keep_ref.shape[0]
    span = place_ref[1]
    own_ref[...] = keep_ref[span] + arrived_ref[span]
    for j, out_ref in enumerate(out_refs, 1):
        at = lax.rem(span + j, spans)
        out_ref[...] = (keep_ref[at] + arrived_ref[at]).astype(jnp.bfloat16)


def back_kernel(own_ref, *refs):
    *arrived, out_ref = refs
    blocks, height, extent = own_ref.shape
    total = own_ref[...]
    for part in arrived:
        total = total + part[...].astype(jnp.float32)
    columns = block_inverse([total[b][:, 0:1] for b in range(blocks)])
    lane = lax.broadcasted_iota(jnp.int32, (height, extent), 1)
    fixed = jnp.concatenate([jnp.where(lane == 0, columns[b], total[b]) for b in range(blocks)], axis=0)
    signs, scale = haar_parts(extent, True)
    result = exact_dot(fixed * scale, signs)
    for b in range(blocks):
        out_ref[:, b * extent : (b + 1) * extent] = result[b * height : (b + 1) * height, :]


def butterfly(value, partner, index, bit):
    active = index % 2**bit == 0
    upper = index // 2**bit % 2 == 1
    combined = jnp.where(upper, partner - value, partner + value) * ROOT_HALF
    return jnp.where(active, combined, value)


def local(sources, tiles, tile_row, tile_col, tile_count):
    n_row, n_col = lax.axis_size("row"), lax.axis_size("col")
    owners = n_row // n_col
    spans = n_col // 2
    extent = tiles.shape[-1]
    slots = tiles.shape[2]
    height = sources.shape[0]
    blocks = sources.shape[1] // extent
    pair = 2 * height
    held = blocks // CHUNKS
    row_index, col_index = lax.axis_index("row"), lax.axis_index("col")
    z, x = row_index // owners, row_index % owners
    span, core = col_index // 2, col_index % 2

    def moved(value, to):
        pairs = []
        for a in range(n_row):
            for b in range(n_col):
                zz, xx, yy, cc = to(a // owners, a % owners, b // 2, b % 2)
                pairs.append((a * n_col + b, (zz * owners + xx) * n_col + yy * 2 + cc))
        return lax.ppermute(value, ("row", "col"), pairs)

    def other_core(value):
        return moved(value, lambda zz, xx, yy, cc: (zz, xx, yy, 1 - cc))

    def along_x(value, j):
        return moved(value, lambda zz, xx, yy, cc: (zz, (xx + j) % owners, yy, cc))

    smem = pl.BlockSpec(memory_space=pltpu.SMEM)
    vmem = pl.BlockSpec(memory_space=pltpu.VMEM)
    hbm = pl.BlockSpec(memory_space=pltpu.HBM)
    unread = pl.BlockSpec(memory_space=pl.ANY)

    def call(kernel, name, out_shape, in_specs, out_specs, limit=16, scratch=(), flops=0, moved_bytes=MIB, **sizes):
        return pl.pallas_call(
            functools.partial(kernel, **sizes) if sizes else kernel,
            out_shape=out_shape,
            in_specs=in_specs,
            out_specs=out_specs,
            scratch_shapes=scratch,
            name=name,
            compiler_params=pltpu.CompilerParams(vmem_limit_bytes=int(limit * MIB)),
            cost_estimate=pl.CostEstimate(flops=flops, bytes_accessed=moved_bytes, transcendentals=0),
        )

    def f32(*dims):
        return jax.ShapeDtypeStruct(dims, jnp.float32)

    def bf16(*dims):
        return jax.ShapeDtypeStruct(dims, jnp.bfloat16)

    place = jnp.stack([core, span, x] + [(z - m) % spans for m in range(spans)]).astype(jnp.int32)

    def after(value, *others):
        return lax.optimization_barrier((value, *others))[0]

    length = owners * blocks
    lead, body, first = call(
        front_kernel,
        "front",
        [bf16(held * pair, extent), bf16(held * pair, extent), f32(FIRST_ROWS, extent)],
        [smem, hbm, vmem],
        [vmem] * 3,
        limit=48,
        scratch=[pltpu.VMEM(sources.shape, jnp.float32), pltpu.SemaphoreType.DMA],
        blocks=blocks,
        extent=extent,
    )(place, sources, other_core(sources))

    def spread(message):
        return [
            moved(message, lambda zz, xx, yy, cc, m=m: (cc * spans + (yy + m) % spans, xx, zz // 2, zz % 2))
            for m in range(spans)
        ]

    direct_lead = spread(lead)
    stack = tiles.reshape(slots, extent, extent)
    first_cols, edge, order, sizes = call(
        edge_kernel,
        "edges",
        [
            f32(length, extent),
            f32(length + 8, extent),
            jax.ShapeDtypeStruct((2, slots + UNROLL), jnp.int32),
            jax.ShapeDtypeStruct((2,), jnp.int32),
        ],
        [smem] * 4 + [hbm, vmem],
        [vmem] * 2 + [smem] * 2,
        limit=50,
        scratch=[
            pltpu.VMEM((slots, SIDE_ROWS, extent), jnp.bfloat16),
            pltpu.VMEM((slots, extent, extent), jnp.bfloat16),
            pltpu.SemaphoreType.DMA,
            pltpu.SemaphoreType.DMA((slots,)),
        ],
        blocks=blocks,
        owners=owners,
    )(place, tile_row.reshape(-1), tile_col.reshape(-1), tile_count.reshape(1), stack, first)
    message, line, rest = call(
        seal_kernel,
        "seal",
        [bf16(held * pair + SIDE_ROWS, extent), f32(length, extent), f32(owners - 1, length, extent)],
        [smem] + [vmem] * (1 + owners),
        [vmem] * 3,
        blocks=blocks,
        owners=owners,
    )(place, body, edge, *[along_x(edge, j) for j in range(1, owners)])
    direct_last = spread(message)
    direct = [piece for m in range(spans) for piece in (direct_lead[m], direct_last[m])]
    swapped = [along_x(piece, j) for j in range(1, owners) for piece in direct]

    firsts = call(
        firsts_kernel,
        "firsts",
        f32(FIRST_ROWS, spans * pair),
        [smem] + [vmem] * spans,
        vmem,
        owners=owners,
        spans=spans,
        pair=pair,
    )(place, *direct_last)
    top_row = (jnp.arange(FIRST_ROWS) == 0)[:, None]
    for bit in range(n_col.bit_length() - 1):
        pairs = [(source, source ^ 2**bit) for source in range(n_col)]
        partner = lax.ppermute(firsts, "col", pairs)
        firsts = jnp.where(top_row, butterfly(firsts, partner, col_index, bit), firsts)

    for bit in reversed(range((n_row // owners).bit_length() - 1)):
        partner = moved(line, lambda zz, xx, yy, cc, bit=bit: (zz ^ 2**bit, xx, yy, cc))
        line = after(butterfly(line, partner, z, bit), *direct_last)
    by_x = block_inverse([line] + [rest[i] for i in range(owners - 1)])
    first_row = by_x[0]
    for i in range(1, owners):
        first_row = jnp.where(x == i, by_x[i], first_row)

    every = (spans * pair, extent)
    held_tiles = [
        pltpu.VMEM((slots + UNROLL, extent, extent), jnp.bfloat16),
        pltpu.SemaphoreType.DMA((slots + UNROLL,)),
    ]
    work = 2 * slots * spans * pair * extent * extent
    near = call(
        near_kernel,
        "near",
        f32(blocks + 1, *every),
        [smem] * 3 + [hbm] + [vmem] * len(direct),
        vmem,
        limit=50,
        scratch=[pltpu.VMEM((blocks, *every), jnp.bfloat16), *held_tiles],
        flops=work // owners,
        moved_bytes=stack.size * 2,
        blocks=blocks,
        spans=spans,
    )(place, order, sizes, stack, *direct)

    shape = (spans, blocks, height, extent)
    keep, send = call(
        far_kernel,
        "far",
        [f32(*shape)] * 2,
        [smem] * 3 + [hbm] + [vmem] * (4 + len(direct) + len(swapped)),
        [vmem] * 2,
        limit=50,
        scratch=[
            pltpu.VMEM(((owners - 1) * blocks, *every), jnp.bfloat16),
            pltpu.VMEM((blocks + 1, *every), jnp.float32),
            *held_tiles,
        ],
        flops=work,
        moved_bytes=stack.size * 2,
        blocks=blocks,
        owners=owners,
        spans=spans,
    )(place, order, sizes, stack, near, firsts, first_cols, first_row, *direct, *swapped)

    own, *outgoing = call(
        combine_kernel,
        "combine",
        [f32(*shape[1:])] + [bf16(*shape[1:])] * (spans - 1),
        [smem, vmem, vmem],
        [vmem] * spans,
    )(place, keep, other_core(send))
    arrived = [
        moved(value, lambda zz, xx, yy, cc, j=j: (zz, xx, (yy + j) % spans, cc)) for j, value in enumerate(outgoing, 1)
    ]
    return call(back_kernel, "back", f32(*sources.shape), [vmem] * spans, vmem)(own, *arrived)


def solution(mesh):
    return jax.shard_map(
        local,
        mesh=mesh,
        in_specs=(
            P("col", "row"),
            P("row", "col", None, None, None),
            P("row", "col", None),
            P("row", "col", None),
            P("row", "col"),
        ),
        out_specs=P("col", "row"),
        check_vma=False,
    )
```

```python
import functools
import math

import jax
import jax.numpy as jnp
from jax import lax
from jax.experimental import pallas as pl
from jax.experimental.pallas import tpu as pltpu
from jax.sharding import PartitionSpec as P

ROOT_HALF = 1.0 / math.sqrt(2.0)
SIDE_ROWS = 16
FIRST_ROWS = 16
CHUNKS = 2
UNROLL = 4
FETCHES = 6
MIB = 2**20


def haar_parts(extent, transposed):
    k = lax.broadcasted_iota(jnp.int32, (extent, extent), 1 if transposed else 0)
    n = lax.broadcasted_iota(jnp.int32, (extent, extent), 0 if transposed else 1)
    stride = jnp.where(n == 0, extent, n & -n)
    signs = jnp.where((k ^ n) < 2 * stride, jnp.where((k & stride) == 0, 1.0, -1.0), 0.0)
    n = lax.broadcasted_iota(jnp.int32, (1, extent), 1)
    scale = jnp.full((1, extent), 1.0 / math.sqrt(extent), jnp.float32)
    level = 1
    while level < extent:
        scale = jnp.where((n & -n) == level, 1.0 / math.sqrt(2 * level), scale)
        level *= 2
    return signs.astype(jnp.bfloat16), scale


def three_terms(value):
    high = value.astype(jnp.bfloat16)
    rest = value - high.astype(jnp.float32)
    middle = rest.astype(jnp.bfloat16)
    low = (rest - middle.astype(jnp.float32)).astype(jnp.bfloat16)
    return high, middle, low


def exact_dot(value, signs):
    return sum(jnp.dot(term, signs, preferred_element_type=jnp.float32) for term in three_terms(value))


def block_forward(columns):
    columns = list(columns)
    stride = 1
    while stride < len(columns):
        for p in range(0, len(columns), 2 * stride):
            u, v = columns[p], columns[p + stride]
            columns[p], columns[p + stride] = (u + v) * ROOT_HALF, (u - v) * ROOT_HALF
        stride *= 2
    return columns


def block_inverse(columns):
    columns = list(columns)
    stride = len(columns) // 2
    while stride >= 1:
        for p in range(0, len(columns), 2 * stride):
            u, v = columns[p], columns[p + stride]
            columns[p], columns[p + stride] = (u + v) * ROOT_HALF, (u - v) * ROOT_HALF
        stride //= 2
    return columns


def packed_place(core, span, x, z):
    return (core + 2 * span + 256 * x + 65536 * z).astype(jnp.int32).reshape(1)


def chunk_of(block, blocks):
    lead = blocks - blocks // 4
    return (0, block) if block < lead else (1, block - lead)


def core_of(place_ref):
    return place_ref[0] & 1


def span_of(place_ref):
    return (place_ref[0] >> 1) & 127


def x_of(place_ref):
    return (place_ref[0] >> 8) & 255


def source_span(place_ref, m, spans):
    return lax.rem((place_ref[0] >> 16) - m + spans * 256, spans)


def front_kernel(place_ref, sources_ref, other_ref, lead_ref, body_ref, first_ref, mine_ref, sem, *, blocks, extent):
    copy = pltpu.make_async_copy(sources_ref, mine_ref, sem)
    copy.start()
    height = mine_ref.shape[0]
    pair = 2 * height
    signs, scale = haar_parts(extent, False)
    copy.wait()
    mine, other = mine_ref[...], other_ref[...]
    first_core = core_of(place_ref) == 0
    both = jnp.concatenate([jnp.where(first_core, mine, other), jnp.where(first_core, other, mine)], axis=0)
    parts = [both[:, b * extent : (b + 1) * extent] for b in range(blocks)]
    coef = exact_dot(jnp.concatenate(parts, axis=0), signs) * scale
    columns = block_forward([coef[b * pair : (b + 1) * pair, 0:1] for b in range(blocks)])
    lane = lax.broadcasted_iota(jnp.int32, (pair, extent), 1)
    for b in range(blocks):
        column = jnp.zeros_like(columns[0]) if b == 0 else columns[b]
        block = jnp.where(lane == 0, column, coef[b * pair : (b + 1) * pair, :])
        chunk, at = chunk_of(b, blocks)
        (lead_ref, body_ref)[chunk][at * pair : (at + 1) * pair, :] = block.astype(jnp.bfloat16)
    total = functools.reduce(jnp.add, parts)
    ones = jnp.ones((FIRST_ROWS, extent), jnp.bfloat16)
    first = sum(
        lax.dot_general(ones, term, (((1,), (1,)), ((), ())), preferred_element_type=jnp.float32)
        for term in three_terms(total)
    )
    first_ref[...] = jnp.zeros_like(first_ref)
    first_ref[:, 0:pair] = first * (1.0 / math.sqrt(blocks * extent))


def edge_kernel(
    place_ref,
    rows_ref,
    cols_ref,
    count_ref,
    tiles_ref,
    first_ref,
    _,
    first_cols_ref,
    edge_ref,
    order_ref,
    sizes_ref,
    held_ref,
    sems,
    *,
    blocks,
    owners,
):
    slots, extent = tiles_ref.shape[0], tiles_ref.shape[-1]
    count = count_ref[0]
    x = x_of(place_ref)
    size = slots // FETCHES
    fetches = [
        pltpu.make_async_copy(tiles_ref.at[pl.ds(i * size, size)], held_ref.at[pl.ds(i * size, size)], sems.at[i])
        for i in range(FETCHES)
    ]
    for fetch in fetches:
        fetch.start()
    first_cols_ref[...] = jnp.zeros_like(first_cols_ref)
    edge_ref[...] = jnp.zeros_like(edge_ref)
    edge_ref[owners * blocks : owners * blocks + 8, :] = first_ref[0:8, :]
    pick = (lax.broadcasted_iota(jnp.int32, (SIDE_ROWS, extent), 1) == 0).astype(jnp.bfloat16)

    def visit(slot, sizes):
        row, col = rows_ref[slot], cols_ref[slot]
        owner, block = col // blocks, lax.rem(col, blocks)
        behind = lax.rem(x - owner + owners, owners)
        own = (behind == 0).astype(jnp.int32)
        side = jnp.where(behind == 0, block, (behind - 1) * blocks + block)
        order_ref[1 - own, jnp.where(own == 1, sizes[0], sizes[1])] = (slot << 16) + (side << 8) + row
        return sizes[0] + own, sizes[1] + 1 - own

    sizes = lax.fori_loop(0, count, visit, (jnp.int32(0), jnp.int32(0)))
    for which in range(2):
        sizes_ref[which] = sizes[which]
        for k in range(UNROLL - 1):
            order_ref[which, sizes[which] + k] = blocks

    def add(slot, _):
        row, col = rows_ref[slot], cols_ref[slot]

        @pl.when(lax.rem(col, blocks) == 0)
        def _():
            first_cols_ref[pl.ds(col + row, 1), :] += held_ref[slot, 0:SIDE_ROWS, :].astype(jnp.float32)[0:1, :]

        @pl.when(row == 0)
        def _():
            column = lax.dot_general(
                pick, held_ref[slot], (((1,), (1,)), ((), ())), preferred_element_type=jnp.float32
            )
            edge_ref[pl.ds(col, 1), :] += column[0:1, :]

        return 0

    for i, fetch in enumerate(fetches):
        fetch.wait()
        lax.fori_loop(jnp.minimum(count, i * size), jnp.minimum(count, (i + 1) * size), add, 0)


def seal_kernel(place_ref, body_ref, *refs, blocks, owners):
    edges, (out_ref, line_ref, rest_ref) = refs[:owners], refs[owners:]
    x = x_of(place_ref)
    by_x = []
    for i in range(owners):
        value = edges[0][...]
        for j in range(1, owners):
            value = jnp.where(lax.rem(x - i + owners, owners) == j, edges[j][...], value)
        by_x.append(value)
    length = owners * blocks
    line_ref[...] = by_x[0][0:length, :]
    for i in range(1, owners):
        rest_ref[i - 1] = by_x[i][0:length, :]
    firsts = block_forward([value[length : length + 1, :] for value in by_x])
    row = lax.broadcasted_iota(jnp.int32, (SIDE_ROWS, body_ref.shape[1]), 0)
    side = jnp.zeros(row.shape, jnp.float32)
    for i, first in enumerate(firsts):
        for k, term in enumerate(three_terms(first)):
            side = jnp.where(row == 3 * i + k, term.astype(jnp.float32), side)
    rows = body_ref.shape[0]
    out_ref[0:rows, :] = body_ref[...]
    out_ref[rows:, :] = side.astype(jnp.bfloat16)


def firsts_kernel(place_ref, *refs, owners, spans, pair):
    messages, out_ref = refs[:spans], refs[-1]
    total = jnp.zeros(out_ref.shape, jnp.float32)
    row = lax.broadcasted_iota(jnp.int32, out_ref.shape, 0)
    lane = lax.broadcasted_iota(jnp.int32, out_ref.shape, 1)
    for m, message in enumerate(messages):
        side = message[message.shape[0] - SIDE_ROWS :, :].astype(jnp.float32)
        copies = jnp.concatenate([side[:, 0:pair]] * spans, axis=1)
        at = source_span(place_ref, m, spans) * pair
        for i in range(owners):
            value = copies[3 * i : 3 * i + 1, :] + copies[3 * i + 1 : 3 * i + 2, :] + copies[3 * i + 2 : 3 * i + 3, :]
            total = jnp.where((row == i) & (lane >= at) & (lane < at + pair), value, total)
    out_ref[...] = total


def fill_sides(sides, messages, place_ref, blocks, spans):
    pair = sides.shape[1] // spans
    for index in range(len(messages) // CHUNKS):
        behind, m = index // spans, index % spans
        rows = pl.ds(pl.multiple_of(source_span(place_ref, m, spans) * pair, pair), pair)
        for b in range(blocks):
            chunk, at = chunk_of(b, blocks)
            sides[behind * blocks + b, rows, :] = messages[index * CHUNKS + chunk][at * pair : (at + 1) * pair, :]


def add_products(order_ref, sizes_ref, which, tiles_ref, sides, acc):
    def group(index, _):
        for k in range(UNROLL):
            entry = order_ref[which, index * UNROLL + k]
            slot, side, row = entry >> 16, (entry >> 8) & 255, entry & 255
            acc[row] += jnp.dot(sides[side], tiles_ref[slot], preferred_element_type=jnp.float32)
        return 0

    lax.fori_loop(0, (sizes_ref[which] + UNROLL - 1) // UNROLL, group, 0)


def near_kernel(place_ref, order_ref, sizes_ref, tiles_ref, *refs, blocks, spans):
    *messages, acc_ref, sides = refs
    fill_sides(sides, messages, place_ref, blocks, spans)
    acc_ref[...] = jnp.zeros_like(acc_ref)
    add_products(order_ref, sizes_ref, 0, tiles_ref, sides, acc_ref)


def far_kernel(
    place_ref, order_ref, sizes_ref, tiles_ref, near_ref, firsts_ref, cols_ref, row_ref, *refs, blocks, owners, spans
):
    direct, swapped = refs[: spans * CHUNKS], refs[spans * CHUNKS : owners * spans * CHUNKS]
    keep_ref, send_ref, sides, acc = refs[owners * spans * CHUNKS :]
    extent = tiles_ref.shape[-1]
    pair = sides.shape[1] // spans
    height = pair // 2
    x = x_of(place_ref)
    fill_sides(sides, swapped, place_ref, blocks, spans)
    messages = (*direct, *swapped)
    columns = jnp.transpose(firsts_ref[...])
    for i in range(blocks):
        total = near_ref[i]
        for owner in range(owners):
            total += columns[:, owner : owner + 1] * cols_ref[owner * blocks + i : owner * blocks + i + 1, :]
        acc[i] = total
    add_products(order_ref, sizes_ref, 1, tiles_ref, sides, acc)

    top = jnp.zeros((spans * pair, 1), jnp.float32)
    for owner in range(owners):
        top += columns[:, owner : owner + 1] * row_ref[owner * blocks : owner * blocks + 1, 0:1]
    lane = lax.broadcasted_iota(jnp.int32, (spans * pair, extent), 1)
    acc[0] = jnp.where(lane == 0, top, acc[0])
    lane = lane[0:pair]
    for m in range(spans):
        rows = pl.ds(pl.multiple_of(source_span(place_ref, m, spans) * pair, pair), pair)
        total = jnp.zeros((pair, extent), jnp.float32)
        for behind in range(owners):
            owner = lax.rem(x - behind + owners, owners)
            for b in range(blocks):
                chunk, at = chunk_of(b, blocks)
                message = messages[(behind * spans + m) * CHUNKS + chunk]
                line = row_ref[pl.ds(owner * blocks + b, 1), :]
                total += message[at * pair : (at + 1) * pair, :].astype(jnp.float32) * line
        part = jnp.sum(total, axis=1, keepdims=True)
        acc[0, rows, :] = acc[0, rows, :] + jnp.where(lane == 0, part, 0.0)
    first_core = core_of(place_ref) == 0
    for i in range(blocks):
        value = acc[i]
        for y in range(spans):
            one = value[y * pair : y * pair + height, :]
            two = value[y * pair + height : (y + 1) * pair, :]
            keep_ref[y, i] = jnp.where(first_core, one, two)
            send_ref[y, i] = jnp.where(first_core, two, one)


def combine_kernel(place_ref, keep_ref, arrived_ref, own_ref, *out_refs):
    spans = keep_ref.shape[0]
    span = span_of(place_ref)
    own_ref[...] = keep_ref[span] + arrived_ref[span]
    for j, out_ref in enumerate(out_refs, 1):
        at = lax.rem(span + j, spans)
        out_ref[...] = (keep_ref[at] + arrived_ref[at]).astype(jnp.bfloat16)


def back_kernel(own_ref, *refs):
    *arrived, out_ref = refs
    blocks, height, extent = own_ref.shape
    total = own_ref[...]
    for part in arrived:
        total = total + part[...].astype(jnp.float32)
    columns = block_inverse([total[b][:, 0:1] for b in range(blocks)])
    lane = lax.broadcasted_iota(jnp.int32, (height, extent), 1)
    fixed = jnp.concatenate([jnp.where(lane == 0, columns[b], total[b]) for b in range(blocks)], axis=0)
    signs, scale = haar_parts(extent, True)
    result = exact_dot(fixed * scale, signs)
    for b in range(blocks):
        out_ref[:, b * extent : (b + 1) * extent] = result[b * height : (b + 1) * height, :]


def butterfly(value, partner, index, bit):
    active = index % 2**bit == 0
    upper = index // 2**bit % 2 == 1
    combined = jnp.where(upper, partner - value, partner + value) * ROOT_HALF
    return jnp.where(active, combined, value)


def local(sources, tiles, tile_row, tile_col, tile_count):
    n_row, n_col = lax.axis_size("row"), lax.axis_size("col")
    owners = n_row // n_col
    spans = n_col // 2
    extent = tiles.shape[-1]
    slots = tiles.shape[2]
    height = sources.shape[0]
    blocks = sources.shape[1] // extent
    pair = 2 * height
    last = blocks // 4
    row_index, col_index = lax.axis_index("row"), lax.axis_index("col")
    z, x = row_index // owners, row_index % owners
    span, core = col_index // 2, col_index % 2

    def moved(value, to):
        pairs = []
        for a in range(n_row):
            for b in range(n_col):
                zz, xx, yy, cc = to(a // owners, a % owners, b // 2, b % 2)
                pairs.append((a * n_col + b, (zz * owners + xx) * n_col + yy * 2 + cc))
        return lax.ppermute(value, ("row", "col"), pairs)

    def other_core(value):
        return moved(value, lambda zz, xx, yy, cc: (zz, xx, yy, 1 - cc))

    def along_x(value, j):
        return moved(value, lambda zz, xx, yy, cc: (zz, (xx + j) % owners, yy, cc))

    smem = pl.BlockSpec(memory_space=pltpu.SMEM)
    vmem = pl.BlockSpec(memory_space=pltpu.VMEM)
    hbm = pl.BlockSpec(memory_space=pltpu.HBM)
    unread = pl.BlockSpec(memory_space=pl.ANY)

    def call(kernel, name, out_shape, in_specs, out_specs, limit=16, scratch=(), flops=0, moved_bytes=MIB, **sizes):
        return pl.pallas_call(
            functools.partial(kernel, **sizes) if sizes else kernel,
            out_shape=out_shape,
            in_specs=in_specs,
            out_specs=out_specs,
            scratch_shapes=scratch,
            name=name,
            compiler_params=pltpu.CompilerParams(vmem_limit_bytes=int(limit * MIB)),
            cost_estimate=pl.CostEstimate(flops=flops, bytes_accessed=moved_bytes, transcendentals=0),
        )

    def in_hbm(value):
        return pltpu.with_memory_space_constraint(value, pltpu.HBM)

    def f32(*dims):
        return jax.ShapeDtypeStruct(dims, jnp.float32)

    def bf16(*dims):
        return jax.ShapeDtypeStruct(dims, jnp.bfloat16)

    place = packed_place(core, span, x, z)

    def after(value, *others):
        return lax.optimization_barrier((value, *others))[0]

    length = owners * blocks
    lead, body, first = call(
        front_kernel,
        "front",
        [bf16((blocks - last) * pair, extent), bf16(last * pair, extent), f32(FIRST_ROWS, extent)],
        [smem, hbm, vmem],
        [vmem] * 3,
        scratch=[pltpu.VMEM(sources.shape, jnp.float32), pltpu.SemaphoreType.DMA],
        blocks=blocks,
        extent=extent,
    )(place, in_hbm(sources), other_core(sources))

    def spread(message):
        return [
            moved(message, lambda zz, xx, yy, cc, m=m: (cc * spans + (yy + m) % spans, xx, zz // 2, zz % 2))
            for m in range(spans)
        ]

    direct_lead = spread(lead)
    stack = tiles.reshape(slots, extent, extent)
    first_cols, edge, order, sizes, held = call(
        edge_kernel,
        "edges",
        [
            f32(length, extent),
            f32(length + 8, extent),
            pltpu.SMEM((2, slots + UNROLL), jnp.int32),
            pltpu.SMEM((2,), jnp.int32),
            pltpu.VMEM((slots, extent, extent), jnp.bfloat16),
        ],
        [smem] * 4 + [hbm, vmem, unread],
        [vmem] * 2 + [smem] * 2 + [vmem],
        scratch=[pltpu.SemaphoreType.DMA((FETCHES,))],
        blocks=blocks,
        owners=owners,
    )(
        place,
        in_hbm(tile_row.reshape(-1)),
        in_hbm(tile_col.reshape(-1)),
        tile_count.reshape(1),
        in_hbm(stack),
        first,
        direct_lead[0],
    )
    message, line, rest = call(
        seal_kernel,
        "seal",
        [bf16(last * pair + SIDE_ROWS, extent), f32(length, extent), f32(owners - 1, length, extent)],
        [smem] + [vmem] * (1 + owners),
        [vmem] * 3,
        blocks=blocks,
        owners=owners,
    )(place, body, edge, *[along_x(edge, j) for j in range(1, owners)])
    direct_last = spread(message)
    direct = [piece for m in range(spans) for piece in (direct_lead[m], direct_last[m])]
    swapped = [along_x(piece, j) for j in range(1, owners) for piece in direct]

    firsts = call(
        firsts_kernel,
        "firsts",
        f32(FIRST_ROWS, spans * pair),
        [smem] + [vmem] * spans + [unread] * spans,
        vmem,
        owners=owners,
        spans=spans,
        pair=pair,
    )(place, *direct_last, *swapped[0 : CHUNKS * spans : CHUNKS])
    top_row = (jnp.arange(FIRST_ROWS) == 0)[:, None]
    for bit in range(n_col.bit_length() - 1):
        pairs = [(source, source ^ 2**bit) for source in range(n_col)]
        partner = lax.ppermute(firsts, "col", pairs)
        firsts = jnp.where(top_row, butterfly(firsts, partner, col_index, bit), firsts)

    for bit in reversed(range((n_row // owners).bit_length() - 1)):
        partner = moved(line, lambda zz, xx, yy, cc, bit=bit: (zz ^ 2**bit, xx, yy, cc))
        line = after(butterfly(line, partner, z, bit), *direct_last)
    by_x = block_inverse([line] + [rest[i] for i in range(owners - 1)])
    first_row = by_x[0]
    for i in range(1, owners):
        first_row = jnp.where(x == i, by_x[i], first_row)

    every = (spans * pair, extent)
    near = call(
        near_kernel,
        "near",
        f32(blocks + 1, *every),
        [smem] * 3 + [vmem] * (1 + len(direct)),
        vmem,
        scratch=[pltpu.VMEM((blocks, *every), jnp.bfloat16)],
        blocks=blocks,
        spans=spans,
    )(place, order, sizes, held, *direct)

    shape = (spans, blocks, height, extent)
    keep, send = call(
        far_kernel,
        "far",
        [f32(*shape)] * 2,
        [smem] * 3 + [vmem] * (5 + len(direct) + len(swapped)),
        [vmem] * 2,
        limit=24,
        scratch=[
            pltpu.VMEM(((owners - 1) * blocks, *every), jnp.bfloat16),
            pltpu.VMEM((blocks + 1, *every), jnp.float32),
        ],
        blocks=blocks,
        owners=owners,
        spans=spans,
    )(place, order, sizes, held, near, firsts, first_cols, first_row, *direct, *swapped)

    own, *outgoing = call(
        combine_kernel,
        "combine",
        [f32(*shape[1:])] + [bf16(*shape[1:])] * (spans - 1),
        [smem, vmem, vmem],
        [vmem] * spans,
    )(place, keep, other_core(send))
    arrived = [
        moved(value, lambda zz, xx, yy, cc, j=j: (zz, xx, (yy + j) % spans, cc)) for j, value in enumerate(outgoing, 1)
    ]
    return call(back_kernel, "back", f32(*sources.shape), [vmem] * spans, vmem)(own, *arrived)


def solution(mesh):
    return jax.shard_map(
        local,
        mesh=mesh,
        in_specs=(
            P("col", "row"),
            P("row", "col", None, None, None),
            P("row", "col", None),
            P("row", "col", None),
            P("row", "col"),
        ),
        out_specs=P("col", "row"),
        check_vma=False,
    )
```

```python
import functools
import math

import jax
import jax.numpy as jnp
from jax import lax
from jax.experimental import pallas as pl
from jax.experimental.pallas import tpu as pltpu
from jax.sharding import PartitionSpec as P

ROOT_HALF = 1.0 / math.sqrt(2.0)
SIDE_ROWS = 16
UNROLL = 4
MIB = 2**20


def haar_parts(extent, transposed):
    k = lax.broadcasted_iota(jnp.int32, (extent, extent), 1 if transposed else 0)
    n = lax.broadcasted_iota(jnp.int32, (extent, extent), 0 if transposed else 1)
    stride = jnp.where(n == 0, extent, n & -n)
    signs = jnp.where((k ^ n) < 2 * stride, jnp.where((k & stride) == 0, 1.0, -1.0), 0.0)
    n = lax.broadcasted_iota(jnp.int32, (1, extent), 1)
    scale = jnp.full((1, extent), 1.0 / math.sqrt(extent), jnp.float32)
    level = 1
    while level < extent:
        scale = jnp.where((n & -n) == level, 1.0 / math.sqrt(2 * level), scale)
        level *= 2
    return signs.astype(jnp.bfloat16), scale


def three_terms(value):
    high = value.astype(jnp.bfloat16)
    rest = value - high.astype(jnp.float32)
    middle = rest.astype(jnp.bfloat16)
    low = (rest - middle.astype(jnp.float32)).astype(jnp.bfloat16)
    return high, middle, low


def exact_dot(value, signs):
    return sum(jnp.dot(term, signs, preferred_element_type=jnp.float32) for term in three_terms(value))


def block_forward(columns):
    columns = list(columns)
    stride = 1
    while stride < len(columns):
        for p in range(0, len(columns), 2 * stride):
            u, v = columns[p], columns[p + stride]
            columns[p], columns[p + stride] = (u + v) * ROOT_HALF, (u - v) * ROOT_HALF
        stride *= 2
    return columns


def block_inverse(columns):
    columns = list(columns)
    stride = len(columns) // 2
    while stride >= 1:
        for p in range(0, len(columns), 2 * stride):
            u, v = columns[p], columns[p + stride]
            columns[p], columns[p + stride] = (u + v) * ROOT_HALF, (u - v) * ROOT_HALF
        stride //= 2
    return columns


def packed_place(core, span, x, z):
    return (core + 2 * span + 256 * x + 65536 * z).astype(jnp.int32).reshape(1)


def core_of(place_ref):
    return place_ref[0] & 1


def span_of(place_ref):
    return (place_ref[0] >> 1) & 127


def x_of(place_ref):
    return (place_ref[0] >> 8) & 255


def source_span(place_ref, m, spans):
    return lax.rem((place_ref[0] >> 16) - m + spans * 256, spans)


def front_kernel(place_ref, sources_ref, other_ref, out_ref, mine_ref, sem, *, blocks, extent):
    copy = pltpu.make_async_copy(sources_ref, mine_ref, sem)
    copy.start()
    height = mine_ref.shape[0]
    pair = 2 * height
    signs, scale = haar_parts(extent, False)
    copy.wait()
    mine, other = mine_ref[...], other_ref[...]
    first_core = core_of(place_ref) == 0
    both = jnp.concatenate([jnp.where(first_core, mine, other), jnp.where(first_core, other, mine)], axis=0)
    parts = [both[:, b * extent : (b + 1) * extent] for b in range(blocks)]
    coef = exact_dot(jnp.concatenate(parts, axis=0), signs) * scale
    columns = block_forward([coef[b * pair : (b + 1) * pair, 0:1] for b in range(blocks)])
    lane = lax.broadcasted_iota(jnp.int32, (pair, extent), 1)
    for b in range(blocks):
        column = jnp.zeros_like(columns[0]) if b == 0 else columns[b]
        block = jnp.where(lane == 0, column, coef[b * pair : (b + 1) * pair, :])
        out_ref[b * pair : (b + 1) * pair, :] = block.astype(jnp.bfloat16)
    total = functools.reduce(jnp.add, parts)
    ones = jnp.ones((SIDE_ROWS, extent), jnp.bfloat16)
    first = sum(
        lax.dot_general(ones, term, (((1,), (1,)), ((), ())), preferred_element_type=jnp.float32)
        for term in three_terms(total)
    ) * (1.0 / math.sqrt(blocks * extent))
    high, middle, low = (term.astype(jnp.float32) for term in three_terms(first))
    row = lax.broadcasted_iota(jnp.int32, first.shape, 0)
    side = jnp.where(row == 0, high, jnp.where(row == 1, middle, jnp.where(row == 2, low, 0.0)))
    out_ref[blocks * pair :, :] = jnp.zeros((SIDE_ROWS, extent), jnp.bfloat16)
    out_ref[blocks * pair :, 0:pair] = side.astype(jnp.bfloat16)


def list_kernel(place_ref, rows_ref, cols_ref, count_ref, order_ref, sizes_ref, *, blocks, owners):
    x = x_of(place_ref)

    def visit(slot, sizes):
        row, col = rows_ref[slot], cols_ref[slot]
        owner, block = col // blocks, lax.rem(col, blocks)
        behind = lax.rem(x - owner + owners, owners)
        near = behind == 0
        side = jnp.where(near, block, (behind - 1) * blocks + block)
        entry = (slot << 16) + (side << 8) + row
        plain = (slot << 16) + (col << 8) + row
        near_size, far_size, row_size, col_size = sizes
        order_ref[jnp.where(near, 0, 1), jnp.where(near, near_size, far_size)] = entry
        order_ref[2, row_size] = plain
        order_ref[3, col_size] = plain
        one = near.astype(jnp.int32)
        return (
            near_size + one,
            far_size + 1 - one,
            row_size + (row == 0).astype(jnp.int32),
            col_size + (block == 0).astype(jnp.int32),
        )

    sizes = lax.fori_loop(0, count_ref[0], visit, (jnp.int32(0),) * 4)
    for which in range(4):
        sizes_ref[which] = sizes[which]
    for which in range(2):
        for k in range(UNROLL - 1):
            order_ref[which, sizes[which] + k] = blocks


def edge_kernel(_, order_ref, sizes_ref, tiles_ref, cols_ref, line_ref, strips, held, strip_sems, held_sems):
    extent = tiles_ref.shape[-1]

    def strip_copy(index):
        slot = order_ref[3, index] >> 16
        return pltpu.make_async_copy(tiles_ref.at[slot, 0:SIDE_ROWS, :], strips.at[index], strip_sems.at[index])

    def tile_copy(index):
        slot = order_ref[2, index] >> 16
        return pltpu.make_async_copy(tiles_ref.at[slot], held.at[index], held_sems.at[index])

    lax.fori_loop(0, sizes_ref[2], lambda i, _: (tile_copy(i).start(), 0)[1], 0)
    lax.fori_loop(0, sizes_ref[3], lambda i, _: (strip_copy(i).start(), 0)[1], 0)
    cols_ref[...] = jnp.zeros_like(cols_ref)
    line_ref[...] = jnp.zeros_like(line_ref)
    pick = (lax.broadcasted_iota(jnp.int32, (SIDE_ROWS, extent), 1) == 0).astype(jnp.bfloat16)

    def add_strip(index, _):
        entry = order_ref[3, index]
        strip_copy(index).wait()
        at = pl.ds(((entry >> 8) & 255) + (entry & 255), 1)
        cols_ref[at, :] += strips[index].astype(jnp.float32)[0:1, :]
        return 0

    def add_column(index, _):
        tile_copy(index).wait()
        column = lax.dot_general(pick, held[index], (((1,), (1,)), ((), ())), preferred_element_type=jnp.float32)
        line_ref[pl.ds((order_ref[2, index] >> 8) & 255, 1), :] += column[0:1, :]
        return 0

    lax.fori_loop(0, sizes_ref[3], add_strip, 0)
    lax.fori_loop(0, sizes_ref[2], add_column, 0)


def corner_kernel(place_ref, lead_ref, partner_ref, cols_ref, *refs, blocks, owners):
    lines, (out_ref, line_ref, rest_ref) = refs[:owners], refs[owners:]
    lead, partner = lead_ref[...], partner_ref[...]
    lead = jnp.where(core_of(place_ref) == 1, partner - lead, partner + lead) * ROOT_HALF
    columns = [lead[0:blocks, :]] + [cols_ref[i * blocks : (i + 1) * blocks, :] for i in range(1, owners)]
    for i, column in enumerate(block_inverse(columns)):
        out_ref[i * blocks : (i + 1) * blocks, :] = column
    index = lax.broadcasted_iota(jnp.int32, line_ref.shape, 0)
    lane = lax.broadcasted_iota(jnp.int32, line_ref.shape, 1)
    for x in range(owners):
        line = lines[x][...]
        corner = [lead[blocks + x : blocks + x + 1, :]] + [line[i * blocks : i * blocks + 1, :] for i in range(1, owners)]
        for i, value in enumerate(block_inverse(corner)):
            line = jnp.where((index == i * blocks) & (lane == 0), value[:, 0:1], line)
        if x == 0:
            line_ref[...] = line
        else:
            rest_ref[x - 1] = line


def fill_sides(sides, messages, place_ref, blocks, spans):
    pair = sides.shape[1] // spans
    for index, message in enumerate(messages):
        behind, m = index // spans, index % spans
        rows = pl.ds(pl.multiple_of(source_span(place_ref, m, spans) * pair, pair), pair)
        for b in range(blocks):
            sides[behind * blocks + b, rows, :] = message[b * pair : (b + 1) * pair, :]


def start_tiles(order_ref, sizes_ref, which, tiles_ref, held, sems):
    def start(index, _):
        slot = order_ref[which, index] >> 16
        pltpu.make_async_copy(tiles_ref.at[slot], held.at[index], sems.at[index]).start()
        return 0

    lax.fori_loop(0, (sizes_ref[which] + UNROLL - 1) // UNROLL * UNROLL, start, 0)


def add_products(order_ref, sizes_ref, which, tiles_ref, held, sems, sides, acc):
    def group(index, _):
        for k in range(UNROLL):
            at = index * UNROLL + k
            pltpu.make_async_copy(tiles_ref.at[0], held.at[at], sems.at[at]).wait()
        for k in range(UNROLL):
            at = index * UNROLL + k
            entry = order_ref[which, at]
            side, row = (entry >> 8) & 255, entry & 255
            acc[row] += jnp.dot(sides[side], held[at], preferred_element_type=jnp.float32)
        return 0

    lax.fori_loop(0, (sizes_ref[which] + UNROLL - 1) // UNROLL, group, 0)


def near_kernel(place_ref, order_ref, sizes_ref, tiles_ref, *refs, blocks, spans):
    *messages, acc_ref, sides, held, sems = refs
    start_tiles(order_ref, sizes_ref, 0, tiles_ref, held, sems)
    fill_sides(sides, messages, place_ref, blocks, spans)
    acc_ref[...] = jnp.zeros_like(acc_ref)
    add_products(order_ref, sizes_ref, 0, tiles_ref, held, sems, sides, acc_ref)


def far_kernel(place_ref, order_ref, sizes_ref, tiles_ref, near_ref, cols_ref, row_ref, *refs, blocks, owners, spans):
    direct, swapped = refs[:spans], refs[spans : owners * spans]
    keep_ref, send_ref, sides, acc, firsts, held, sems = refs[owners * spans :]
    start_tiles(order_ref, sizes_ref, 1, tiles_ref, held, sems)
    extent = tiles_ref.shape[-1]
    pair = sides.shape[1] // spans
    height = pair // 2
    x = x_of(place_ref)
    fill_sides(sides, swapped, place_ref, blocks, spans)
    messages = (*direct, *swapped)
    for index, message in enumerate(messages):
        owner = lax.rem(x - index // spans + owners, owners)
        side = jnp.transpose(message[blocks * pair :, :].astype(jnp.float32))
        column = side[0:pair, 0:1] + side[0:pair, 1:2] + side[0:pair, 2:3]
        rows = pl.ds(pl.multiple_of(source_span(place_ref, index % spans, spans) * pair, pair), pair)
        firsts[owner, rows, :] = jnp.broadcast_to(column, (pair, firsts.shape[2]))
    for i in range(blocks):
        total = near_ref[i]
        for owner in range(owners):
            total += firsts[owner][:, 0:1] * cols_ref[owner * blocks + i : owner * blocks + i + 1, :]
        acc[i] = total
    add_products(order_ref, sizes_ref, 1, tiles_ref, held, sems, sides, acc)

    lane = lax.broadcasted_iota(jnp.int32, (pair, extent), 1)
    for m in range(spans):
        rows = pl.ds(pl.multiple_of(source_span(place_ref, m, spans) * pair, pair), pair)
        total = jnp.zeros((pair, extent), jnp.float32)
        top = jnp.zeros((pair, 1), jnp.float32)
        for behind in range(owners):
            owner = lax.rem(x - behind + owners, owners)
            message = messages[behind * spans + m]
            for b in range(blocks):
                line = row_ref[pl.ds(owner * blocks + b, 1), :]
                total += message[b * pair : (b + 1) * pair, :].astype(jnp.float32) * line
                if b == 0:
                    top += firsts[owner, rows, :][:, 0:1] * line[:, 0:1]
        top += jnp.sum(total, axis=1, keepdims=True)
        acc[0, rows, :] = jnp.where(lane == 0, top, acc[0, rows, :])
    first_core = core_of(place_ref) == 0
    for i in range(blocks):
        value = acc[i]
        for y in range(spans):
            one = value[y * pair : y * pair + height, :]
            two = value[y * pair + height : (y + 1) * pair, :]
            keep_ref[y, i] = jnp.where(first_core, one, two)
            send_ref[y, i] = jnp.where(first_core, two, one)


def combine_kernel(place_ref, keep_ref, arrived_ref, own_ref, *out_refs):
    spans = keep_ref.shape[0]
    span = span_of(place_ref)
    own_ref[...] = keep_ref[span] + arrived_ref[span]
    for j, out_ref in enumerate(out_refs, 1):
        at = lax.rem(span + j, spans)
        out_ref[...] = (keep_ref[at] + arrived_ref[at]).astype(jnp.bfloat16)


def back_kernel(own_ref, *refs):
    *arrived, out_ref = refs
    blocks, height, extent = own_ref.shape
    total = own_ref[...]
    for part in arrived:
        total = total + part[...].astype(jnp.float32)
    columns = block_inverse([total[b][:, 0:1] for b in range(blocks)])
    lane = lax.broadcasted_iota(jnp.int32, (height, extent), 1)
    fixed = jnp.concatenate([jnp.where(lane == 0, columns[b], total[b]) for b in range(blocks)], axis=0)
    signs, scale = haar_parts(extent, True)
    result = exact_dot(fixed * scale, signs)
    for b in range(blocks):
        out_ref[:, b * extent : (b + 1) * extent] = result[b * height : (b + 1) * height, :]


def butterfly(value, partner, index, bit):
    active = index % 2**bit == 0
    upper = index // 2**bit % 2 == 1
    combined = jnp.where(upper, partner - value, partner + value) * ROOT_HALF
    return jnp.where(active, combined, value)


def local(sources, tiles, tile_row, tile_col, tile_count):
    n_row, n_col = lax.axis_size("row"), lax.axis_size("col")
    owners = n_row // n_col
    spans = n_col // 2
    extent = tiles.shape[-1]
    slots = tiles.shape[2]
    height = sources.shape[0]
    blocks = sources.shape[1] // extent
    pair = 2 * height
    row_index, col_index = lax.axis_index("row"), lax.axis_index("col")
    z, x = row_index // owners, row_index % owners
    span, core = col_index // 2, col_index % 2

    def moved(value, to):
        pairs = []
        for a in range(n_row):
            for b in range(n_col):
                zz, xx, yy, cc = to(a // owners, a % owners, b // 2, b % 2)
                pairs.append((a * n_col + b, (zz * owners + xx) * n_col + yy * 2 + cc))
        return lax.ppermute(value, ("row", "col"), pairs)

    def other_core(value):
        return moved(value, lambda zz, xx, yy, cc: (zz, xx, yy, 1 - cc))

    def along_x(value, j):
        return moved(value, lambda zz, xx, yy, cc: (zz, (xx + j) % owners, yy, cc))

    smem = pl.BlockSpec(memory_space=pltpu.SMEM)
    vmem = pl.BlockSpec(memory_space=pltpu.VMEM)
    hbm = pl.BlockSpec(memory_space=pltpu.HBM)

    def call(kernel, name, out_shape, in_specs, out_specs, limit=16, scratch=(), flops=0, moved_bytes=MIB, **sizes):
        return pl.pallas_call(
            functools.partial(kernel, **sizes) if sizes else kernel,
            out_shape=out_shape,
            in_specs=in_specs,
            out_specs=out_specs,
            scratch_shapes=scratch,
            name=name,
            compiler_params=pltpu.CompilerParams(vmem_limit_bytes=int(limit * MIB)),
            cost_estimate=pl.CostEstimate(flops=flops, bytes_accessed=moved_bytes, transcendentals=0),
        )

    def in_hbm(value):
        return pltpu.with_memory_space_constraint(value, pltpu.HBM)

    def f32(*dims):
        return jax.ShapeDtypeStruct(dims, jnp.float32)

    def bf16(*dims):
        return jax.ShapeDtypeStruct(dims, jnp.bfloat16)

    place = packed_place(core, span, x, z)

    def after(value, *others):
        return lax.optimization_barrier((value, *others))[0]

    def apart(body, state):
        return lax.fori_loop(0, jnp.minimum(tile_count.reshape(()), 1), body, tuple(state))

    length = owners * blocks
    stack = tiles.reshape(slots, extent, extent)
    from_core = other_core(sources)
    order, sizes = call(
        list_kernel,
        "lists",
        [pltpu.SMEM((4, slots + UNROLL), jnp.int32), pltpu.SMEM((4,), jnp.int32)],
        [smem] * 4,
        [smem] * 2,
        blocks=blocks,
        owners=owners,
    )(place, in_hbm(tile_row.reshape(-1)), in_hbm(tile_col.reshape(-1)), tile_count.reshape(1))
    message = call(
        front_kernel,
        "front",
        bf16(blocks * pair + SIDE_ROWS, extent),
        [smem, hbm, vmem],
        vmem,
        scratch=[pltpu.VMEM(sources.shape, jnp.float32), pltpu.SemaphoreType.DMA],
        blocks=blocks,
        extent=extent,
    )(place, in_hbm(sources), from_core)

    direct = [
        moved(message, lambda zz, xx, yy, cc, m=m: (cc * spans + (yy + m) % spans, xx, zz // 2, zz % 2))
        for m in range(spans)
    ]

    def early(trip, _):
        cols, line = call(
            edge_kernel,
            "edges",
            [f32(length, extent)] * 2,
            [smem, smem, smem, hbm],
            [vmem] * 2,
            scratch=[
                pltpu.VMEM((slots, SIDE_ROWS, extent), jnp.bfloat16),
                pltpu.VMEM((slots, extent, extent), jnp.bfloat16),
                pltpu.SemaphoreType.DMA((slots,)),
                pltpu.SemaphoreType.DMA((slots,)),
            ],
        )(trip.reshape(1), order, sizes, in_hbm(stack))
        behind = [line] + [along_x(line, j) for j in range(1, owners)]
        lines = []
        for i in range(owners):
            value = behind[0]
            for j in range(1, owners):
                value = jnp.where((x - i) % owners == j, behind[j], value)
            lines.append(value)
        lead = jnp.concatenate([cols[0:blocks]] + [value[0:1] for value in lines] + [cols[0 : blocks - owners]])
        for bit in reversed(range(1, n_col.bit_length() - 1)):
            step = 2 ** (bit - 1)
            partner = moved(lead, lambda zz, xx, yy, cc, step=step: (zz, xx, yy ^ step, cc))
            lead = butterfly(lead, partner, col_index, bit)
        return (lead, cols, *lines)

    sized = [jnp.zeros((2 * blocks, extent), jnp.float32)] + [jnp.zeros((length, extent), jnp.float32)] * (1 + owners)
    lead, cols, *lines = apart(early, sized)
    swapped = [along_x(after(piece, lead), j) for j in range(1, owners) for piece in direct]
    lead = after(lead, direct[0])

    def late(_, state):
        lead, cols, *lines = state
        first_cols, line, rest = call(
            corner_kernel,
            "corner",
            [f32(length, extent)] * 2 + [f32(owners - 1, length, extent)],
            [smem] + [vmem] * (3 + owners),
            [vmem] * 3,
            blocks=blocks,
            owners=owners,
        )(place, lead, other_core(lead), cols, *lines)
        for bit in reversed(range((n_row // owners).bit_length() - 1)):
            partner = moved(line, lambda zz, xx, yy, cc, bit=bit: (zz ^ 2**bit, xx, yy, cc))
            line = butterfly(line, partner, z, bit)
        by_x = block_inverse([line] + [rest[i] for i in range(owners - 1)])
        first_row = by_x[0]
        for i in range(1, owners):
            first_row = jnp.where(x == i, by_x[i], first_row)
        return (lead, first_cols, first_row, *lines[1:])

    _, first_cols, first_row, *_ = apart(late, [lead, cols, *lines])

    every = (spans * pair, extent)
    held_tiles = [
        pltpu.VMEM((slots + UNROLL, extent, extent), jnp.bfloat16),
        pltpu.SemaphoreType.DMA((slots + UNROLL,)),
    ]
    near = call(
        near_kernel,
        "near",
        f32(blocks + 1, *every),
        [smem] * 3 + [hbm] + [vmem] * len(direct),
        vmem,
        limit=24,
        scratch=[pltpu.VMEM((blocks, *every), jnp.bfloat16), *held_tiles],
        blocks=blocks,
        spans=spans,
    )(place, order, sizes, in_hbm(stack), *direct)

    shape = (spans, blocks, height, extent)
    keep, send = call(
        far_kernel,
        "far",
        [f32(*shape)] * 2,
        [smem] * 3 + [hbm] + [vmem] * (3 + len(direct) + len(swapped)),
        [vmem] * 2,
        limit=24,
        scratch=[
            pltpu.VMEM(((owners - 1) * blocks, *every), jnp.bfloat16),
            pltpu.VMEM((blocks + 1, *every), jnp.float32),
            pltpu.VMEM((owners, spans * pair, 128), jnp.float32),
            *held_tiles,
        ],
        blocks=blocks,
        owners=owners,
        spans=spans,
    )(place, order, sizes, in_hbm(stack), near, first_cols, first_row, *direct, *swapped)

    own, *outgoing = call(
        combine_kernel,
        "combine",
        [f32(*shape[1:])] + [bf16(*shape[1:])] * (spans - 1),
        [smem, vmem, vmem],
        [vmem] * spans,
    )(place, keep, other_core(send))
    arrived = [
        moved(value, lambda zz, xx, yy, cc, j=j: (zz, xx, (yy + j) % spans, cc)) for j, value in enumerate(outgoing, 1)
    ]
    return call(back_kernel, "back", f32(*sources.shape), [vmem] * spans, vmem)(own, *arrived)


def solution(mesh):
    return jax.shard_map(
        local,
        mesh=mesh,
        in_specs=(
            P("col", "row"),
            P("row", "col", None, None, None),
            P("row", "col", None),
            P("row", "col", None),
            P("row", "col"),
        ),
        out_specs=P("col", "row"),
        check_vma=False,
    )
```

```python
import functools
import math

import jax
import jax.numpy as jnp
from jax import lax
from jax.experimental import pallas as pl
from jax.experimental.pallas import tpu as pltpu
from jax.sharding import PartitionSpec as P

ROOT_HALF = 1.0 / math.sqrt(2.0)
SIDE_ROWS = 16
UNROLL = 4
LANES = 128
MIB = 2**20


def haar_parts(extent, transposed):
    k = lax.broadcasted_iota(jnp.int32, (extent, extent), 1 if transposed else 0)
    n = lax.broadcasted_iota(jnp.int32, (extent, extent), 0 if transposed else 1)
    stride = jnp.where(n == 0, extent, n & -n)
    signs = jnp.where((k ^ n) < 2 * stride, jnp.where((k & stride) == 0, 1.0, -1.0), 0.0)
    n = lax.broadcasted_iota(jnp.int32, (1, extent), 1)
    scale = jnp.full((1, extent), 1.0 / math.sqrt(extent), jnp.float32)
    level = 1
    while level < extent:
        scale = jnp.where((n & -n) == level, 1.0 / math.sqrt(2 * level), scale)
        level *= 2
    return signs.astype(jnp.bfloat16), scale


def three_terms(value):
    high = value.astype(jnp.bfloat16)
    rest = value - high.astype(jnp.float32)
    middle = rest.astype(jnp.bfloat16)
    low = (rest - middle.astype(jnp.float32)).astype(jnp.bfloat16)
    return high, middle, low


def exact_dot(value, signs):
    return sum(jnp.dot(term, signs, preferred_element_type=jnp.float32) for term in three_terms(value))


def block_forward(columns):
    columns = list(columns)
    stride = 1
    while stride < len(columns):
        for p in range(0, len(columns), 2 * stride):
            u, v = columns[p], columns[p + stride]
            columns[p], columns[p + stride] = (u + v) * ROOT_HALF, (u - v) * ROOT_HALF
        stride *= 2
    return columns


def block_inverse(columns):
    columns = list(columns)
    stride = len(columns) // 2
    while stride >= 1:
        for p in range(0, len(columns), 2 * stride):
            u, v = columns[p], columns[p + stride]
            columns[p], columns[p + stride] = (u + v) * ROOT_HALF, (u - v) * ROOT_HALF
        stride //= 2
    return columns


def packed_place(core, span, x, z):
    return (core + 2 * span + 256 * x + 65536 * z).astype(jnp.int32).reshape(1)


def core_of(place_ref):
    return place_ref[0] & 1


def span_of(place_ref):
    return (place_ref[0] >> 1) & 127


def x_of(place_ref):
    return (place_ref[0] >> 8) & 255


def z_of(place_ref):
    return place_ref[0] >> 16


def source_span(place_ref, m, spans):
    return lax.rem(z_of(place_ref) - m + spans * 256, spans)


def front_kernel(place_ref, sources_ref, other_ref, _, out_ref, mine_ref, sem, *, blocks, extent):
    copy = pltpu.make_async_copy(sources_ref, mine_ref, sem)
    copy.start()
    height = mine_ref.shape[0]
    pair = 2 * height
    signs, scale = haar_parts(extent, False)
    copy.wait()
    mine, other = mine_ref[...], other_ref[...]
    first_core = core_of(place_ref) == 0
    both = jnp.concatenate([jnp.where(first_core, mine, other), jnp.where(first_core, other, mine)], axis=0)
    parts = [both[:, b * extent : (b + 1) * extent] for b in range(blocks)]
    coef = exact_dot(jnp.concatenate(parts, axis=0), signs) * scale
    columns = block_forward([coef[b * pair : (b + 1) * pair, 0:1] for b in range(blocks)])
    lane = lax.broadcasted_iota(jnp.int32, (pair, extent), 1)
    for b in range(blocks):
        column = jnp.zeros_like(columns[0]) if b == 0 else columns[b]
        block = jnp.where(lane == 0, column, coef[b * pair : (b + 1) * pair, :])
        out_ref[b * pair : (b + 1) * pair, :] = block.astype(jnp.bfloat16)
    total = functools.reduce(jnp.add, parts)
    ones = jnp.ones((SIDE_ROWS, extent), jnp.bfloat16)
    first = sum(
        lax.dot_general(ones, term, (((1,), (1,)), ((), ())), preferred_element_type=jnp.float32)
        for term in three_terms(total)
    ) * (1.0 / math.sqrt(blocks * extent))
    high, middle, low = (term.astype(jnp.float32) for term in three_terms(first))
    row = lax.broadcasted_iota(jnp.int32, first.shape, 0)
    side = jnp.where(row == 0, high, jnp.where(row == 1, middle, jnp.where(row == 2, low, 0.0)))
    out_ref[blocks * pair :, :] = jnp.zeros((SIDE_ROWS, extent), jnp.bfloat16)
    out_ref[blocks * pair :, 0:pair] = side.astype(jnp.bfloat16)


def list_kernel(
    place_ref, rows_ref, cols_ref, count_ref, order_ref, sizes_ref, lead_ref, others_ref, *, blocks, owners
):
    lead_ref[...] = jnp.zeros_like(lead_ref)
    others_ref[...] = jnp.zeros_like(others_ref)
    x = x_of(place_ref)

    def visit(slot, sizes):
        row, col = rows_ref[slot], cols_ref[slot]
        owner, block = col // blocks, lax.rem(col, blocks)
        behind = lax.rem(x - owner + owners, owners)
        near = behind == 0
        side = jnp.where(near, block, (behind - 1) * blocks + block)
        entry = (slot << 16) + (side << 8) + row
        plain = (slot << 16) + (col << 8) + row
        near_size, far_size, row_size, col_size = sizes
        order_ref[jnp.where(near, 0, 1), jnp.where(near, near_size, far_size)] = entry
        order_ref[2, row_size] = plain
        order_ref[3, col_size] = plain
        one = near.astype(jnp.int32)
        return (
            near_size + one,
            far_size + 1 - one,
            row_size + (row == 0).astype(jnp.int32),
            col_size + (block == 0).astype(jnp.int32),
        )

    sizes = lax.fori_loop(0, count_ref[0], visit, (jnp.int32(0),) * 4)
    for which in range(4):
        sizes_ref[which] = sizes[which]
    for which in range(2):
        for k in range(UNROLL - 1):
            order_ref[which, sizes[which] + k] = blocks


def edge_kernel(
    _, order_ref, sizes_ref, tiles_ref, cols_ref, line_ref, strips, columns, summed, strip_sems, column_sems
):
    def strip_copy(index):
        slot = order_ref[3, index] >> 16
        return pltpu.make_async_copy(tiles_ref.at[slot, 0:SIDE_ROWS, :], strips.at[index], strip_sems.at[index])

    def column_copy(index):
        slot = order_ref[2, index] >> 16
        return pltpu.make_async_copy(tiles_ref.at[slot, :, 0:LANES], columns.at[index], column_sems.at[index])

    lax.fori_loop(0, sizes_ref[2], lambda i, _: (column_copy(i).start(), 0)[1], 0)
    lax.fori_loop(0, sizes_ref[3], lambda i, _: (strip_copy(i).start(), 0)[1], 0)
    cols_ref[...] = jnp.zeros_like(cols_ref)
    summed[...] = jnp.zeros_like(summed)
    lane = lax.broadcasted_iota(jnp.int32, summed.shape, 1)

    def add_strip(index, _):
        entry = order_ref[3, index]
        strip_copy(index).wait()
        at = pl.ds(((entry >> 8) & 255) + (entry & 255), 1)
        cols_ref[at, :] += strips[index].astype(jnp.float32)[0:1, :]
        return 0

    def add_column(index, _):
        column_copy(index).wait()
        column = columns[index].astype(jnp.float32)[:, 0:1]
        summed[...] += jnp.where(lane == ((order_ref[2, index] >> 8) & 255), column, 0.0)
        return 0

    lax.fori_loop(0, sizes_ref[3], add_strip, 0)
    lax.fori_loop(0, sizes_ref[2], add_column, 0)
    line_ref[...] = jnp.transpose(summed[...])[0 : line_ref.shape[0], :]


def butterfly(value, partner, index, bit):
    active = lax.rem(index, 2**bit) == 0
    upper = ((index >> bit) & 1) == 1
    return jnp.where(active, jnp.where(upper, partner - value, partner + value) * ROOT_HALF, value)


def pack_kernel(cols_ref, *refs, blocks):
    lines, lead_ref = refs[:-1], refs[-1]
    lead_ref[...] = jnp.zeros_like(lead_ref)
    lead_ref[0:blocks, :] = cols_ref[0:blocks, :]
    for j, line in enumerate(lines):
        lead_ref[blocks + j : blocks + j + 1, :] = line[0:1, :]


def col_level_kernel(place_ref, value_ref, partner_ref, out_ref, *, bit):
    index = 2 * span_of(place_ref) + core_of(place_ref)
    out_ref[...] = butterfly(value_ref[...], partner_ref[...], index, bit)


def join_kernel(*refs):
    *parts, out_ref = refs
    at = 0
    for part in parts:
        out_ref[at : at + part.shape[0], :] = part[...]
        at += part.shape[0]


def row_level_kernel(place_ref, value_ref, partner_ref, out_ref, *, bit):
    out_ref[...] = butterfly(value_ref[...], partner_ref[...], z_of(place_ref), bit)


def x_levels_kernel(place_ref, cols_ref, line_ref, rest_ref, out_ref):
    x = x_of(place_ref)
    by_x = block_inverse([line_ref[...]] + [rest_ref[i] for i in range(rest_ref.shape[0])])
    value = by_x[0]
    for i in range(1, len(by_x)):
        value = jnp.where(x == i, by_x[i], value)
    length = value.shape[0]
    out_ref[0:length, :] = cols_ref[...]
    out_ref[length : 2 * length, :] = value
    out_ref[2 * length :, :] = jnp.zeros((out_ref.shape[0] - 2 * length, value.shape[1]), jnp.float32)


def corner_kernel(place_ref, lead_ref, partner_ref, others_ref, out_ref, line_ref, rest_ref, *, blocks, owners):
    x = x_of(place_ref)
    length = owners * blocks
    cols_ref = others_ref.at[0:length]
    behind = [others_ref.at[(j + 1) * length : (j + 2) * length] for j in range(owners)]
    lead = butterfly(lead_ref[...], partner_ref[...], core_of(place_ref), 0)
    columns = [lead[0:blocks, :]] + [cols_ref[i * blocks : (i + 1) * blocks, :] for i in range(1, owners)]
    for i, column in enumerate(block_inverse(columns)):
        out_ref[i * blocks : (i + 1) * blocks, :] = column
    index = lax.broadcasted_iota(jnp.int32, line_ref.shape, 0)
    lane = lax.broadcasted_iota(jnp.int32, line_ref.shape, 1)
    fixed = []
    for j in range(owners):
        line = behind[j][...]
        corner = [lead[blocks + j : blocks + j + 1, :]] + [line[i * blocks : i * blocks + 1, :] for i in range(1, owners)]
        for i, value in enumerate(block_inverse(corner)):
            line = jnp.where((index == i * blocks) & (lane == 0), value[:, 0:1], line)
        fixed.append(line)
    for i in range(owners):
        line = fixed[0]
        for j in range(1, owners):
            line = jnp.where(lax.rem(x - i + owners, owners) == j, fixed[j], line)
        if i == 0:
            line_ref[...] = line
        else:
            rest_ref[i - 1] = line


def fill_sides(sides, messages, place_ref, blocks, spans):
    pair = sides.shape[1] // spans
    for index, message in enumerate(messages):
        behind, m = index // spans, index % spans
        rows = pl.ds(pl.multiple_of(source_span(place_ref, m, spans) * pair, pair), pair)
        for b in range(blocks):
            sides[behind * blocks + b, rows, :] = message[b * pair : (b + 1) * pair, :]


def add_products(order_ref, sizes_ref, which, first, tiles_ref, sides, acc, sems=None):
    def group(index, _):
        if sems is not None:
            for k in range(UNROLL):
                at = first + index * UNROLL + k
                pltpu.make_async_copy(tiles_ref.at[at], tiles_ref.at[at], sems.at[at]).wait()
        for k in range(UNROLL):
            entry = order_ref[which, index * UNROLL + k]
            side, row = (entry >> 8) & 255, entry & 255
            tile = tiles_ref[first + index * UNROLL + k]
            acc[row] += jnp.dot(sides[side], tile, preferred_element_type=jnp.float32)
        return 0

    lax.fori_loop(0, groups_of(sizes_ref, which), group, 0)


def groups_of(sizes_ref, which):
    return (sizes_ref[which] + UNROLL - 1) // UNROLL


def near_kernel(place_ref, order_ref, sizes_ref, tiles_ref, _, *refs, blocks, spans):
    *messages, acc_ref, held_ref, sides, sems = refs
    near_places = groups_of(sizes_ref, 0) * UNROLL
    far_places = groups_of(sizes_ref, 1) * UNROLL

    def fetch(which, index, at):
        slot = order_ref[which, index] >> 16
        return pltpu.make_async_copy(tiles_ref.at[slot], held_ref.at[at], sems.at[at])

    lax.fori_loop(0, near_places, lambda i, _: (fetch(0, i, i).start(), 0)[1], 0)
    lax.fori_loop(0, far_places, lambda i, _: (fetch(1, i, near_places + i).start(), 0)[1], 0)
    fill_sides(sides, messages, place_ref, blocks, spans)
    acc_ref[...] = jnp.zeros_like(acc_ref)
    add_products(order_ref, sizes_ref, 0, 0, held_ref, sides, acc_ref, sems)
    lax.fori_loop(0, far_places, lambda i, _: (fetch(1, i, near_places + i).wait(), 0)[1], 0)


def far_kernel(place_ref, order_ref, sizes_ref, tiles_ref, near_ref, others_ref, *refs, blocks, owners, spans):
    direct, swapped = refs[:spans], refs[spans : owners * spans]
    keep_ref, send_ref, sides, acc, firsts = refs[owners * spans :]
    extent = tiles_ref.shape[-1]
    pair = sides.shape[1] // spans
    height = pair // 2
    length = owners * blocks
    cols_ref, row_ref = others_ref.at[0:length], others_ref.at[length : 2 * length]
    x = x_of(place_ref)
    fill_sides(sides, swapped, place_ref, blocks, spans)
    messages = (*direct, *swapped)
    for index, message in enumerate(messages):
        owner = lax.rem(x - index // spans + owners, owners)
        side = jnp.transpose(message[blocks * pair :, :].astype(jnp.float32))
        column = side[0:pair, 0:1] + side[0:pair, 1:2] + side[0:pair, 2:3]
        rows = pl.ds(pl.multiple_of(source_span(place_ref, index % spans, spans) * pair, pair), pair)
        firsts[owner, rows, :] = jnp.broadcast_to(column, (pair, firsts.shape[2]))
    for i in range(blocks):
        total = near_ref[i]
        for owner in range(owners):
            total += firsts[owner][:, 0:1] * cols_ref[owner * blocks + i : owner * blocks + i + 1, :]
        acc[i] = total
    add_products(order_ref, sizes_ref, 1, groups_of(sizes_ref, 0) * UNROLL, tiles_ref, sides, acc)

    lane = lax.broadcasted_iota(jnp.int32, (pair, extent), 1)
    for m in range(spans):
        rows = pl.ds(pl.multiple_of(source_span(place_ref, m, spans) * pair, pair), pair)
        total = jnp.zeros((pair, extent), jnp.float32)
        top = jnp.zeros((pair, 1), jnp.float32)
        for behind in range(owners):
            owner = lax.rem(x - behind + owners, owners)
            message = messages[behind * spans + m]
            for b in range(blocks):
                line = row_ref[pl.ds(owner * blocks + b, 1), :]
                total += message[b * pair : (b + 1) * pair, :].astype(jnp.float32) * line
                if b == 0:
                    top += firsts[owner, rows, :][:, 0:1] * line[:, 0:1]
        top += jnp.sum(total, axis=1, keepdims=True)
        acc[0, rows, :] = jnp.where(lane == 0, top, acc[0, rows, :])
    first_core = core_of(place_ref) == 0
    for i in range(blocks):
        value = acc[i]
        for y in range(spans):
            one = value[y * pair : y * pair + height, :]
            two = value[y * pair + height : (y + 1) * pair, :]
            keep_ref[y, i] = jnp.where(first_core, one, two)
            send_ref[y, i] = jnp.where(first_core, two, one)


def combine_kernel(place_ref, keep_ref, arrived_ref, own_ref, *out_refs):
    spans = keep_ref.shape[0]
    span = span_of(place_ref)
    own_ref[...] = keep_ref[span] + arrived_ref[span]
    for j, out_ref in enumerate(out_refs, 1):
        at = lax.rem(span + j, spans)
        out_ref[...] = (keep_ref[at] + arrived_ref[at]).astype(jnp.bfloat16)


def back_kernel(own_ref, *refs):
    *arrived, out_ref = refs
    blocks, height, extent = own_ref.shape
    total = own_ref[...]
    for part in arrived:
        total = total + part[...].astype(jnp.float32)
    columns = block_inverse([total[b][:, 0:1] for b in range(blocks)])
    lane = lax.broadcasted_iota(jnp.int32, (height, extent), 1)
    fixed = jnp.concatenate([jnp.where(lane == 0, columns[b], total[b]) for b in range(blocks)], axis=0)
    signs, scale = haar_parts(extent, True)
    result = exact_dot(fixed * scale, signs)
    for b in range(blocks):
        out_ref[:, b * extent : (b + 1) * extent] = result[b * height : (b + 1) * height, :]


def local(sources, tiles, tile_row, tile_col, tile_count):
    n_row, n_col = lax.axis_size("row"), lax.axis_size("col")
    owners = n_row // n_col
    spans = n_col // 2
    extent = tiles.shape[-1]
    slots = tiles.shape[2]
    height = sources.shape[0]
    blocks = sources.shape[1] // extent
    pair = 2 * height
    row_index, col_index = lax.axis_index("row"), lax.axis_index("col")
    z, x = row_index // owners, row_index % owners
    span, core = col_index // 2, col_index % 2

    def moved(value, to):
        pairs = []
        for a in range(n_row):
            for b in range(n_col):
                zz, xx, yy, cc = to(a // owners, a % owners, b // 2, b % 2)
                pairs.append((a * n_col + b, (zz * owners + xx) * n_col + yy * 2 + cc))
        return lax.ppermute(value, ("row", "col"), pairs)

    def other_core(value):
        return moved(value, lambda zz, xx, yy, cc: (zz, xx, yy, 1 - cc))

    def along_x(value, j):
        return moved(value, lambda zz, xx, yy, cc: (zz, (xx + j) % owners, yy, cc))

    smem = pl.BlockSpec(memory_space=pltpu.SMEM)
    vmem = pl.BlockSpec(memory_space=pltpu.VMEM)
    hbm = pl.BlockSpec(memory_space=pltpu.HBM)
    unread = pl.BlockSpec(memory_space=pl.ANY)

    def call(kernel, name, out_shape, in_specs, out_specs, limit=16, scratch=(), aliases=None, **sizes):
        return pl.pallas_call(
            functools.partial(kernel, **sizes) if sizes else kernel,
            out_shape=out_shape,
            in_specs=in_specs,
            out_specs=out_specs,
            scratch_shapes=scratch,
            input_output_aliases=aliases or {},
            name=name,
            compiler_params=pltpu.CompilerParams(vmem_limit_bytes=int(limit * MIB)),
            cost_estimate=pl.CostEstimate(flops=0, bytes_accessed=MIB, transcendentals=0),
        )

    def in_hbm(value):
        return pltpu.with_memory_space_constraint(value, pltpu.HBM)

    def f32(*dims):
        return jax.ShapeDtypeStruct(dims, jnp.float32)

    def kept(*dims):
        return pltpu.VMEM(dims, jnp.float32)

    def bf16(*dims):
        return jax.ShapeDtypeStruct(dims, jnp.bfloat16)

    place = packed_place(core, span, x, z)

    def after(value, *others):
        return lax.optimization_barrier((value, *others))[0]

    def apart(body, *state):
        return lax.fori_loop(0, jnp.minimum(tile_count.reshape(()), 1), body, state)

    length = owners * blocks
    stack = in_hbm(tiles.reshape(slots, extent, extent))
    from_core = other_core(sources)
    order, sizes, blank_lead, blank = call(
        list_kernel,
        "lists",
        [
            pltpu.SMEM((4, slots + UNROLL), jnp.int32),
            pltpu.SMEM((4,), jnp.int32),
            kept(2 * blocks, extent),
            kept((owners + 1) * length, extent),
        ],
        [smem] * 4,
        [smem] * 2 + [vmem] * 2,
        blocks=blocks,
        owners=owners,
    )(place, in_hbm(tile_row.reshape(-1)), in_hbm(tile_col.reshape(-1)), tile_count.reshape(1))
    message = call(
        front_kernel,
        "front",
        bf16(blocks * pair + SIDE_ROWS, extent),
        [smem, hbm, vmem, unread],
        vmem,
        scratch=[pltpu.VMEM(sources.shape, jnp.float32), pltpu.SemaphoreType.DMA],
        blocks=blocks,
        extent=extent,
    )(place, in_hbm(sources), from_core, blank)

    direct = [
        moved(message, lambda zz, xx, yy, cc, m=m: (cc * spans + (yy + m) % spans, xx, zz // 2, zz % 2))
        for m in range(spans)
    ]

    def col_level(value, bit):
        if bit == 0:
            return other_core(value)
        step = 2 ** (bit - 1)
        return moved(value, lambda zz, xx, yy, cc: (zz, xx, yy ^ step, cc))

    def early(trip, _):
        cols, line = call(
            edge_kernel,
            "edges",
            [f32(length, extent)] * 2,
            [smem] * 3 + [hbm],
            [vmem] * 2,
            scratch=[
                pltpu.VMEM((slots, SIDE_ROWS, extent), jnp.bfloat16),
                pltpu.VMEM((slots, extent, LANES), jnp.bfloat16),
                pltpu.VMEM((extent, LANES), jnp.float32),
                pltpu.SemaphoreType.DMA((slots,)),
                pltpu.SemaphoreType.DMA((slots,)),
            ],
        )(trip.reshape(1), order, sizes, stack)
        behind = [line] + [along_x(line, j) for j in range(1, owners)]
        lead = call(pack_kernel, "pack", f32(2 * blocks, extent), [vmem] * (1 + owners), vmem, blocks=blocks)(cols, *behind)
        others = call(join_kernel, "join", kept(*blank.shape), [vmem] * (1 + owners), vmem)(cols, *behind)
        for bit in reversed(range(1, n_col.bit_length() - 1)):
            lead = call(col_level_kernel, "col_level", kept(2 * blocks, extent), [smem, vmem, vmem], vmem, bit=bit)(
                place, lead, col_level(lead, bit)
            )
        return lead, others

    lead, others = apart(early, blank_lead, blank)
    swapped = [along_x(after(piece, lead), j) for j in range(1, owners) for piece in direct]

    def late(_, state):
        lead, others = state
        first_cols, line, rest = call(
            corner_kernel,
            "corner",
            [f32(length, extent)] * 2 + [f32(owners - 1, length, extent)],
            [smem] + [vmem] * 3,
            [vmem] * 3,
            blocks=blocks,
            owners=owners,
        )(place, lead, col_level(lead, 0), others)
        for bit in reversed(range((n_row // owners).bit_length() - 1)):
            partner = moved(line, lambda zz, xx, yy, cc, bit=bit: (zz ^ 2**bit, xx, yy, cc))
            line = call(row_level_kernel, "row_level", f32(length, extent), [smem, vmem, vmem], vmem, bit=bit)(
                place, line, partner
            )
        others = call(x_levels_kernel, "x_levels", kept(*blank.shape), [smem, vmem, vmem, vmem], vmem)(
            place, first_cols, line, rest
        )
        return lead, others

    _, others = apart(late, after(lead, *direct), others)

    every = (spans * pair, extent)
    places = slots + 2 * UNROLL
    near, held = call(
        near_kernel,
        "near",
        [f32(blocks + 1, *every), pltpu.VMEM((places, extent, extent), jnp.bfloat16)],
        [smem] * 3 + [hbm, unread] + [vmem] * len(direct),
        [vmem] * 2,
        scratch=[pltpu.VMEM((blocks, *every), jnp.bfloat16), pltpu.SemaphoreType.DMA((places,))],
        blocks=blocks,
        spans=spans,
    )(place, order, sizes, stack, others, *direct)

    shape = (spans, blocks, height, extent)
    keep, send = call(
        far_kernel,
        "far",
        [f32(*shape)] * 2,
        [smem] * 3 + [vmem] * (3 + len(direct) + len(swapped)),
        [vmem] * 2,
        scratch=[
            pltpu.VMEM(((owners - 1) * blocks, *every), jnp.bfloat16),
            pltpu.VMEM((blocks + 1, *every), jnp.float32),
            pltpu.VMEM((owners, spans * pair, 128), jnp.float32),
        ],
        blocks=blocks,
        owners=owners,
        spans=spans,
    )(place, order, sizes, held, near, others, *direct, *swapped)

    own, *outgoing = call(
        combine_kernel,
        "combine",
        [f32(*shape[1:])] + [bf16(*shape[1:])] * (spans - 1),
        [smem, vmem, vmem],
        [vmem] * spans,
    )(place, keep, other_core(send))
    arrived = [
        moved(value, lambda zz, xx, yy, cc, j=j: (zz, xx, (yy + j) % spans, cc)) for j, value in enumerate(outgoing, 1)
    ]
    return call(back_kernel, "back", f32(*sources.shape), [vmem] * spans, vmem)(own, *arrived)


def solution(mesh):
    return jax.shard_map(
        local,
        mesh=mesh,
        in_specs=(
            P("col", "row"),
            P("row", "col", None, None, None),
            P("row", "col", None),
            P("row", "col", None),
            P("row", "col"),
        ),
        out_specs=P("col", "row"),
        check_vma=False,
    )
```

```python
import functools
import math

import jax
import jax.numpy as jnp
from jax import lax
from jax.experimental import pallas as pl
from jax.experimental.pallas import tpu as pltpu
from jax.sharding import PartitionSpec as P

ROOT_HALF = 1.0 / math.sqrt(2.0)
SIDE_ROWS = 16
UNROLL = 4
LANES = 128
MIB = 2**20


def haar_parts(extent, transposed):
    k = lax.broadcasted_iota(jnp.int32, (extent, extent), 1 if transposed else 0)
    n = lax.broadcasted_iota(jnp.int32, (extent, extent), 0 if transposed else 1)
    stride = jnp.where(n == 0, extent, n & -n)
    signs = jnp.where((k ^ n) < 2 * stride, jnp.where((k & stride) == 0, 1.0, -1.0), 0.0)
    n = lax.broadcasted_iota(jnp.int32, (1, extent), 1)
    scale = jnp.full((1, extent), 1.0 / math.sqrt(extent), jnp.float32)
    level = 1
    while level < extent:
        scale = jnp.where((n & -n) == level, 1.0 / math.sqrt(2 * level), scale)
        level *= 2
    return signs.astype(jnp.bfloat16), scale


def three_terms(value):
    high = value.astype(jnp.bfloat16)
    rest = value - high.astype(jnp.float32)
    middle = rest.astype(jnp.bfloat16)
    low = (rest - middle.astype(jnp.float32)).astype(jnp.bfloat16)
    return high, middle, low


def exact_dot(value, signs):
    return sum(jnp.dot(term, signs, preferred_element_type=jnp.float32) for term in three_terms(value))


def block_forward(columns):
    columns = list(columns)
    stride = 1
    while stride < len(columns):
        for p in range(0, len(columns), 2 * stride):
            u, v = columns[p], columns[p + stride]
            columns[p], columns[p + stride] = (u + v) * ROOT_HALF, (u - v) * ROOT_HALF
        stride *= 2
    return columns


def block_inverse(columns):
    columns = list(columns)
    stride = len(columns) // 2
    while stride >= 1:
        for p in range(0, len(columns), 2 * stride):
            u, v = columns[p], columns[p + stride]
            columns[p], columns[p + stride] = (u + v) * ROOT_HALF, (u - v) * ROOT_HALF
        stride //= 2
    return columns


def packed_place(core, span, x, z):
    return (core + 2 * span + 256 * x + 65536 * z).astype(jnp.int32).reshape(1)


def core_of(place_ref):
    return place_ref[0] & 1


def span_of(place_ref):
    return (place_ref[0] >> 1) & 127


def x_of(place_ref):
    return (place_ref[0] >> 8) & 255


def z_of(place_ref):
    return place_ref[0] >> 16


def source_span(place_ref, m, spans):
    return (z_of(place_ref) & (spans - 1)) ^ m


def front_kernel(place_ref, sources_ref, other_ref, _, out_ref, first_ref, mine_ref, sem, *, blocks, extent):
    copy = pltpu.make_async_copy(sources_ref, mine_ref, sem)
    copy.start()
    height = mine_ref.shape[0]
    pair = 2 * height
    signs, scale = haar_parts(extent, False)
    copy.wait()
    mine, other = mine_ref[...], other_ref[...]
    first_core = core_of(place_ref) == 0
    both = jnp.concatenate([jnp.where(first_core, mine, other), jnp.where(first_core, other, mine)], axis=0)
    parts = [both[:, b * extent : (b + 1) * extent] for b in range(blocks)]
    coef = exact_dot(jnp.concatenate(parts, axis=0), signs) * scale
    columns = block_forward([coef[b * pair : (b + 1) * pair, 0:1] for b in range(blocks)])
    lane = lax.broadcasted_iota(jnp.int32, (pair, extent), 1)
    for b in range(blocks):
        column = jnp.zeros_like(columns[0]) if b == 0 else columns[b]
        block = jnp.where(lane == 0, column, coef[b * pair : (b + 1) * pair, :])
        out_ref[b * pair : (b + 1) * pair, :] = block.astype(jnp.bfloat16)
    total = functools.reduce(jnp.add, parts)
    ones = jnp.ones((SIDE_ROWS, extent), jnp.bfloat16)
    first = sum(
        lax.dot_general(ones, term, (((1,), (1,)), ((), ())), preferred_element_type=jnp.float32)
        for term in three_terms(total)
    )
    first_ref[...] = jnp.zeros_like(first_ref)
    first_ref[:, 0:pair] = first[0:8, :] * (1.0 / math.sqrt(blocks * extent))


def list_kernel(
    place_ref, rows_ref, cols_ref, count_ref, order_ref, sizes_ref, walk_ref, rest_ref, *, blocks, owners
):
    walk_ref[...] = jnp.zeros_like(walk_ref)
    rest_ref[...] = jnp.zeros_like(rest_ref)
    x = x_of(place_ref)

    def visit(slot, sizes):
        row, col = rows_ref[slot], cols_ref[slot]
        owner, block = col // blocks, lax.rem(col, blocks)
        behind = lax.rem(x - owner + owners, owners)
        near = behind == 0
        side = jnp.where(near, block, (behind - 1) * blocks + block)
        entry = (slot << 16) + (side << 8) + row
        plain = (slot << 16) + (col << 8) + row
        near_size, far_size, row_size, col_size = sizes
        order_ref[jnp.where(near, 0, 1), jnp.where(near, near_size, far_size)] = entry
        order_ref[2, row_size] = plain
        order_ref[3, col_size] = plain
        one = near.astype(jnp.int32)
        return (
            near_size + one,
            far_size + 1 - one,
            row_size + (row == 0).astype(jnp.int32),
            col_size + (block == 0).astype(jnp.int32),
        )

    sizes = lax.fori_loop(0, count_ref[0], visit, (jnp.int32(0),) * 4)
    for which in range(4):
        sizes_ref[which] = sizes[which]
    for which in range(2):
        for k in range(UNROLL - 1):
            order_ref[which, sizes[which] + k] = blocks


def edge_kernel(
    place_ref,
    _,
    order_ref,
    sizes_ref,
    tiles_ref,
    first_ref,
    cols_ref,
    line_ref,
    strips,
    columns,
    summed,
    strip_sems,
    column_sems,
    *,
    owners,
):
    def strip_copy(index):
        slot = order_ref[3, index] >> 16
        return pltpu.make_async_copy(tiles_ref.at[slot, 0:SIDE_ROWS, :], strips.at[index], strip_sems.at[index])

    def column_copy(index):
        slot = order_ref[2, index] >> 16
        return pltpu.make_async_copy(tiles_ref.at[slot, :, 0:LANES], columns.at[index], column_sems.at[index])

    lax.fori_loop(0, sizes_ref[2], lambda i, _: (column_copy(i).start(), 0)[1], 0)
    lax.fori_loop(0, sizes_ref[3], lambda i, _: (strip_copy(i).start(), 0)[1], 0)
    cols_ref[...] = jnp.zeros_like(cols_ref)
    summed[...] = jnp.zeros_like(summed)
    lane = lax.broadcasted_iota(jnp.int32, summed.shape, 1)

    def add_strip(index, _):
        entry = order_ref[3, index]
        strip_copy(index).wait()
        at = pl.ds(((entry >> 8) & 255) + (entry & 255), 1)
        cols_ref[at, :] += strips[index].astype(jnp.float32)[0:1, :]
        return 0

    def add_column(index, _):
        column_copy(index).wait()
        column = columns[index].astype(jnp.float32)[:, 0:1]
        summed[...] += jnp.where(lane == ((order_ref[2, index] >> 8) & 255), column, 0.0)
        return 0

    lax.fori_loop(0, sizes_ref[3], add_strip, 0)
    lax.fori_loop(0, sizes_ref[2], add_column, 0)
    length = cols_ref.shape[0]
    line_ref[0:length, :] = jnp.transpose(summed[...])[0:length, :]
    index = lax.broadcasted_iota(jnp.int32, (line_ref.shape[0] - length, line_ref.shape[1]), 0)
    own = z_of(place_ref) * owners + x_of(place_ref)
    line_ref[length:, :] = jnp.where(index == own, first_ref[0:1, :], 0.0)


def butterfly(value, partner, index, bit):
    active = lax.rem(index, 2**bit) == 0
    upper = ((index >> bit) & 1) == 1
    return jnp.where(active, jnp.where(upper, partner - value, partner + value) * ROOT_HALF, value)


def arrange_kernel(place_ref, cols_ref, *refs):
    *behind, walk_ref, rest_ref = refs
    owners = len(behind)
    length = cols_ref.shape[0]
    x = x_of(place_ref)
    rest_ref[0:length, :] = cols_ref[...]
    gathered = behind[0][length:, :]
    for j in range(1, owners):
        gathered = gathered + behind[j][length:, :]
    walk_ref[length:, :] = gathered
    for i in range(owners):
        value = behind[0][0:length, :]
        for j in range(1, owners):
            value = jnp.where(lax.rem(x - i + owners, owners) == j, behind[j][0:length, :], value)
        if i == 0:
            walk_ref[0:length, :] = value
        else:
            rest_ref[i * length : (i + 1) * length, :] = value


def z_level_kernel(place_ref, walk_ref, partner_ref, out_ref, *, bit, length):
    walk, partner = walk_ref[...], partner_ref[...]
    row = lax.broadcasted_iota(jnp.int32, walk.shape, 0)
    out_ref[...] = jnp.where(row < length, butterfly(walk, partner, z_of(place_ref), bit), walk + partner)


def coarse_kernel(place_ref, walk_ref, rest_ref, row_ref, cols_ref, firsts_ref, *, blocks, rows):
    x = x_of(place_ref)
    length = row_ref.shape[0]
    owners = length // blocks
    by_x = [walk_ref[0:length, :]] + [rest_ref[i * length : (i + 1) * length, :] for i in range(1, owners)]
    by_x = block_inverse(by_x)
    value = by_x[0]
    for i in range(1, owners):
        value = jnp.where(x == i, by_x[i], value)
    row_ref[...] = value
    cols = rest_ref[0:length, :]
    index = lax.broadcasted_iota(jnp.int32, cols.shape, 0)
    lane = lax.broadcasted_iota(jnp.int32, cols.shape, 1)
    cols_ref[...] = jnp.where((lax.rem(index, blocks) == 0) & (lane == 0), value, cols)
    firsts_ref[...] = jnp.zeros_like(firsts_ref)
    for i, first in enumerate(block_forward([walk_ref[length + i : length + i + 1, :] for i in range(rows)])):
        firsts_ref[i : i + 1, :] = first


def fill_sides(sides, messages, place_ref, blocks, spans):
    pair = sides.shape[1] // spans
    for index, message in enumerate(messages):
        behind, m = index // spans, index % spans
        rows = pl.ds(pl.multiple_of(source_span(place_ref, m, spans) * pair, pair), pair)
        for b in range(blocks):
            sides[behind * blocks + b, rows, :] = message[b * pair : (b + 1) * pair, :]


def add_products(order_ref, sizes_ref, which, first, tiles_ref, sides, acc, sems=None):
    def group(index, _):
        if sems is not None:
            for k in range(UNROLL):
                at = first + index * UNROLL + k
                pltpu.make_async_copy(tiles_ref.at[at], tiles_ref.at[at], sems.at[at]).wait()
        for k in range(UNROLL):
            entry = order_ref[which, index * UNROLL + k]
            side, row = (entry >> 8) & 255, entry & 255
            tile = tiles_ref[first + index * UNROLL + k]
            acc[row] += jnp.dot(sides[side], tile, preferred_element_type=jnp.float32)
        return 0

    lax.fori_loop(0, groups_of(sizes_ref, which), group, 0)


def groups_of(sizes_ref, which):
    return (sizes_ref[which] + UNROLL - 1) // UNROLL


def near_kernel(place_ref, order_ref, sizes_ref, tiles_ref, _, *refs, blocks, spans):
    *messages, acc_ref, held_ref, sides, sems = refs
    near_places = groups_of(sizes_ref, 0) * UNROLL
    far_places = groups_of(sizes_ref, 1) * UNROLL

    def fetch(which, index, at):
        slot = order_ref[which, index] >> 16
        return pltpu.make_async_copy(tiles_ref.at[slot], held_ref.at[at], sems.at[at])

    lax.fori_loop(0, near_places, lambda i, _: (fetch(0, i, i).start(), 0)[1], 0)
    lax.fori_loop(0, far_places, lambda i, _: (fetch(1, i, near_places + i).start(), 0)[1], 0)
    fill_sides(sides, messages, place_ref, blocks, spans)
    acc_ref[...] = jnp.zeros_like(acc_ref)
    add_products(order_ref, sizes_ref, 0, 0, held_ref, sides, acc_ref, sems)
    lax.fori_loop(0, far_places, lambda i, _: (fetch(1, i, near_places + i).wait(), 0)[1], 0)


def far_kernel(
    place_ref, order_ref, sizes_ref, tiles_ref, near_ref, row_ref, cols_ref, *refs, blocks, owners, spans
):
    messages = refs[: owners * spans]
    keep_ref, send_ref, sides, acc = refs[owners * spans :]
    extent = tiles_ref.shape[-1]
    pair = sides.shape[1] // spans
    height = pair // 2
    x = x_of(place_ref)
    fill_sides(sides, messages[spans:], place_ref, blocks, spans)
    acc[...] = near_ref[...]
    add_products(order_ref, sizes_ref, 1, groups_of(sizes_ref, 0) * UNROLL, tiles_ref, sides, acc)

    lane = lax.broadcasted_iota(jnp.int32, (pair, extent), 1)
    for m in range(spans):
        rows = pl.ds(pl.multiple_of(source_span(place_ref, m, spans) * pair, pair), pair)
        total = jnp.zeros((pair, extent), jnp.float32)
        for behind in range(owners):
            owner = lax.rem(x - behind + owners, owners)
            message = messages[behind * spans + m]
            for b in range(blocks):
                line = row_ref[pl.ds(owner * blocks + b, 1), :]
                total += message[b * pair : (b + 1) * pair, :].astype(jnp.float32) * line
        top = jnp.sum(total, axis=1, keepdims=True)
        acc[0, rows, :] = jnp.where(lane == 0, top, acc[0, rows, :])
    first_core = core_of(place_ref) == 0
    for i in range(blocks):
        value = acc[i]
        for y in range(spans):
            one = value[y * pair : y * pair + height, :]
            two = value[y * pair + height : (y + 1) * pair, :]
            at = (y * blocks + i) * height
            keep_ref[at : at + height, :] = jnp.where(first_core, one, two)
            send_ref[at : at + height, :] = jnp.where(first_core, two, one)
    send_ref[spans * blocks * height :, :] = cols_ref[...]


def combine_kernel(place_ref, keep_ref, arrived_ref, cols_ref, own_ref, both_ref, *out_refs):
    spans = len(out_refs) + 1
    span = span_of(place_ref)
    rows = own_ref.shape[0]
    length = cols_ref.shape[0]
    first_core = core_of(place_ref) == 0
    mine, other = cols_ref[...], arrived_ref[spans * rows :, :]
    both_ref[0:length, :] = jnp.where(first_core, mine, other)
    both_ref[length:, :] = jnp.where(first_core, other, mine)
    at = pl.ds(pl.multiple_of(span * rows, rows), rows)
    own_ref[...] = keep_ref[at, :] + arrived_ref[at, :]
    high, low, _ = three_terms(both_ref[...])
    for j, out_ref in enumerate(out_refs, 1):
        at = pl.ds(pl.multiple_of(lax.rem(span + j, spans) * rows, rows), rows)
        out_ref[0:rows, :] = (keep_ref[at, :] + arrived_ref[at, :]).astype(jnp.bfloat16)
        out_ref[rows : rows + 2 * length, :] = high
        out_ref[rows + 2 * length :, :] = low


def back_kernel(place_ref, own_ref, both_ref, firsts_ref, *refs, blocks, owners):
    *arrived, out_ref = refs
    spans = len(arrived) + 1
    extent = own_ref.shape[1]
    rows = own_ref.shape[0]
    height = rows // blocks
    length = owners * blocks
    span = span_of(place_ref)
    total = own_ref[...]
    for part in arrived:
        total = total + part[0:rows, :].astype(jnp.float32)
    tables, picked = [both_ref[...]], []
    for part in arrived:
        high, low = part[rows : rows + 2 * length, :], part[rows + 2 * length :, :]
        tables.append(high.astype(jnp.float32) + low.astype(jnp.float32))
    for j in range(spans):
        source = lax.rem(span - j + spans, spans)
        for k in range(2 * owners):
            picked.append(firsts_ref[pl.ds(source * 2 * owners + k, 1), :])
    picked += [jnp.zeros_like(picked[0])] * (-len(picked) % 16)
    columns = jnp.transpose(jnp.concatenate(picked, axis=0))
    columns = jnp.where(core_of(place_ref) == 0, columns[0:height, :], columns[height : 2 * height, :])
    blocks_of = []
    for b in range(blocks):
        value = total[b * height : (b + 1) * height, :]
        for j, table in enumerate(tables):
            for k in range(2 * owners):
                at = k * blocks + b
                index = j * 2 * owners + k
                value = value + columns[:, index : index + 1] * table[at : at + 1, :]
        blocks_of.append(value)
    columns = block_inverse([value[:, 0:1] for value in blocks_of])
    lane = lax.broadcasted_iota(jnp.int32, (height, extent), 1)
    fixed = jnp.concatenate([jnp.where(lane == 0, columns[b], blocks_of[b]) for b in range(blocks)], axis=0)
    signs, scale = haar_parts(extent, True)
    result = exact_dot(fixed * scale, signs)
    for b in range(blocks):
        out_ref[:, b * extent : (b + 1) * extent] = result[b * height : (b + 1) * height, :]


def local(sources, tiles, tile_row, tile_col, tile_count):
    n_row, n_col = lax.axis_size("row"), lax.axis_size("col")
    owners = n_row // n_col
    spans = n_col // 2
    extent = tiles.shape[-1]
    slots = tiles.shape[2]
    height = sources.shape[0]
    blocks = sources.shape[1] // extent
    pair = 2 * height
    row_index, col_index = lax.axis_index("row"), lax.axis_index("col")
    z, x = row_index // owners, row_index % owners
    span, core = col_index // 2, col_index % 2

    def moved(value, to):
        pairs = []
        for a in range(n_row):
            for b in range(n_col):
                zz, xx, yy, cc = to(a // owners, a % owners, b // 2, b % 2)
                pairs.append((a * n_col + b, (zz * owners + xx) * n_col + yy * 2 + cc))
        return lax.ppermute(value, ("row", "col"), pairs)

    def other_core(value):
        return moved(value, lambda zz, xx, yy, cc: (zz, xx, yy, 1 - cc))

    def along_x(value, j):
        return moved(value, lambda zz, xx, yy, cc: (zz, (xx + j) % owners, yy, cc))

    smem = pl.BlockSpec(memory_space=pltpu.SMEM)
    vmem = pl.BlockSpec(memory_space=pltpu.VMEM)
    hbm = pl.BlockSpec(memory_space=pltpu.HBM)
    unread = pl.BlockSpec(memory_space=pl.ANY)

    def call(kernel, name, out_shape, in_specs, out_specs, limit=16, scratch=(), aliases=None, **sizes):
        return pl.pallas_call(
            functools.partial(kernel, **sizes) if sizes else kernel,
            out_shape=out_shape,
            in_specs=in_specs,
            out_specs=out_specs,
            scratch_shapes=scratch,
            input_output_aliases=aliases or {},
            name=name,
            compiler_params=pltpu.CompilerParams(vmem_limit_bytes=int(limit * MIB)),
            cost_estimate=pl.CostEstimate(flops=0, bytes_accessed=MIB, transcendentals=0),
        )

    def in_hbm(value):
        return pltpu.with_memory_space_constraint(value, pltpu.HBM)

    def f32(*dims):
        return jax.ShapeDtypeStruct(dims, jnp.float32)

    def kept(*dims):
        return pltpu.VMEM(dims, jnp.float32)

    def bf16(*dims):
        return jax.ShapeDtypeStruct(dims, jnp.bfloat16)

    place = packed_place(core, span, x, z)

    def after(value, *others):
        return lax.optimization_barrier((value, *others))[0]

    def apart(body, *state):
        return lax.fori_loop(0, jnp.minimum(tile_count.reshape(()), 1), body, state if len(state) > 1 else state[0])

    length = owners * blocks
    stack = in_hbm(tiles.reshape(slots, extent, extent))
    from_core = other_core(sources)
    gathered = -(-n_row // 8) * 8
    order, sizes, blank_walk, blank_rest = call(
        list_kernel,
        "lists",
        [
            pltpu.SMEM((4, slots + UNROLL), jnp.int32),
            pltpu.SMEM((4,), jnp.int32),
            kept(length + gathered, extent),
            kept(owners * length, extent),
        ],
        [smem] * 4,
        [smem] * 2 + [vmem] * 2,
        blocks=blocks,
        owners=owners,
    )(place, in_hbm(tile_row.reshape(-1)), in_hbm(tile_col.reshape(-1)), tile_count.reshape(1))
    message, first = call(
        front_kernel,
        "front",
        [bf16(blocks * pair, extent), f32(8, extent)],
        [smem, hbm, vmem, unread],
        [vmem] * 2,
        scratch=[pltpu.VMEM(sources.shape, jnp.float32), pltpu.SemaphoreType.DMA],
        blocks=blocks,
        extent=extent,
    )(place, in_hbm(sources), from_core, blank_rest)

    def spread(message, m):
        return moved(message, lambda zz, xx, yy, cc: (cc * spans + (yy ^ m), xx, zz // 2, zz % 2))

    direct = [spread(message, m) for m in range(spans)]

    def early(trip, _):
        cols, line = call(
            edge_kernel,
            "edges",
            [f32(length, extent), f32(length + gathered, extent)],
            [smem] * 4 + [hbm, vmem],
            [vmem] * 2,
            scratch=[
                pltpu.VMEM((slots, SIDE_ROWS, extent), jnp.bfloat16),
                pltpu.VMEM((slots, extent, LANES), jnp.bfloat16),
                pltpu.VMEM((extent, LANES), jnp.float32),
                pltpu.SemaphoreType.DMA((slots,)),
                pltpu.SemaphoreType.DMA((slots,)),
            ],
            owners=owners,
        )(place, trip.reshape(1), order, sizes, stack, first)
        behind = [along_x(line, j) for j in range(1, owners)]
        return call(
            arrange_kernel,
            "arrange",
            [kept(*blank_walk.shape), kept(*blank_rest.shape)],
            [smem] + [vmem] * (1 + owners),
            [vmem] * 2,
        )(place, cols, line, *behind)

    def z_levels(walk, bits):
        for bit in bits:
            partner = moved(walk, lambda zz, xx, yy, cc, bit=bit: (zz ^ 2**bit, xx, yy, cc))
            walk = call(
                z_level_kernel, "z_level", kept(*walk.shape), [smem, vmem, vmem], vmem, bit=bit, length=length
            )(place, walk, partner)
        return walk

    walk, rest = apart(early, blank_walk, blank_rest)
    swapped = [along_x(after(piece, walk), j) for j in range(1, owners) for piece in direct]
    z_bits = list(reversed(range((n_row // owners).bit_length() - 1)))
    walk = apart(lambda _, walk: z_levels(walk, z_bits), after(walk, *direct))

    first_row, first_cols, firsts = call(
        coarse_kernel,
        "coarse",
        [f32(length, extent), f32(length, extent), f32(gathered, extent)],
        [smem, vmem, vmem],
        [vmem] * 3,
        blocks=blocks,
        rows=n_row,
    )(place, walk, rest)

    every = (spans * pair, extent)
    places = slots + 2 * UNROLL
    near, held = call(
        near_kernel,
        "near",
        [f32(blocks + 1, *every), pltpu.VMEM((places, extent, extent), jnp.bfloat16)],
        [smem] * 3 + [hbm, unread] + [vmem] * len(direct),
        [vmem] * 2,
        scratch=[pltpu.VMEM((blocks, *every), jnp.bfloat16), pltpu.SemaphoreType.DMA((places,))],
        blocks=blocks,
        spans=spans,
    )(place, order, sizes, stack, first_row, *direct)

    part = blocks * height
    keep, send = call(
        far_kernel,
        "far",
        [f32(spans * part, extent), f32(spans * part + length, extent)],
        [smem] * 3 + [vmem] * (4 + len(direct) + len(swapped)),
        [vmem] * 2,
        scratch=[
            pltpu.VMEM(((owners - 1) * blocks, *every), jnp.bfloat16),
            pltpu.VMEM((blocks + 1, *every), jnp.float32),
        ],
        blocks=blocks,
        owners=owners,
        spans=spans,
    )(place, order, sizes, held, near, first_row, first_cols, *direct, *swapped)

    own, both, *outgoing = call(
        combine_kernel,
        "combine",
        [f32(part, extent), f32(2 * length, extent)] + [bf16(part + 4 * length, extent)] * (spans - 1),
        [smem, vmem, vmem, vmem],
        [vmem] * (spans + 1),
    )(place, keep, other_core(send), first_cols)
    arrived = [
        moved(value, lambda zz, xx, yy, cc, j=j: (zz, xx, (yy + j) % spans, cc)) for j, value in enumerate(outgoing, 1)
    ]
    return call(
        back_kernel,
        "back",
        f32(*sources.shape),
        [smem] + [vmem] * (2 + spans),
        vmem,
        blocks=blocks,
        owners=owners,
    )(place, own, both, firsts, *arrived)


def solution(mesh):
    return jax.shard_map(
        local,
        mesh=mesh,
        in_specs=(
            P("col", "row"),
            P("row", "col", None, None, None),
            P("row", "col", None),
            P("row", "col", None),
            P("row", "col"),
        ),
        out_specs=P("col", "row"),
        check_vma=False,
    )
```

```python
import functools
import math

import jax
import jax.numpy as jnp
from jax import lax
from jax.experimental import pallas as pl
from jax.experimental.pallas import tpu as pltpu
from jax.sharding import PartitionSpec as P

ROOT_HALF = 1.0 / math.sqrt(2.0)
SIDE_ROWS = 16
UNROLL = 4
AHEAD = 16
LANES = 128
MIB = 2**20


def haar_parts(extent, transposed):
    k = lax.broadcasted_iota(jnp.int32, (extent, extent), 1 if transposed else 0)
    n = lax.broadcasted_iota(jnp.int32, (extent, extent), 0 if transposed else 1)
    stride = jnp.where(n == 0, extent, n & -n)
    signs = jnp.where((k ^ n) < 2 * stride, jnp.where((k & stride) == 0, 1.0, -1.0), 0.0)
    n = lax.broadcasted_iota(jnp.int32, (1, extent), 1)
    scale = jnp.full((1, extent), 1.0 / math.sqrt(extent), jnp.float32)
    level = 1
    while level < extent:
        scale = jnp.where((n & -n) == level, 1.0 / math.sqrt(2 * level), scale)
        level *= 2
    return signs.astype(jnp.bfloat16), scale


def three_terms(value):
    high = value.astype(jnp.bfloat16)
    rest = value - high.astype(jnp.float32)
    middle = rest.astype(jnp.bfloat16)
    low = (rest - middle.astype(jnp.float32)).astype(jnp.bfloat16)
    return high, middle, low


def exact_dot(value, signs, terms=3):
    return sum(jnp.dot(term, signs, preferred_element_type=jnp.float32) for term in three_terms(value)[:terms])


def block_forward(columns):
    columns = list(columns)
    stride = 1
    while stride < len(columns):
        for p in range(0, len(columns), 2 * stride):
            u, v = columns[p], columns[p + stride]
            columns[p], columns[p + stride] = (u + v) * ROOT_HALF, (u - v) * ROOT_HALF
        stride *= 2
    return columns


def block_inverse(columns):
    columns = list(columns)
    stride = len(columns) // 2
    while stride >= 1:
        for p in range(0, len(columns), 2 * stride):
            u, v = columns[p], columns[p + stride]
            columns[p], columns[p + stride] = (u + v) * ROOT_HALF, (u - v) * ROOT_HALF
        stride //= 2
    return columns


def packed_place(core, span, x, z):
    return (core + 2 * span + 256 * x + 65536 * z).astype(jnp.int32).reshape(1)


def core_of(place_ref):
    return place_ref[0] & 1


def span_of(place_ref):
    return (place_ref[0] >> 1) & 127


def x_of(place_ref):
    return (place_ref[0] >> 8) & 255


def z_of(place_ref):
    return place_ref[0] >> 16


def source_span(place_ref, m, spans):
    return (z_of(place_ref) ^ m ^ (spans - 1)) & (spans - 1)


def front_kernel(place_ref, sources_ref, other_ref, _, out_ref, first_ref, mine_ref, sem, *, blocks, extent):
    copy = pltpu.make_async_copy(sources_ref, mine_ref, sem)
    copy.start()
    height = mine_ref.shape[0]
    pair = 2 * height
    signs, scale = haar_parts(extent, False)
    copy.wait()
    mine, other = mine_ref[...], other_ref[...]
    first_core = core_of(place_ref) == 0
    both = jnp.concatenate([jnp.where(first_core, mine, other), jnp.where(first_core, other, mine)], axis=0)
    parts = [both[:, b * extent : (b + 1) * extent] for b in range(blocks)]
    coef = exact_dot(jnp.concatenate(parts, axis=0), signs) * scale
    columns = block_forward([coef[b * pair : (b + 1) * pair, 0:1] for b in range(blocks)])
    lane = lax.broadcasted_iota(jnp.int32, (pair, extent), 1)
    for b in range(blocks):
        column = jnp.zeros_like(columns[0]) if b == 0 else columns[b]
        block = jnp.where(lane == 0, column, coef[b * pair : (b + 1) * pair, :])
        out_ref[b * pair : (b + 1) * pair, :] = block.astype(jnp.bfloat16)
    total = functools.reduce(jnp.add, parts)
    ones = jnp.ones((SIDE_ROWS, extent), jnp.bfloat16)
    first = sum(
        lax.dot_general(ones, term, (((1,), (1,)), ((), ())), preferred_element_type=jnp.float32)
        for term in three_terms(total)
    )
    first_ref[...] = jnp.zeros_like(first_ref)
    first_ref[:, 0:pair] = first[0:8, :] * (1.0 / math.sqrt(blocks * extent))


def list_kernel(
    place_ref, rows_ref, cols_ref, count_ref, order_ref, sizes_ref, walk_ref, rest_ref, *, blocks, owners
):
    walk_ref[...] = jnp.zeros_like(walk_ref)
    rest_ref[...] = jnp.zeros_like(rest_ref)
    x = x_of(place_ref)

    def visit(slot, sizes):
        row, col = rows_ref[slot], cols_ref[slot]
        owner, block = col // blocks, lax.rem(col, blocks)
        behind = lax.rem(x - owner + owners, owners)
        near = behind == 0
        side = jnp.where(near, block, (behind - 1) * blocks + block)
        entry = (slot << 16) + (side << 8) + row
        plain = (slot << 16) + (col << 8) + row
        near_size, far_size, row_size, col_size = sizes
        order_ref[jnp.where(near, 0, 1), jnp.where(near, near_size, far_size)] = entry
        order_ref[2, row_size] = plain
        order_ref[3, col_size] = plain
        one = near.astype(jnp.int32)
        return (
            near_size + one,
            far_size + 1 - one,
            row_size + (row == 0).astype(jnp.int32),
            col_size + (block == 0).astype(jnp.int32),
        )

    sizes = lax.fori_loop(0, count_ref[0], visit, (jnp.int32(0),) * 4)
    for which in range(4):
        sizes_ref[which] = sizes[which]
    for which in range(2):
        for k in range(UNROLL - 1):
            order_ref[which, sizes[which] + k] = blocks


def edge_kernel(
    place_ref,
    _,
    order_ref,
    sizes_ref,
    tiles_ref,
    first_ref,
    cols_ref,
    line_ref,
    strips,
    columns,
    summed,
    strip_sems,
    column_sems,
    *,
    owners,
):
    def strip_copy(index):
        slot = order_ref[3, index] >> 16
        return pltpu.make_async_copy(tiles_ref.at[slot, 0:SIDE_ROWS, :], strips.at[index], strip_sems.at[index])

    def column_copy(index):
        slot = order_ref[2, index] >> 16
        return pltpu.make_async_copy(tiles_ref.at[slot, :, 0:LANES], columns.at[index], column_sems.at[index])

    lax.fori_loop(0, sizes_ref[2], lambda i, _: (column_copy(i).start(), 0)[1], 0)
    lax.fori_loop(0, sizes_ref[3], lambda i, _: (strip_copy(i).start(), 0)[1], 0)
    cols_ref[...] = jnp.zeros_like(cols_ref)
    summed[...] = jnp.zeros_like(summed)
    lane = lax.broadcasted_iota(jnp.int32, summed.shape, 1)

    def add_strip(index, _):
        entry = order_ref[3, index]
        strip_copy(index).wait()
        at = pl.ds(((entry >> 8) & 255) + (entry & 255), 1)
        cols_ref[at, :] += strips[index].astype(jnp.float32)[0:1, :]
        return 0

    def add_column(index, _):
        column_copy(index).wait()
        column = columns[index].astype(jnp.float32)[:, 0:1]
        summed[...] += jnp.where(lane == ((order_ref[2, index] >> 8) & 255), column, 0.0)
        return 0

    lax.fori_loop(0, sizes_ref[3], add_strip, 0)
    lax.fori_loop(0, sizes_ref[2], add_column, 0)
    length = cols_ref.shape[0]
    line_ref[0:length, :] = jnp.transpose(summed[...])[0:length, :]
    index = lax.broadcasted_iota(jnp.int32, (line_ref.shape[0] - length, line_ref.shape[1]), 0)
    own = z_of(place_ref) * owners + x_of(place_ref)
    line_ref[length:, :] = jnp.where(index == own, first_ref[0:1, :], 0.0)


def butterfly(value, partner, index, bit):
    active = lax.rem(index, 2**bit) == 0
    upper = ((index >> bit) & 1) == 1
    return jnp.where(active, jnp.where(upper, partner - value, partner + value) * ROOT_HALF, value)


def arrange_kernel(place_ref, cols_ref, *refs):
    *behind, walk_ref, rest_ref = refs
    owners = len(behind)
    length = cols_ref.shape[0]
    x = x_of(place_ref)
    rest_ref[0:length, :] = cols_ref[...]
    gathered = behind[0][length:, :]
    for j in range(1, owners):
        gathered = gathered + behind[j][length:, :]
    walk_ref[length:, :] = gathered
    for i in range(owners):
        value = behind[0][0:length, :]
        for j in range(1, owners):
            value = jnp.where(lax.rem(x - i + owners, owners) == j, behind[j][0:length, :], value)
        if i == 0:
            walk_ref[0:length, :] = value
        else:
            rest_ref[i * length : (i + 1) * length, :] = value


def z_level_kernel(place_ref, walk_ref, partner_ref, _, out_ref, *, bit, length):
    walk, partner = walk_ref[...], partner_ref[...]
    row = lax.broadcasted_iota(jnp.int32, walk.shape, 0)
    out_ref[...] = jnp.where(row < length, butterfly(walk, partner, z_of(place_ref), bit), walk + partner)


def coarse_kernel(place_ref, walk_ref, rest_ref, row_ref, cols_ref, firsts_ref, *, blocks, rows):
    x = x_of(place_ref)
    length = row_ref.shape[0]
    owners = length // blocks
    by_x = [walk_ref[0:length, :]] + [rest_ref[i * length : (i + 1) * length, :] for i in range(1, owners)]
    by_x = block_inverse(by_x)
    value = by_x[0]
    for i in range(1, owners):
        value = jnp.where(x == i, by_x[i], value)
    row_ref[...] = value
    cols = rest_ref[0:length, :]
    index = lax.broadcasted_iota(jnp.int32, cols.shape, 0)
    lane = lax.broadcasted_iota(jnp.int32, cols.shape, 1)
    cols_ref[...] = jnp.where((lax.rem(index, blocks) == 0) & (lane == 0), value, cols)
    firsts_ref[...] = jnp.zeros_like(firsts_ref)
    for i, first in enumerate(block_forward([walk_ref[length + i : length + i + 1, :] for i in range(rows)])):
        firsts_ref[i : i + 1, :] = first


def fill_sides(sides, messages, place_ref, blocks, spans):
    pair = sides.shape[1] // spans
    for index, message in enumerate(messages):
        behind, m = index // spans, index % spans
        rows = pl.ds(pl.multiple_of(source_span(place_ref, m, spans) * pair, pair), pair)
        for b in range(blocks):
            sides[behind * blocks + b, rows, :] = message[b * pair : (b + 1) * pair, :]


def groups_of(sizes_ref, which):
    return (sizes_ref[which] + UNROLL - 1) // UNROLL


def tile_copy(order_ref, which, index, tiles_ref, held, sems, at):
    slot = order_ref[which, index] >> 16
    return pltpu.make_async_copy(tiles_ref.at[slot], held.at[at], sems.at[at])


def add_group(order_ref, which, index, held, sides, acc):
    for k in range(UNROLL):
        entry = order_ref[which, index * UNROLL + k]
        side, row = (entry >> 8) & 255, entry & 255
        acc[row] += jnp.dot(sides[side], held[index * UNROLL + k], preferred_element_type=jnp.float32)


def blank_kernel(_, sum_ref, ahead_ref):
    sum_ref[0] = jnp.zeros(sum_ref.shape[1:], jnp.float32)
    ahead_ref[0] = jnp.zeros(ahead_ref.shape[1:], jnp.bfloat16)


def near_kernel(place_ref, _, order_ref, sizes_ref, tiles_ref, *refs, blocks, spans):
    *messages, acc_ref, ahead_ref, sides, held, sems, ahead_sems = refs
    groups = groups_of(sizes_ref, 0)
    ahead = jnp.minimum(groups_of(sizes_ref, 1) * UNROLL, AHEAD)

    def own(i):
        return tile_copy(order_ref, 0, i, tiles_ref, held, sems, i)

    def other(i):
        return tile_copy(order_ref, 1, i, tiles_ref, ahead_ref, ahead_sems, i)

    lax.fori_loop(0, groups * UNROLL, lambda i, _: (own(i).start(), 0)[1], 0)
    lax.fori_loop(0, ahead, lambda i, _: (other(i).start(), 0)[1], 0)
    fill_sides(sides, messages, place_ref, blocks, spans)
    acc_ref[...] = jnp.zeros_like(acc_ref)

    def group(index, _):
        for k in range(UNROLL):
            own(index * UNROLL + k).wait()
        add_group(order_ref, 0, index, held, sides, acc_ref)
        return 0

    lax.fori_loop(0, groups, group, 0)
    lax.fori_loop(0, ahead, lambda i, _: (other(i).wait(), 0)[1], 0)


def far_kernel(
    place_ref, order_ref, sizes_ref, tiles_ref, near_ref, ahead_ref, row_ref, cols_ref, *refs, blocks, owners, spans
):
    messages = refs[: owners * spans]
    keep_ref, send_ref, sides, acc, held, sems = refs[owners * spans :]
    groups = groups_of(sizes_ref, 1)
    ahead = jnp.minimum(groups, AHEAD // UNROLL)

    def fetch(i):
        return tile_copy(order_ref, 1, i, tiles_ref, held, sems, i)

    lax.fori_loop(ahead * UNROLL, groups * UNROLL, lambda i, _: (fetch(i).start(), 0)[1], 0)
    extent = tiles_ref.shape[-1]
    pair = sides.shape[1] // spans
    height = pair // 2
    x = x_of(place_ref)
    fill_sides(sides, messages[spans:], place_ref, blocks, spans)
    acc[...] = near_ref[...]

    def ready(index, _):
        add_group(order_ref, 1, index, ahead_ref, sides, acc)
        return 0

    def group(index, _):
        for k in range(UNROLL):
            fetch(index * UNROLL + k).wait()
        add_group(order_ref, 1, index, held, sides, acc)
        return 0

    lax.fori_loop(0, ahead, ready, 0)
    lax.fori_loop(ahead, groups, group, 0)

    lane = lax.broadcasted_iota(jnp.int32, (pair, extent), 1)
    for m in range(spans):
        rows = pl.ds(pl.multiple_of(source_span(place_ref, m, spans) * pair, pair), pair)
        total = jnp.zeros((pair, extent), jnp.float32)
        for behind in range(owners):
            owner = lax.rem(x - behind + owners, owners)
            message = messages[behind * spans + m]
            for b in range(blocks):
                line = row_ref[pl.ds(owner * blocks + b, 1), :]
                total += message[b * pair : (b + 1) * pair, :].astype(jnp.float32) * line
        top = jnp.sum(total, axis=1, keepdims=True)
        acc[0, rows, :] = jnp.where(lane == 0, top, acc[0, rows, :])
    first_core = core_of(place_ref) == 0
    for i in range(blocks):
        value = acc[i]
        for y in range(spans):
            one = value[y * pair : y * pair + height, :]
            two = value[y * pair + height : (y + 1) * pair, :]
            at = (y * blocks + i) * height
            keep_ref[at : at + height, :] = jnp.where(first_core, one, two)
            send_ref[at : at + height, :] = jnp.where(first_core, two, one)
    send_ref[spans * blocks * height :, :] = cols_ref[...]


def combine_kernel(place_ref, keep_ref, arrived_ref, cols_ref, own_ref, both_ref, *out_refs):
    spans = len(out_refs) + 1
    span = span_of(place_ref)
    rows = own_ref.shape[0]
    length = cols_ref.shape[0]
    first_core = core_of(place_ref) == 0
    mine, other = cols_ref[...], arrived_ref[spans * rows :, :]
    both_ref[0:length, :] = jnp.where(first_core, mine, other)
    both_ref[length:, :] = jnp.where(first_core, other, mine)
    at = pl.ds(pl.multiple_of(span * rows, rows), rows)
    own_ref[...] = keep_ref[at, :] + arrived_ref[at, :]
    both = both_ref[...].astype(jnp.bfloat16)
    for j, out_ref in enumerate(out_refs, 1):
        at = pl.ds(pl.multiple_of(lax.rem(span + j, spans) * rows, rows), rows)
        out_ref[0:rows, :] = (keep_ref[at, :] + arrived_ref[at, :]).astype(jnp.bfloat16)
        out_ref[rows:, :] = both


def back_kernel(place_ref, own_ref, both_ref, firsts_ref, *refs, blocks, owners):
    *arrived, out_ref = refs
    spans = len(arrived) + 1
    extent = own_ref.shape[1]
    rows = own_ref.shape[0]
    height = rows // blocks
    span = span_of(place_ref)
    total = own_ref[...]
    for part in arrived:
        total = total + part[0:rows, :].astype(jnp.float32)
    tables, picked = [both_ref[...]], []
    for part in arrived:
        tables.append(part[rows:, :].astype(jnp.float32))
    for j in range(spans):
        source = lax.rem(span - j + spans, spans)
        for k in range(2 * owners):
            picked.append(firsts_ref[pl.ds(source * 2 * owners + k, 1), :])
    picked += [jnp.zeros_like(picked[0])] * (-len(picked) % 16)
    columns = jnp.transpose(jnp.concatenate(picked, axis=0))
    columns = jnp.where(core_of(place_ref) == 0, columns[0:height, :], columns[height : 2 * height, :])
    blocks_of = []
    for b in range(blocks):
        value = total[b * height : (b + 1) * height, :]
        for j, table in enumerate(tables):
            for k in range(2 * owners):
                at = k * blocks + b
                index = j * 2 * owners + k
                value = value + columns[:, index : index + 1] * table[at : at + 1, :]
        blocks_of.append(value)
    columns = block_inverse([value[:, 0:1] for value in blocks_of])
    lane = lax.broadcasted_iota(jnp.int32, (height, extent), 1)
    fixed = jnp.concatenate([jnp.where(lane == 0, columns[b], blocks_of[b]) for b in range(blocks)], axis=0)
    signs, scale = haar_parts(extent, True)
    result = exact_dot(fixed * scale, signs, 2)
    for b in range(blocks):
        out_ref[:, b * extent : (b + 1) * extent] = result[b * height : (b + 1) * height, :]


def local(sources, tiles, tile_row, tile_col, tile_count):
    n_row, n_col = lax.axis_size("row"), lax.axis_size("col")
    owners = n_row // n_col
    spans = n_col // 2
    extent = tiles.shape[-1]
    slots = tiles.shape[2]
    height = sources.shape[0]
    blocks = sources.shape[1] // extent
    pair = 2 * height
    row_index, col_index = lax.axis_index("row"), lax.axis_index("col")
    z, x = row_index // owners, row_index % owners
    span, core = col_index // 2, col_index % 2

    def moved(value, to):
        pairs = []
        for a in range(n_row):
            for b in range(n_col):
                zz, xx, yy, cc = to(a // owners, a % owners, b // 2, b % 2)
                pairs.append((a * n_col + b, (zz * owners + xx) * n_col + yy * 2 + cc))
        return lax.ppermute(value, ("row", "col"), pairs)

    def other_core(value):
        return moved(value, lambda zz, xx, yy, cc: (zz, xx, yy, 1 - cc))

    def along_x(value, j):
        return moved(value, lambda zz, xx, yy, cc: (zz, (xx + j) % owners, yy, cc))

    smem = pl.BlockSpec(memory_space=pltpu.SMEM)
    vmem = pl.BlockSpec(memory_space=pltpu.VMEM)
    hbm = pl.BlockSpec(memory_space=pltpu.HBM)
    unread = pl.BlockSpec(memory_space=pl.ANY)

    def call(kernel, name, out_shape, in_specs, out_specs, limit=16, scratch=(), aliases=None, **sizes):
        return pl.pallas_call(
            functools.partial(kernel, **sizes) if sizes else kernel,
            out_shape=out_shape,
            in_specs=in_specs,
            out_specs=out_specs,
            scratch_shapes=scratch,
            input_output_aliases=aliases or {},
            name=name,
            compiler_params=pltpu.CompilerParams(vmem_limit_bytes=int(limit * MIB)),
            cost_estimate=pl.CostEstimate(flops=0, bytes_accessed=MIB, transcendentals=0),
        )

    def in_hbm(value):
        return pltpu.with_memory_space_constraint(value, pltpu.HBM)

    def f32(*dims):
        return jax.ShapeDtypeStruct(dims, jnp.float32)

    def kept(*dims):
        return pltpu.VMEM(dims, jnp.float32)

    def bf16(*dims):
        return jax.ShapeDtypeStruct(dims, jnp.bfloat16)

    place = packed_place(core, span, x, z)

    def after(value, *others):
        return lax.optimization_barrier((value, *others))[0]

    def apart(body, *state):
        return lax.fori_loop(0, jnp.minimum(tile_count.reshape(()), 1), body, state if len(state) > 1 else state[0])

    length = owners * blocks
    stack = in_hbm(tiles.reshape(slots, extent, extent))
    from_core = other_core(sources)
    gathered = -(-n_row // 8) * 8
    every = (spans * pair, extent)
    order, sizes, blank_walk, blank_rest = call(
        list_kernel,
        "lists",
        [
            pltpu.SMEM((4, slots + UNROLL), jnp.int32),
            pltpu.SMEM((4,), jnp.int32),
            kept(length + gathered, extent),
            kept(owners * length, extent),
        ],
        [smem] * 4,
        [smem] * 2 + [vmem] * 2,
        blocks=blocks,
        owners=owners,
    )(place, in_hbm(tile_row.reshape(-1)), in_hbm(tile_col.reshape(-1)), tile_count.reshape(1))
    message, first = call(
        front_kernel,
        "front",
        [bf16(blocks * pair, extent), f32(8, extent)],
        [smem, hbm, vmem, unread],
        [vmem] * 2,
        scratch=[pltpu.VMEM(sources.shape, jnp.float32), pltpu.SemaphoreType.DMA],
        blocks=blocks,
        extent=extent,
    )(place, in_hbm(sources), from_core, blank_rest)

    direct = [
        moved(message, lambda zz, xx, yy, cc, m=m: (cc * spans + (yy ^ m ^ (spans - 1)), xx, zz // 2, zz % 2))
        for m in range(spans)
    ]

    def early(trip, _):
        cols, line = call(
            edge_kernel,
            "edges",
            [f32(length, extent), f32(length + gathered, extent)],
            [smem] * 4 + [hbm, vmem],
            [vmem] * 2,
            scratch=[
                pltpu.VMEM((slots, SIDE_ROWS, extent), jnp.bfloat16),
                pltpu.VMEM((slots, extent, LANES), jnp.bfloat16),
                pltpu.VMEM((extent, LANES), jnp.float32),
                pltpu.SemaphoreType.DMA((slots,)),
                pltpu.SemaphoreType.DMA((slots,)),
            ],
            owners=owners,
        )(place, trip.reshape(1), order, sizes, stack, first)
        behind = [along_x(line, j) for j in range(1, owners)]
        return call(
            arrange_kernel,
            "arrange",
            [kept(*blank_walk.shape), kept(*blank_rest.shape)],
            [smem] + [vmem] * (1 + owners),
            [vmem] * 2,
        )(place, cols, line, *behind)

    walk, rest = apart(early, blank_walk, blank_rest)
    swapped = [along_x(after(piece, walk), j) for j in range(1, owners) for piece in direct]

    held_tiles = [
        pltpu.VMEM((slots + UNROLL, extent, extent), jnp.bfloat16),
        pltpu.SemaphoreType.DMA((slots + UNROLL,)),
    ]

    sum_shape, ahead_shape = (blocks + 1, *every), (AHEAD, extent, extent)
    later = [kept(*sum_shape), pltpu.VMEM(ahead_shape, jnp.bfloat16)]
    blank_sum, blank_ahead = call(blank_kernel, "blank", later, [unread], [vmem] * 2)(walk)

    def late(trip, state):
        walk, *_ = state
        near, ahead = call(
            near_kernel,
            "near",
            later,
            [smem] * 4 + [hbm] + [vmem] * len(direct),
            [vmem] * 2,
            scratch=[pltpu.VMEM((blocks, *every), jnp.bfloat16), *held_tiles, pltpu.SemaphoreType.DMA((AHEAD,))],
            blocks=blocks,
            spans=spans,
        )(place, trip.reshape(1), order, sizes, stack, *direct)
        for bit in reversed(range((n_row // owners).bit_length() - 1)):
            partner = moved(walk, lambda zz, xx, yy, cc, bit=bit: (zz ^ 2**bit, xx, yy, cc))
            walk = call(
                z_level_kernel, "z_level", kept(*walk.shape), [smem, vmem, vmem, unread], vmem, bit=bit, length=length
            )(place, walk, partner, near)
        return walk, near, ahead

    walk, near, ahead = apart(late, after(walk, *direct), blank_sum, blank_ahead)
    first_row, first_cols, firsts = call(
        coarse_kernel,
        "coarse",
        [f32(length, extent), f32(length, extent), f32(gathered, extent)],
        [smem, vmem, vmem],
        [vmem] * 3,
        blocks=blocks,
        rows=n_row,
    )(place, walk, rest)

    part = blocks * height
    keep, send = call(
        far_kernel,
        "far",
        [f32(spans * part, extent), f32(spans * part + length, extent)],
        [smem] * 3 + [hbm] + [vmem] * (4 + len(direct) + len(swapped)),
        [vmem] * 2,
        scratch=[
            pltpu.VMEM(((owners - 1) * blocks, *every), jnp.bfloat16),
            pltpu.VMEM((blocks + 1, *every), jnp.float32),
            *held_tiles,
        ],
        blocks=blocks,
        owners=owners,
        spans=spans,
    )(place, order, sizes, stack, near, ahead, first_row, first_cols, *direct, *swapped)

    own, both, *outgoing = call(
        combine_kernel,
        "combine",
        [f32(part, extent), f32(2 * length, extent)] + [bf16(part + 2 * length, extent)] * (spans - 1),
        [smem, vmem, vmem, vmem],
        [vmem] * (spans + 1),
    )(place, keep, other_core(send), first_cols)
    arrived = [
        moved(value, lambda zz, xx, yy, cc, j=j: (zz, xx, (yy + j) % spans, cc)) for j, value in enumerate(outgoing, 1)
    ]
    return call(
        back_kernel,
        "back",
        f32(*sources.shape),
        [smem] + [vmem] * (2 + spans),
        vmem,
        blocks=blocks,
        owners=owners,
    )(place, own, both, firsts, *arrived)


def solution(mesh):
    return jax.shard_map(
        local,
        mesh=mesh,
        in_specs=(
            P("col", "row"),
            P("row", "col", None, None, None),
            P("row", "col", None),
            P("row", "col", None),
            P("row", "col"),
        ),
        out_specs=P("col", "row"),
        check_vma=False,
    )
```

```python
import functools
import math

import jax
import jax.numpy as jnp
from jax import lax
from jax.experimental import pallas as pl
from jax.experimental.pallas import tpu as pltpu
from jax.sharding import PartitionSpec as P

ROOT_HALF = 1.0 / math.sqrt(2.0)
SIDE_ROWS = 16
UNROLL = 4
AHEAD = 16
LANES = 128
MIB = 2**20


def haar_parts(extent, transposed):
    k = lax.broadcasted_iota(jnp.int32, (extent, extent), 1 if transposed else 0)
    n = lax.broadcasted_iota(jnp.int32, (extent, extent), 0 if transposed else 1)
    stride = jnp.where(n == 0, extent, n & -n)
    signs = jnp.where((k ^ n) < 2 * stride, jnp.where((k & stride) == 0, 1.0, -1.0), 0.0)
    n = lax.broadcasted_iota(jnp.int32, (1, extent), 1)
    scale = jnp.full((1, extent), 1.0 / math.sqrt(extent), jnp.float32)
    level = 1
    while level < extent:
        scale = jnp.where((n & -n) == level, 1.0 / math.sqrt(2 * level), scale)
        level *= 2
    return signs.astype(jnp.bfloat16), scale


def three_terms(value):
    high = value.astype(jnp.bfloat16)
    rest = value - high.astype(jnp.float32)
    middle = rest.astype(jnp.bfloat16)
    low = (rest - middle.astype(jnp.float32)).astype(jnp.bfloat16)
    return high, middle, low


def exact_dot(value, signs, terms=3):
    return sum(jnp.dot(term, signs, preferred_element_type=jnp.float32) for term in three_terms(value)[:terms])


def block_forward(columns):
    columns = list(columns)
    stride = 1
    while stride < len(columns):
        for p in range(0, len(columns), 2 * stride):
            u, v = columns[p], columns[p + stride]
            columns[p], columns[p + stride] = (u + v) * ROOT_HALF, (u - v) * ROOT_HALF
        stride *= 2
    return columns


def block_inverse(columns):
    columns = list(columns)
    stride = len(columns) // 2
    while stride >= 1:
        for p in range(0, len(columns), 2 * stride):
            u, v = columns[p], columns[p + stride]
            columns[p], columns[p + stride] = (u + v) * ROOT_HALF, (u - v) * ROOT_HALF
        stride //= 2
    return columns


def packed_place(core, span, x, z):
    return (core + 2 * span + 256 * x + 65536 * z).astype(jnp.int32).reshape(1)


def core_of(place_ref):
    return place_ref[0] & 1


def span_of(place_ref):
    return (place_ref[0] >> 1) & 127


def x_of(place_ref):
    return (place_ref[0] >> 8) & 255


def z_of(place_ref):
    return place_ref[0] >> 16


def source_span(place_ref, m, spans):
    return (z_of(place_ref) ^ m ^ (spans - 1)) & (spans - 1)


def prepare_kernel(sources_ref, mine_ref, walk_ref, rest_ref, sem):
    copy = pltpu.make_async_copy(sources_ref, mine_ref, sem)
    copy.start()
    walk_ref[...] = jnp.zeros_like(walk_ref)
    rest_ref[...] = jnp.zeros_like(rest_ref)
    copy.wait()


def front_kernel(place_ref, mine_ref, other_ref, out_ref, first_ref, *, blocks, extent):
    height = mine_ref.shape[0]
    pair = 2 * height
    signs, scale = haar_parts(extent, False)
    mine, other = mine_ref[...], other_ref[...]
    first_core = core_of(place_ref) == 0
    both = jnp.concatenate([jnp.where(first_core, mine, other), jnp.where(first_core, other, mine)], axis=0)
    parts = [both[:, b * extent : (b + 1) * extent] for b in range(blocks)]
    coef = exact_dot(jnp.concatenate(parts, axis=0), signs) * scale
    columns = block_forward([coef[b * pair : (b + 1) * pair, 0:1] for b in range(blocks)])
    lane = lax.broadcasted_iota(jnp.int32, (pair, extent), 1)
    for b in range(blocks):
        column = jnp.zeros_like(columns[0]) if b == 0 else columns[b]
        block = jnp.where(lane == 0, column, coef[b * pair : (b + 1) * pair, :])
        out_ref[b * pair : (b + 1) * pair, :] = block.astype(jnp.bfloat16)
    total = functools.reduce(jnp.add, parts)
    ones = jnp.ones((SIDE_ROWS, extent), jnp.bfloat16)
    first = sum(
        lax.dot_general(ones, term, (((1,), (1,)), ((), ())), preferred_element_type=jnp.float32)
        for term in three_terms(total)
    )
    first_ref[...] = jnp.zeros_like(first_ref)
    first_ref[:, 0:pair] = first[0:8, :] * (1.0 / math.sqrt(blocks * extent))


def list_kernel(place_ref, rows_ref, cols_ref, count_ref, order_ref, sizes_ref, *, blocks, owners):
    x = x_of(place_ref)

    def visit(slot, sizes):
        row, col = rows_ref[slot], cols_ref[slot]
        owner, block = col // blocks, lax.rem(col, blocks)
        behind = lax.rem(x - owner + owners, owners)
        near = behind == 0
        side = jnp.where(near, block, (behind - 1) * blocks + block)
        entry = (slot << 16) + (side << 8) + row
        plain = (slot << 16) + (col << 8) + row
        near_size, far_size, row_size, col_size = sizes
        order_ref[jnp.where(near, 0, 1), jnp.where(near, near_size, far_size)] = entry
        order_ref[2, row_size] = plain
        order_ref[3, col_size] = plain
        one = near.astype(jnp.int32)
        return (
            near_size + one,
            far_size + 1 - one,
            row_size + (row == 0).astype(jnp.int32),
            col_size + (block == 0).astype(jnp.int32),
        )

    sizes = lax.fori_loop(0, count_ref[0], visit, (jnp.int32(0),) * 4)
    for which in range(4):
        sizes_ref[which] = sizes[which]
    for which in range(2):
        for k in range(UNROLL - 1):
            order_ref[which, sizes[which] + k] = blocks


def edge_kernel(
    place_ref,
    _,
    order_ref,
    sizes_ref,
    tiles_ref,
    first_ref,
    cols_ref,
    line_ref,
    strips,
    columns,
    summed,
    strip_sems,
    column_sems,
    *,
    owners,
):
    def strip_copy(index):
        slot = order_ref[3, index] >> 16
        return pltpu.make_async_copy(tiles_ref.at[slot, 0:SIDE_ROWS, :], strips.at[index], strip_sems.at[index])

    def column_copy(index):
        slot = order_ref[2, index] >> 16
        return pltpu.make_async_copy(tiles_ref.at[slot, :, 0:LANES], columns.at[index], column_sems.at[index])

    lax.fori_loop(0, sizes_ref[2], lambda i, _: (column_copy(i).start(), 0)[1], 0)
    lax.fori_loop(0, sizes_ref[3], lambda i, _: (strip_copy(i).start(), 0)[1], 0)
    cols_ref[...] = jnp.zeros_like(cols_ref)
    summed[...] = jnp.zeros_like(summed)
    lane = lax.broadcasted_iota(jnp.int32, summed.shape, 1)

    def add_strip(index, _):
        entry = order_ref[3, index]
        strip_copy(index).wait()
        at = pl.ds(((entry >> 8) & 255) + (entry & 255), 1)
        cols_ref[at, :] += strips[index].astype(jnp.float32)[0:1, :]
        return 0

    def add_column(index, _):
        column_copy(index).wait()
        column = columns[index].astype(jnp.float32)[:, 0:1]
        summed[...] += jnp.where(lane == ((order_ref[2, index] >> 8) & 255), column, 0.0)
        return 0

    lax.fori_loop(0, sizes_ref[3], add_strip, 0)
    lax.fori_loop(0, sizes_ref[2], add_column, 0)
    length = cols_ref.shape[0]
    line_ref[0:length, :] = jnp.transpose(summed[...])[0:length, :]
    index = lax.broadcasted_iota(jnp.int32, (line_ref.shape[0] - length, line_ref.shape[1]), 0)
    own = z_of(place_ref) * owners + x_of(place_ref)
    line_ref[length:, :] = jnp.where(index == own, first_ref[0:1, :], 0.0)


def butterfly(value, partner, index, bit):
    active = lax.rem(index, 2**bit) == 0
    upper = ((index >> bit) & 1) == 1
    return jnp.where(active, jnp.where(upper, partner - value, partner + value) * ROOT_HALF, value)


def arrange_kernel(place_ref, cols_ref, *refs):
    *behind, walk_ref, rest_ref = refs
    owners = len(behind)
    length = cols_ref.shape[0]
    x = x_of(place_ref)
    rest_ref[0:length, :] = cols_ref[...]
    gathered = behind[0][length:, :]
    for j in range(1, owners):
        gathered = gathered + behind[j][length:, :]
    walk_ref[length:, :] = gathered
    for i in range(owners):
        value = behind[0][0:length, :]
        for j in range(1, owners):
            value = jnp.where(lax.rem(x - i + owners, owners) == j, behind[j][0:length, :], value)
        if i == 0:
            walk_ref[0:length, :] = value
        else:
            rest_ref[i * length : (i + 1) * length, :] = value


def z_level_kernel(place_ref, walk_ref, partner_ref, _, out_ref, *, bit, length):
    walk, partner = walk_ref[...], partner_ref[...]
    row = lax.broadcasted_iota(jnp.int32, walk.shape, 0)
    out_ref[...] = jnp.where(row < length, butterfly(walk, partner, z_of(place_ref), bit), walk + partner)


def coarse_kernel(place_ref, walk_ref, rest_ref, row_ref, cols_ref, firsts_ref, *, blocks, rows):
    x = x_of(place_ref)
    length = row_ref.shape[0]
    owners = length // blocks
    by_x = [walk_ref[0:length, :]] + [rest_ref[i * length : (i + 1) * length, :] for i in range(1, owners)]
    by_x = block_inverse(by_x)
    value = by_x[0]
    for i in range(1, owners):
        value = jnp.where(x == i, by_x[i], value)
    row_ref[...] = value
    cols = rest_ref[0:length, :]
    index = lax.broadcasted_iota(jnp.int32, cols.shape, 0)
    lane = lax.broadcasted_iota(jnp.int32, cols.shape, 1)
    cols_ref[...] = jnp.where((lax.rem(index, blocks) == 0) & (lane == 0), value, cols)
    firsts_ref[...] = jnp.zeros_like(firsts_ref)
    for i, first in enumerate(block_forward([walk_ref[length + i : length + i + 1, :] for i in range(rows)])):
        firsts_ref[i : i + 1, :] = first


def fill_sides(sides, messages, place_ref, blocks, spans):
    pair = sides.shape[1] // spans
    for index, message in enumerate(messages):
        behind, m = index // spans, index % spans
        rows = pl.ds(pl.multiple_of(source_span(place_ref, m, spans) * pair, pair), pair)
        for b in range(blocks):
            sides[behind * blocks + b, rows, :] = message[b * pair : (b + 1) * pair, :]


def groups_of(sizes_ref, which):
    return (sizes_ref[which] + UNROLL - 1) // UNROLL


def tile_copy(order_ref, which, index, tiles_ref, held, sems, at):
    slot = order_ref[which, index] >> 16
    return pltpu.make_async_copy(tiles_ref.at[slot], held.at[at], sems.at[at])


def add_group(order_ref, which, index, held, sides, acc):
    for k in range(UNROLL):
        entry = order_ref[which, index * UNROLL + k]
        side, row = (entry >> 8) & 255, entry & 255
        acc[row] += jnp.dot(sides[side], held[index * UNROLL + k], preferred_element_type=jnp.float32)


def blank_kernel(_, sum_ref, ahead_ref):
    sum_ref[0] = jnp.zeros(sum_ref.shape[1:], jnp.float32)
    ahead_ref[0] = jnp.zeros(ahead_ref.shape[1:], jnp.bfloat16)


def near_kernel(place_ref, _, order_ref, sizes_ref, tiles_ref, *refs, blocks, spans):
    *messages, acc_ref, ahead_ref, sides, held, sems, ahead_sems = refs
    groups = groups_of(sizes_ref, 0)
    ahead = jnp.minimum(groups_of(sizes_ref, 1) * UNROLL, AHEAD)

    def own(i):
        return tile_copy(order_ref, 0, i, tiles_ref, held, sems, i)

    def other(i):
        return tile_copy(order_ref, 1, i, tiles_ref, ahead_ref, ahead_sems, i)

    lax.fori_loop(0, groups * UNROLL, lambda i, _: (own(i).start(), 0)[1], 0)
    lax.fori_loop(0, ahead, lambda i, _: (other(i).start(), 0)[1], 0)
    fill_sides(sides, messages, place_ref, blocks, spans)
    acc_ref[...] = jnp.zeros_like(acc_ref)

    def group(index, _):
        for k in range(UNROLL):
            own(index * UNROLL + k).wait()
        add_group(order_ref, 0, index, held, sides, acc_ref)
        return 0

    lax.fori_loop(0, groups, group, 0)
    lax.fori_loop(0, ahead, lambda i, _: (other(i).wait(), 0)[1], 0)


def far_kernel(
    place_ref, order_ref, sizes_ref, tiles_ref, near_ref, ahead_ref, row_ref, cols_ref, *refs, blocks, owners, spans
):
    messages = refs[: owners * spans]
    keep_ref, send_ref, sides, acc, held, sems, near_sides, near_sems = refs[owners * spans :]
    copies = [
        pltpu.make_async_copy(messages[m], near_sides.at[m], near_sems.at[m]) for m in range(spans)
    ]
    for copy in copies:
        copy.start()
    groups = groups_of(sizes_ref, 1)
    ahead = jnp.minimum(groups, AHEAD // UNROLL)

    def fetch(i):
        return tile_copy(order_ref, 1, i, tiles_ref, held, sems, i)

    lax.fori_loop(ahead * UNROLL, groups * UNROLL, lambda i, _: (fetch(i).start(), 0)[1], 0)
    extent = tiles_ref.shape[-1]
    pair = sides.shape[1] // spans
    height = pair // 2
    x = x_of(place_ref)
    fill_sides(sides, messages[spans:], place_ref, blocks, spans)
    acc[...] = near_ref[...]

    def ready(index, _):
        add_group(order_ref, 1, index, ahead_ref, sides, acc)
        return 0

    def group(index, _):
        for k in range(UNROLL):
            fetch(index * UNROLL + k).wait()
        add_group(order_ref, 1, index, held, sides, acc)
        return 0

    lax.fori_loop(0, ahead, ready, 0)
    lax.fori_loop(ahead, groups, group, 0)

    for copy in copies:
        copy.wait()
    messages = (*(near_sides.at[m] for m in range(spans)), *messages[spans:])
    lane = lax.broadcasted_iota(jnp.int32, (pair, extent), 1)
    for m in range(spans):
        rows = pl.ds(pl.multiple_of(source_span(place_ref, m, spans) * pair, pair), pair)
        total = jnp.zeros((pair, extent), jnp.float32)
        for behind in range(owners):
            owner = lax.rem(x - behind + owners, owners)
            message = messages[behind * spans + m]
            for b in range(blocks):
                line = row_ref[pl.ds(owner * blocks + b, 1), :]
                total += message[b * pair : (b + 1) * pair, :].astype(jnp.float32) * line
        top = jnp.sum(total, axis=1, keepdims=True)
        acc[0, rows, :] = jnp.where(lane == 0, top, acc[0, rows, :])
    first_core = core_of(place_ref) == 0
    for i in range(blocks):
        value = acc[i]
        for y in range(spans):
            one = value[y * pair : y * pair + height, :]
            two = value[y * pair + height : (y + 1) * pair, :]
            at = (y * blocks + i) * height
            keep_ref[at : at + height, :] = jnp.where(first_core, one, two)
            send_ref[at : at + height, :] = jnp.where(first_core, two, one)
    send_ref[spans * blocks * height :, :] = cols_ref[...]


def combine_kernel(place_ref, keep_ref, arrived_ref, cols_ref, own_ref, both_ref, *out_refs):
    spans = len(out_refs) + 1
    span = span_of(place_ref)
    rows = own_ref.shape[0]
    length = cols_ref.shape[0]
    first_core = core_of(place_ref) == 0
    mine, other = cols_ref[...], arrived_ref[spans * rows :, :]
    both_ref[0:length, :] = jnp.where(first_core, mine, other)
    both_ref[length:, :] = jnp.where(first_core, other, mine)
    at = pl.ds(pl.multiple_of(span * rows, rows), rows)
    own_ref[...] = keep_ref[at, :] + arrived_ref[at, :]
    both = both_ref[...].astype(jnp.bfloat16)
    for j, out_ref in enumerate(out_refs, 1):
        at = pl.ds(pl.multiple_of(lax.rem(span + j, spans) * rows, rows), rows)
        out_ref[0:rows, :] = (keep_ref[at, :] + arrived_ref[at, :]).astype(jnp.bfloat16)
        out_ref[rows:, :] = both


def back_kernel(place_ref, own_ref, both_ref, firsts_ref, *refs, blocks, owners):
    *arrived, out_ref = refs
    spans = len(arrived) + 1
    extent = own_ref.shape[1]
    rows = own_ref.shape[0]
    height = rows // blocks
    span = span_of(place_ref)
    total = own_ref[...]
    for part in arrived:
        total = total + part[0:rows, :].astype(jnp.float32)
    tables, picked = [both_ref[...]], []
    for part in arrived:
        tables.append(part[rows:, :].astype(jnp.float32))
    for j in range(spans):
        source = lax.rem(span - j + spans, spans)
        for k in range(2 * owners):
            picked.append(firsts_ref[pl.ds(source * 2 * owners + k, 1), :])
    picked += [jnp.zeros_like(picked[0])] * (-len(picked) % 16)
    columns = jnp.transpose(jnp.concatenate(picked, axis=0))
    columns = jnp.where(core_of(place_ref) == 0, columns[0:height, :], columns[height : 2 * height, :])
    blocks_of = []
    for b in range(blocks):
        value = total[b * height : (b + 1) * height, :]
        for j, table in enumerate(tables):
            for k in range(2 * owners):
                at = k * blocks + b
                index = j * 2 * owners + k
                value = value + columns[:, index : index + 1] * table[at : at + 1, :]
        blocks_of.append(value)
    columns = block_inverse([value[:, 0:1] for value in blocks_of])
    lane = lax.broadcasted_iota(jnp.int32, (height, extent), 1)
    fixed = jnp.concatenate([jnp.where(lane == 0, columns[b], blocks_of[b]) for b in range(blocks)], axis=0)
    signs, scale = haar_parts(extent, True)
    result = exact_dot(fixed * scale, signs, 2)
    for b in range(blocks):
        out_ref[:, b * extent : (b + 1) * extent] = result[b * height : (b + 1) * height, :]


def local(sources, tiles, tile_row, tile_col, tile_count):
    n_row, n_col = lax.axis_size("row"), lax.axis_size("col")
    owners = n_row // n_col
    spans = n_col // 2
    extent = tiles.shape[-1]
    slots = tiles.shape[2]
    height = sources.shape[0]
    blocks = sources.shape[1] // extent
    pair = 2 * height
    row_index, col_index = lax.axis_index("row"), lax.axis_index("col")
    z, x = row_index // owners, row_index % owners
    span, core = col_index // 2, col_index % 2

    def moved(value, to):
        pairs = []
        for a in range(n_row):
            for b in range(n_col):
                zz, xx, yy, cc = to(a // owners, a % owners, b // 2, b % 2)
                pairs.append((a * n_col + b, (zz * owners + xx) * n_col + yy * 2 + cc))
        return lax.ppermute(value, ("row", "col"), pairs)

    def other_core(value):
        return moved(value, lambda zz, xx, yy, cc: (zz, xx, yy, 1 - cc))

    def along_x(value, j):
        return moved(value, lambda zz, xx, yy, cc: (zz, (xx + j) % owners, yy, cc))

    smem = pl.BlockSpec(memory_space=pltpu.SMEM)
    vmem = pl.BlockSpec(memory_space=pltpu.VMEM)
    hbm = pl.BlockSpec(memory_space=pltpu.HBM)
    unread = pl.BlockSpec(memory_space=pl.ANY)

    def call(kernel, name, out_shape, in_specs, out_specs, limit=16, scratch=(), aliases=None, **sizes):
        return pl.pallas_call(
            functools.partial(kernel, **sizes) if sizes else kernel,
            out_shape=out_shape,
            in_specs=in_specs,
            out_specs=out_specs,
            scratch_shapes=scratch,
            input_output_aliases=aliases or {},
            name=name,
            compiler_params=pltpu.CompilerParams(vmem_limit_bytes=int(limit * MIB)),
            cost_estimate=pl.CostEstimate(flops=0, bytes_accessed=MIB, transcendentals=0),
        )

    def in_hbm(value):
        return pltpu.with_memory_space_constraint(value, pltpu.HBM)

    def f32(*dims):
        return jax.ShapeDtypeStruct(dims, jnp.float32)

    def kept(*dims):
        return pltpu.VMEM(dims, jnp.float32)

    def bf16(*dims):
        return jax.ShapeDtypeStruct(dims, jnp.bfloat16)

    place = packed_place(core, span, x, z)

    def after(value, *others):
        return lax.optimization_barrier((value, *others))[0]

    def apart(body, *state):
        return lax.fori_loop(0, jnp.minimum(tile_count.reshape(()), 1), body, state if len(state) > 1 else state[0])

    length = owners * blocks
    stack = in_hbm(tiles.reshape(slots, extent, extent))
    from_core = other_core(sources)
    gathered = -(-n_row // 8) * 8
    every = (spans * pair, extent)
    mine, blank_walk, blank_rest = call(
        prepare_kernel,
        "prepare",
        [kept(*sources.shape), kept(length + gathered, extent), kept(owners * length, extent)],
        [hbm],
        [vmem] * 3,
        scratch=[pltpu.SemaphoreType.DMA],
    )(in_hbm(sources))
    message, first = call(
        front_kernel,
        "front",
        [bf16(blocks * pair, extent), f32(8, extent)],
        [smem, vmem, vmem],
        [vmem] * 2,
        blocks=blocks,
        extent=extent,
    )(place, mine, from_core)
    order, sizes = call(
        list_kernel,
        "lists",
        [pltpu.SMEM((4, slots + UNROLL), jnp.int32), pltpu.SMEM((4,), jnp.int32)],
        [smem] * 4,
        [smem] * 2,
        blocks=blocks,
        owners=owners,
    )(place, in_hbm(tile_row.reshape(-1)), in_hbm(tile_col.reshape(-1)), tile_count.reshape(1))

    direct = [
        moved(message, lambda zz, xx, yy, cc, m=m: (cc * spans + (yy ^ m ^ (spans - 1)), xx, zz // 2, zz % 2))
        for m in range(spans)
    ]

    def early(trip, _):
        cols, line = call(
            edge_kernel,
            "edges",
            [f32(length, extent), f32(length + gathered, extent)],
            [smem] * 4 + [hbm, vmem],
            [vmem] * 2,
            scratch=[
                pltpu.VMEM((slots, SIDE_ROWS, extent), jnp.bfloat16),
                pltpu.VMEM((slots, extent, LANES), jnp.bfloat16),
                pltpu.VMEM((extent, LANES), jnp.float32),
                pltpu.SemaphoreType.DMA((slots,)),
                pltpu.SemaphoreType.DMA((slots,)),
            ],
            owners=owners,
        )(place, trip.reshape(1), order, sizes, stack, first)
        behind = [along_x(line, j) for j in range(1, owners)]
        return call(
            arrange_kernel,
            "arrange",
            [kept(*blank_walk.shape), kept(*blank_rest.shape)],
            [smem] + [vmem] * (1 + owners),
            [vmem] * 2,
        )(place, cols, line, *behind)

    walk, rest = apart(early, blank_walk, blank_rest)
    swapped = [along_x(after(piece, walk), j) for j in range(1, owners) for piece in direct]

    held_tiles = [
        pltpu.VMEM((slots + UNROLL, extent, extent), jnp.bfloat16),
        pltpu.SemaphoreType.DMA((slots + UNROLL,)),
    ]

    sum_shape, ahead_shape = (blocks + 1, *every), (AHEAD, extent, extent)
    later = [kept(*sum_shape), pltpu.VMEM(ahead_shape, jnp.bfloat16)]
    blank_sum, blank_ahead = call(blank_kernel, "blank", later, [unread], [vmem] * 2)(walk)

    def late(trip, state):
        walk, *_ = state
        near, ahead = call(
            near_kernel,
            "near",
            later,
            [smem] * 4 + [hbm] + [vmem] * len(direct),
            [vmem] * 2,
            scratch=[pltpu.VMEM((blocks, *every), jnp.bfloat16), *held_tiles, pltpu.SemaphoreType.DMA((AHEAD,))],
            blocks=blocks,
            spans=spans,
        )(place, trip.reshape(1), order, sizes, stack, *direct)
        for bit in reversed(range((n_row // owners).bit_length() - 1)):
            partner = moved(walk, lambda zz, xx, yy, cc, bit=bit: (zz ^ 2**bit, xx, yy, cc))
            walk = call(
                z_level_kernel, "z_level", kept(*walk.shape), [smem, vmem, vmem, unread], vmem, bit=bit, length=length
            )(place, walk, partner, near)
        return walk, near, ahead

    walk, near, ahead = apart(late, after(walk, *direct), blank_sum, blank_ahead)
    first_row, first_cols, firsts = call(
        coarse_kernel,
        "coarse",
        [f32(length, extent), f32(length, extent), f32(gathered, extent)],
        [smem, vmem, vmem],
        [vmem] * 3,
        blocks=blocks,
        rows=n_row,
    )(place, walk, rest)

    part = blocks * height
    keep, send = call(
        far_kernel,
        "far",
        [f32(spans * part, extent), f32(spans * part + length, extent)],
        [smem] * 3 + [hbm] + [vmem] * 4 + [unread] * len(direct) + [vmem] * len(swapped),
        [vmem] * 2,
        scratch=[
            pltpu.VMEM(((owners - 1) * blocks, *every), jnp.bfloat16),
            pltpu.VMEM((blocks + 1, *every), jnp.float32),
            *held_tiles,
            pltpu.VMEM((spans, blocks * pair, extent), jnp.bfloat16),
            pltpu.SemaphoreType.DMA((spans,)),
        ],
        blocks=blocks,
        owners=owners,
        spans=spans,
    )(place, order, sizes, stack, near, ahead, first_row, first_cols, *direct, *swapped)

    own, both, *outgoing = call(
        combine_kernel,
        "combine",
        [f32(part, extent), f32(2 * length, extent)] + [bf16(part + 2 * length, extent)] * (spans - 1),
        [smem, vmem, vmem, vmem],
        [vmem] * (spans + 1),
    )(place, keep, other_core(send), first_cols)
    arrived = [
        moved(value, lambda zz, xx, yy, cc, j=j: (zz, xx, (yy + j) % spans, cc)) for j, value in enumerate(outgoing, 1)
    ]
    return call(
        back_kernel,
        "back",
        f32(*sources.shape),
        [smem] + [vmem] * (2 + spans),
        vmem,
        blocks=blocks,
        owners=owners,
    )(place, own, both, firsts, *arrived)


def solution(mesh):
    return jax.shard_map(
        local,
        mesh=mesh,
        in_specs=(
            P("col", "row"),
            P("row", "col", None, None, None),
            P("row", "col", None),
            P("row", "col", None),
            P("row", "col"),
        ),
        out_specs=P("col", "row"),
        check_vma=False,
    )
```

```python
import functools
import math

import jax
import jax.numpy as jnp
from jax import lax
from jax.experimental import pallas as pl
from jax.experimental.pallas import tpu as pltpu
from jax.sharding import PartitionSpec as P

ROOT_HALF = 1.0 / math.sqrt(2.0)
SIDE_ROWS = 16
UNROLL = 4
AHEAD = 16
LANES = 128
MIB = 2**20


def haar_parts(extent, transposed):
    k = lax.broadcasted_iota(jnp.int32, (extent, extent), 1 if transposed else 0)
    n = lax.broadcasted_iota(jnp.int32, (extent, extent), 0 if transposed else 1)
    stride = jnp.where(n == 0, extent, n & -n)
    signs = jnp.where((k ^ n) < 2 * stride, jnp.where((k & stride) == 0, 1.0, -1.0), 0.0)
    n = lax.broadcasted_iota(jnp.int32, (1, extent), 1)
    scale = jnp.full((1, extent), 1.0 / math.sqrt(extent), jnp.float32)
    level = 1
    while level < extent:
        scale = jnp.where((n & -n) == level, 1.0 / math.sqrt(2 * level), scale)
        level *= 2
    return signs.astype(jnp.bfloat16), scale


def three_terms(value):
    high = value.astype(jnp.bfloat16)
    rest = value - high.astype(jnp.float32)
    middle = rest.astype(jnp.bfloat16)
    low = (rest - middle.astype(jnp.float32)).astype(jnp.bfloat16)
    return high, middle, low


def exact_dot(value, signs, terms=3):
    return sum(jnp.dot(term, signs, preferred_element_type=jnp.float32) for term in three_terms(value)[:terms])


def block_forward(columns):
    columns = list(columns)
    stride = 1
    while stride < len(columns):
        for p in range(0, len(columns), 2 * stride):
            u, v = columns[p], columns[p + stride]
            columns[p], columns[p + stride] = (u + v) * ROOT_HALF, (u - v) * ROOT_HALF
        stride *= 2
    return columns


def block_inverse(columns):
    columns = list(columns)
    stride = len(columns) // 2
    while stride >= 1:
        for p in range(0, len(columns), 2 * stride):
            u, v = columns[p], columns[p + stride]
            columns[p], columns[p + stride] = (u + v) * ROOT_HALF, (u - v) * ROOT_HALF
        stride //= 2
    return columns


def packed_place(core, span, x, z):
    return (core + 2 * span + 256 * x + 65536 * z).astype(jnp.int32).reshape(1)


def core_of(place_ref):
    return place_ref[0] & 1


def span_of(place_ref):
    return (place_ref[0] >> 1) & 127


def x_of(place_ref):
    return (place_ref[0] >> 8) & 255


def z_of(place_ref):
    return place_ref[0] >> 16


def source_span(place_ref, m, spans):
    return (z_of(place_ref) ^ m ^ (spans - 1)) & (spans - 1)


def prepare_kernel(sources_ref, mine_ref, walk_ref, rest_ref, sem):
    copy = pltpu.make_async_copy(sources_ref, mine_ref, sem)
    copy.start()
    walk_ref[...] = jnp.zeros_like(walk_ref)
    rest_ref[...] = jnp.zeros_like(rest_ref)
    copy.wait()


def front_kernel(place_ref, mine_ref, other_ref, out_ref, first_ref, *, blocks, extent):
    height = mine_ref.shape[0]
    pair = 2 * height
    signs, scale = haar_parts(extent, False)
    mine, other = mine_ref[...], other_ref[...]
    first_core = core_of(place_ref) == 0
    both = jnp.concatenate([jnp.where(first_core, mine, other), jnp.where(first_core, other, mine)], axis=0)
    parts = [both[:, b * extent : (b + 1) * extent] for b in range(blocks)]
    coef = exact_dot(jnp.concatenate(parts, axis=0), signs) * scale
    columns = block_forward([coef[b * pair : (b + 1) * pair, 0:1] for b in range(blocks)])
    lane = lax.broadcasted_iota(jnp.int32, (pair, extent), 1)
    for b in range(blocks):
        column = jnp.zeros_like(columns[0]) if b == 0 else columns[b]
        block = jnp.where(lane == 0, column, coef[b * pair : (b + 1) * pair, :])
        out_ref[b * pair : (b + 1) * pair, :] = block.astype(jnp.bfloat16)
    total = functools.reduce(jnp.add, parts)
    ones = jnp.ones((SIDE_ROWS, extent), jnp.bfloat16)
    first = sum(
        lax.dot_general(ones, term, (((1,), (1,)), ((), ())), preferred_element_type=jnp.float32)
        for term in three_terms(total)
    )
    first_ref[...] = jnp.zeros_like(first_ref)
    first_ref[:, 0:pair] = first[0:8, :] * (1.0 / math.sqrt(blocks * extent))


def list_kernel(place_ref, rows_ref, cols_ref, count_ref, order_ref, sizes_ref, *, blocks, owners):
    x = x_of(place_ref)

    def visit(slot, sizes):
        row, col = rows_ref[slot], cols_ref[slot]
        owner, block = col // blocks, lax.rem(col, blocks)
        behind = lax.rem(x - owner + owners, owners)
        near = behind == 0
        side = jnp.where(near, block, (behind - 1) * blocks + block)
        entry = (slot << 16) + (side << 8) + row
        plain = (slot << 16) + (col << 8) + row
        near_size, far_size, row_size, col_size = sizes
        order_ref[jnp.where(near, 0, 1), jnp.where(near, near_size, far_size)] = entry
        order_ref[2, row_size] = plain
        order_ref[3, col_size] = plain
        one = near.astype(jnp.int32)
        return (
            near_size + one,
            far_size + 1 - one,
            row_size + (row == 0).astype(jnp.int32),
            col_size + (block == 0).astype(jnp.int32),
        )

    sizes = lax.fori_loop(0, count_ref[0], visit, (jnp.int32(0),) * 4)
    for which in range(4):
        sizes_ref[which] = sizes[which]
    for which in range(2):
        for k in range(UNROLL - 1):
            order_ref[which, sizes[which] + k] = blocks


def edge_kernel(
    place_ref,
    _,
    order_ref,
    sizes_ref,
    tiles_ref,
    first_ref,
    cols_ref,
    line_ref,
    strips,
    columns,
    summed,
    strip_sems,
    column_sems,
    *,
    owners,
):
    def strip_copy(index):
        slot = order_ref[3, index] >> 16
        return pltpu.make_async_copy(tiles_ref.at[slot, 0:SIDE_ROWS, :], strips.at[index], strip_sems.at[index])

    def column_copy(index):
        slot = order_ref[2, index] >> 16
        return pltpu.make_async_copy(tiles_ref.at[slot, :, 0:LANES], columns.at[index], column_sems.at[index])

    lax.fori_loop(0, sizes_ref[2], lambda i, _: (column_copy(i).start(), 0)[1], 0)
    lax.fori_loop(0, sizes_ref[3], lambda i, _: (strip_copy(i).start(), 0)[1], 0)
    cols_ref[...] = jnp.zeros_like(cols_ref)
    summed[...] = jnp.zeros_like(summed)
    lane = lax.broadcasted_iota(jnp.int32, summed.shape, 1)

    def add_strip(index, _):
        entry = order_ref[3, index]
        strip_copy(index).wait()
        at = pl.ds(((entry >> 8) & 255) + (entry & 255), 1)
        cols_ref[at, :] += strips[index].astype(jnp.float32)[0:1, :]
        return 0

    def add_column(index, _):
        column_copy(index).wait()
        column = columns[index].astype(jnp.float32)[:, 0:1]
        summed[...] += jnp.where(lane == ((order_ref[2, index] >> 8) & 255), column, 0.0)
        return 0

    lax.fori_loop(0, sizes_ref[3], add_strip, 0)
    lax.fori_loop(0, sizes_ref[2], add_column, 0)
    length = cols_ref.shape[0]
    line_ref[0:length, :] = jnp.transpose(summed[...])[0:length, :]
    index = lax.broadcasted_iota(jnp.int32, (line_ref.shape[0] - length, line_ref.shape[1]), 0)
    own = z_of(place_ref) * owners + x_of(place_ref)
    line_ref[length:, :] = jnp.where(index == own, first_ref[0:1, :], 0.0)


def butterfly(value, partner, index, bit):
    active = lax.rem(index, 2**bit) == 0
    upper = ((index >> bit) & 1) == 1
    return jnp.where(active, jnp.where(upper, partner - value, partner + value) * ROOT_HALF, value)


def arrange_kernel(place_ref, cols_ref, *refs):
    *behind, walk_ref, rest_ref = refs
    owners = len(behind)
    length = cols_ref.shape[0]
    x = x_of(place_ref)
    rest_ref[0:length, :] = cols_ref[...]
    gathered = behind[0][length:, :]
    for j in range(1, owners):
        gathered = gathered + behind[j][length:, :]
    walk_ref[length:, :] = gathered
    for i in range(owners):
        value = behind[0][0:length, :]
        for j in range(1, owners):
            value = jnp.where(lax.rem(x - i + owners, owners) == j, behind[j][0:length, :], value)
        if i == 0:
            walk_ref[0:length, :] = value
        else:
            rest_ref[i * length : (i + 1) * length, :] = value


def z_level_kernel(place_ref, walk_ref, partner_ref, _, out_ref, *, bit, length):
    walk, partner = walk_ref[...], partner_ref[...]
    row = lax.broadcasted_iota(jnp.int32, walk.shape, 0)
    out_ref[...] = jnp.where(row < length, butterfly(walk, partner, z_of(place_ref), bit), walk + partner)


def coarse_kernel(place_ref, walk_ref, rest_ref, row_ref, cols_ref, firsts_ref, *, blocks, rows):
    x = x_of(place_ref)
    length = row_ref.shape[0]
    owners = length // blocks
    by_x = [walk_ref[0:length, :]] + [rest_ref[i * length : (i + 1) * length, :] for i in range(1, owners)]
    by_x = block_inverse(by_x)
    value = by_x[0]
    for i in range(1, owners):
        value = jnp.where(x == i, by_x[i], value)
    row_ref[...] = value
    cols = rest_ref[0:length, :]
    index = lax.broadcasted_iota(jnp.int32, cols.shape, 0)
    lane = lax.broadcasted_iota(jnp.int32, cols.shape, 1)
    cols_ref[...] = jnp.where((lax.rem(index, blocks) == 0) & (lane == 0), value, cols)
    firsts_ref[...] = jnp.zeros_like(firsts_ref)
    for i, first in enumerate(block_forward([walk_ref[length + i : length + i + 1, :] for i in range(rows)])):
        firsts_ref[i : i + 1, :] = first


def fill_sides(sides, messages, place_ref, blocks, spans):
    pair = sides.shape[1] // spans
    for index, message in enumerate(messages):
        behind, m = index // spans, index % spans
        rows = pl.ds(pl.multiple_of(source_span(place_ref, m, spans) * pair, pair), pair)
        for b in range(blocks):
            sides[behind * blocks + b, rows, :] = message[b * pair : (b + 1) * pair, :]


def groups_of(sizes_ref, which):
    return (sizes_ref[which] + UNROLL - 1) // UNROLL


def tile_copy(order_ref, which, index, tiles_ref, held, sems, at):
    slot = order_ref[which, index] >> 16
    return pltpu.make_async_copy(tiles_ref.at[slot], held.at[at], sems.at[at])


def add_group(order_ref, which, index, held, sides, acc):
    for k in range(UNROLL):
        entry = order_ref[which, index * UNROLL + k]
        side, row = (entry >> 8) & 255, entry & 255
        acc[row] += jnp.dot(sides[side], held[index * UNROLL + k], preferred_element_type=jnp.float32)


def blank_kernel(_, sum_ref, ahead_ref):
    sum_ref[0] = jnp.zeros(sum_ref.shape[1:], jnp.float32)
    ahead_ref[0] = jnp.zeros(ahead_ref.shape[1:], jnp.bfloat16)


def near_kernel(place_ref, _, order_ref, sizes_ref, tiles_ref, *refs, blocks, spans):
    *messages, acc_ref, ahead_ref, sides, held, sems, ahead_sems = refs
    groups = groups_of(sizes_ref, 0)
    ahead = jnp.minimum(groups_of(sizes_ref, 1) * UNROLL, AHEAD)

    def own(i):
        return tile_copy(order_ref, 0, i, tiles_ref, held, sems, i)

    def other(i):
        return tile_copy(order_ref, 1, i, tiles_ref, ahead_ref, ahead_sems, i)

    lax.fori_loop(0, groups * UNROLL, lambda i, _: (own(i).start(), 0)[1], 0)
    lax.fori_loop(0, ahead, lambda i, _: (other(i).start(), 0)[1], 0)
    fill_sides(sides, messages, place_ref, blocks, spans)
    acc_ref[...] = jnp.zeros_like(acc_ref)

    def group(index, _):
        for k in range(UNROLL):
            own(index * UNROLL + k).wait()
        add_group(order_ref, 0, index, held, sides, acc_ref)
        return 0

    lax.fori_loop(0, groups, group, 0)
    lax.fori_loop(0, ahead, lambda i, _: (other(i).wait(), 0)[1], 0)


def far_kernel(
    place_ref, order_ref, sizes_ref, tiles_ref, _, ahead_ref, row_ref, cols_ref, *refs, blocks, owners, spans
):
    messages = refs[: owners * spans]
    keep_ref, send_ref, acc, sides, held, sems, near_sides, near_sems = refs[owners * spans :]
    copies = [
        pltpu.make_async_copy(messages[m], near_sides.at[m], near_sems.at[m]) for m in range(spans)
    ]
    for copy in copies:
        copy.start()
    groups = groups_of(sizes_ref, 1)
    ahead = jnp.minimum(groups, AHEAD // UNROLL)

    def fetch(i):
        return tile_copy(order_ref, 1, i, tiles_ref, held, sems, i)

    lax.fori_loop(ahead * UNROLL, groups * UNROLL, lambda i, _: (fetch(i).start(), 0)[1], 0)
    extent = tiles_ref.shape[-1]
    pair = sides.shape[1] // spans
    height = pair // 2
    x = x_of(place_ref)
    fill_sides(sides, messages[spans:], place_ref, blocks, spans)

    def ready(index, _):
        add_group(order_ref, 1, index, ahead_ref, sides, acc)
        return 0

    def group(index, _):
        for k in range(UNROLL):
            fetch(index * UNROLL + k).wait()
        add_group(order_ref, 1, index, held, sides, acc)
        return 0

    lax.fori_loop(0, ahead, ready, 0)
    lax.fori_loop(ahead, groups, group, 0)

    for copy in copies:
        copy.wait()
    messages = (*(near_sides.at[m] for m in range(spans)), *messages[spans:])
    lane = lax.broadcasted_iota(jnp.int32, (pair, extent), 1)
    for m in range(spans):
        rows = pl.ds(pl.multiple_of(source_span(place_ref, m, spans) * pair, pair), pair)
        total = jnp.zeros((pair, extent), jnp.float32)
        for behind in range(owners):
            owner = lax.rem(x - behind + owners, owners)
            message = messages[behind * spans + m]
            for b in range(blocks):
                line = row_ref[pl.ds(owner * blocks + b, 1), :]
                total += message[b * pair : (b + 1) * pair, :].astype(jnp.float32) * line
        top = jnp.sum(total, axis=1, keepdims=True)
        acc[0, rows, :] = jnp.where(lane == 0, top, acc[0, rows, :])
    first_core = core_of(place_ref) == 0
    for i in range(blocks):
        value = acc[i]
        for y in range(spans):
            one = value[y * pair : y * pair + height, :]
            two = value[y * pair + height : (y + 1) * pair, :]
            at = (y * blocks + i) * height
            keep_ref[at : at + height, :] = jnp.where(first_core, one, two)
            send_ref[at : at + height, :] = jnp.where(first_core, two, one).astype(jnp.bfloat16)
    send_ref[spans * blocks * height :, :] = cols_ref[...].astype(jnp.bfloat16)


def combine_kernel(place_ref, keep_ref, arrived_ref, cols_ref, own_ref, both_ref, *out_refs):
    spans = len(out_refs) + 1
    span = span_of(place_ref)
    rows = own_ref.shape[0]
    length = cols_ref.shape[0]
    first_core = core_of(place_ref) == 0
    mine, other = cols_ref[...], arrived_ref[spans * rows :, :].astype(jnp.float32)
    both_ref[0:length, :] = jnp.where(first_core, mine, other)
    both_ref[length:, :] = jnp.where(first_core, other, mine)
    at = pl.ds(pl.multiple_of(span * rows, rows), rows)
    own_ref[...] = keep_ref[at, :] + arrived_ref[at, :].astype(jnp.float32)
    both = both_ref[...].astype(jnp.bfloat16)
    for j, out_ref in enumerate(out_refs, 1):
        at = pl.ds(pl.multiple_of(lax.rem(span + j, spans) * rows, rows), rows)
        out_ref[0:rows, :] = (keep_ref[at, :] + arrived_ref[at, :].astype(jnp.float32)).astype(jnp.bfloat16)
        out_ref[rows:, :] = both


def back_kernel(place_ref, own_ref, both_ref, firsts_ref, *refs, blocks, owners):
    *arrived, out_ref = refs
    spans = len(arrived) + 1
    extent = own_ref.shape[1]
    rows = own_ref.shape[0]
    height = rows // blocks
    span = span_of(place_ref)
    total = own_ref[...]
    for part in arrived:
        total = total + part[0:rows, :].astype(jnp.float32)
    tables, picked = [both_ref[...]], []
    for part in arrived:
        tables.append(part[rows:, :].astype(jnp.float32))
    for j in range(spans):
        source = lax.rem(span - j + spans, spans)
        for k in range(2 * owners):
            picked.append(firsts_ref[pl.ds(source * 2 * owners + k, 1), :])
    picked += [jnp.zeros_like(picked[0])] * (-len(picked) % 16)
    columns = jnp.transpose(jnp.concatenate(picked, axis=0))
    columns = jnp.where(core_of(place_ref) == 0, columns[0:height, :], columns[height : 2 * height, :])
    blocks_of = []
    for b in range(blocks):
        value = total[b * height : (b + 1) * height, :]
        for j, table in enumerate(tables):
            for k in range(2 * owners):
                at = k * blocks + b
                index = j * 2 * owners + k
                value = value + columns[:, index : index + 1] * table[at : at + 1, :]
        blocks_of.append(value)
    columns = block_inverse([value[:, 0:1] for value in blocks_of])
    lane = lax.broadcasted_iota(jnp.int32, (height, extent), 1)
    fixed = jnp.concatenate([jnp.where(lane == 0, columns[b], blocks_of[b]) for b in range(blocks)], axis=0)
    signs, scale = haar_parts(extent, True)
    result = exact_dot(fixed * scale, signs, 2)
    for b in range(blocks):
        out_ref[:, b * extent : (b + 1) * extent] = result[b * height : (b + 1) * height, :]


def local(sources, tiles, tile_row, tile_col, tile_count):
    n_row, n_col = lax.axis_size("row"), lax.axis_size("col")
    owners = n_row // n_col
    spans = n_col // 2
    extent = tiles.shape[-1]
    slots = tiles.shape[2]
    height = sources.shape[0]
    blocks = sources.shape[1] // extent
    pair = 2 * height
    row_index, col_index = lax.axis_index("row"), lax.axis_index("col")
    z, x = row_index // owners, row_index % owners
    span, core = col_index // 2, col_index % 2

    def moved(value, to):
        pairs = []
        for a in range(n_row):
            for b in range(n_col):
                zz, xx, yy, cc = to(a // owners, a % owners, b // 2, b % 2)
                pairs.append((a * n_col + b, (zz * owners + xx) * n_col + yy * 2 + cc))
        return lax.ppermute(value, ("row", "col"), pairs)

    def other_core(value):
        return moved(value, lambda zz, xx, yy, cc: (zz, xx, yy, 1 - cc))

    def along_x(value, j):
        return moved(value, lambda zz, xx, yy, cc: (zz, (xx + j) % owners, yy, cc))

    smem = pl.BlockSpec(memory_space=pltpu.SMEM)
    vmem = pl.BlockSpec(memory_space=pltpu.VMEM)
    hbm = pl.BlockSpec(memory_space=pltpu.HBM)
    unread = pl.BlockSpec(memory_space=pl.ANY)

    def call(kernel, name, out_shape, in_specs, out_specs, limit=16, scratch=(), aliases=None, **sizes):
        return pl.pallas_call(
            functools.partial(kernel, **sizes) if sizes else kernel,
            out_shape=out_shape,
            in_specs=in_specs,
            out_specs=out_specs,
            scratch_shapes=scratch,
            input_output_aliases=aliases or {},
            name=name,
            compiler_params=pltpu.CompilerParams(vmem_limit_bytes=int(limit * MIB)),
            cost_estimate=pl.CostEstimate(flops=0, bytes_accessed=MIB, transcendentals=0),
        )

    def in_hbm(value):
        return pltpu.with_memory_space_constraint(value, pltpu.HBM)

    def f32(*dims):
        return jax.ShapeDtypeStruct(dims, jnp.float32)

    def kept(*dims):
        return pltpu.VMEM(dims, jnp.float32)

    def bf16(*dims):
        return jax.ShapeDtypeStruct(dims, jnp.bfloat16)

    place = packed_place(core, span, x, z)

    def after(value, *others):
        return lax.optimization_barrier((value, *others))[0]

    def apart(body, *state):
        return lax.fori_loop(0, jnp.minimum(tile_count.reshape(()), 1), body, state if len(state) > 1 else state[0])

    length = owners * blocks
    stack = in_hbm(tiles.reshape(slots, extent, extent))
    from_core = other_core(sources)
    gathered = -(-n_row // 8) * 8
    every = (spans * pair, extent)
    mine, blank_walk, blank_rest = call(
        prepare_kernel,
        "prepare",
        [kept(*sources.shape), kept(length + gathered, extent), kept(owners * length, extent)],
        [hbm],
        [vmem] * 3,
        scratch=[pltpu.SemaphoreType.DMA],
    )(in_hbm(sources))
    message, first = call(
        front_kernel,
        "front",
        [bf16(blocks * pair, extent), f32(8, extent)],
        [smem, vmem, vmem],
        [vmem] * 2,
        blocks=blocks,
        extent=extent,
    )(place, mine, from_core)
    order, sizes = call(
        list_kernel,
        "lists",
        [pltpu.SMEM((4, slots + UNROLL), jnp.int32), pltpu.SMEM((4,), jnp.int32)],
        [smem] * 4,
        [smem] * 2,
        blocks=blocks,
        owners=owners,
    )(place, in_hbm(tile_row.reshape(-1)), in_hbm(tile_col.reshape(-1)), tile_count.reshape(1))

    direct = [
        moved(message, lambda zz, xx, yy, cc, m=m: (cc * spans + (yy ^ m ^ (spans - 1)), xx, zz // 2, zz % 2))
        for m in range(spans)
    ]

    def early(trip, _):
        cols, line = call(
            edge_kernel,
            "edges",
            [f32(length, extent), f32(length + gathered, extent)],
            [smem] * 4 + [hbm, vmem],
            [vmem] * 2,
            scratch=[
                pltpu.VMEM((slots, SIDE_ROWS, extent), jnp.bfloat16),
                pltpu.VMEM((slots, extent, LANES), jnp.bfloat16),
                pltpu.VMEM((extent, LANES), jnp.float32),
                pltpu.SemaphoreType.DMA((slots,)),
                pltpu.SemaphoreType.DMA((slots,)),
            ],
            owners=owners,
        )(place, trip.reshape(1), order, sizes, stack, first)
        behind = [along_x(line, j) for j in range(1, owners)]
        return call(
            arrange_kernel,
            "arrange",
            [kept(*blank_walk.shape), kept(*blank_rest.shape)],
            [smem] + [vmem] * (1 + owners),
            [vmem] * 2,
        )(place, cols, line, *behind)

    walk, rest = apart(early, blank_walk, blank_rest)
    swapped = [along_x(after(piece, walk), j) for j in range(1, owners) for piece in direct]

    held_tiles = [
        pltpu.VMEM((slots + UNROLL, extent, extent), jnp.bfloat16),
        pltpu.SemaphoreType.DMA((slots + UNROLL,)),
    ]

    sum_shape, ahead_shape = (blocks + 1, *every), (AHEAD, extent, extent)
    later = [kept(*sum_shape), pltpu.VMEM(ahead_shape, jnp.bfloat16)]
    blank_sum, blank_ahead = call(blank_kernel, "blank", later, [unread], [vmem] * 2)(walk)

    def late(trip, state):
        walk, *_ = state
        near, ahead = call(
            near_kernel,
            "near",
            later,
            [smem] * 4 + [hbm] + [vmem] * len(direct),
            [vmem] * 2,
            scratch=[pltpu.VMEM((blocks, *every), jnp.bfloat16), *held_tiles, pltpu.SemaphoreType.DMA((AHEAD,))],
            blocks=blocks,
            spans=spans,
        )(place, trip.reshape(1), order, sizes, stack, *direct)
        for bit in reversed(range((n_row // owners).bit_length() - 1)):
            partner = moved(walk, lambda zz, xx, yy, cc, bit=bit: (zz ^ 2**bit, xx, yy, cc))
            walk = call(
                z_level_kernel, "z_level", kept(*walk.shape), [smem, vmem, vmem, unread], vmem, bit=bit, length=length
            )(place, walk, partner, near)
        return walk, near, ahead

    walk, near, ahead = apart(late, after(walk, *direct), blank_sum, blank_ahead)
    first_row, first_cols, firsts = call(
        coarse_kernel,
        "coarse",
        [f32(length, extent), f32(length, extent), f32(gathered, extent)],
        [smem, vmem, vmem],
        [vmem] * 3,
        blocks=blocks,
        rows=n_row,
    )(place, walk, rest)

    part = blocks * height
    keep, send, _ = call(
        far_kernel,
        "far",
        [f32(spans * part, extent), bf16(spans * part + length, extent), kept(*sum_shape)],
        [smem] * 3 + [hbm] + [vmem] * 4 + [unread] * len(direct) + [vmem] * len(swapped),
        [vmem] * 3,
        aliases={4: 2},
        scratch=[
            pltpu.VMEM(((owners - 1) * blocks, *every), jnp.bfloat16),
            *held_tiles,
            pltpu.VMEM((spans, blocks * pair, extent), jnp.bfloat16),
            pltpu.SemaphoreType.DMA((spans,)),
        ],
        blocks=blocks,
        owners=owners,
        spans=spans,
    )(place, order, sizes, stack, near, ahead, first_row, first_cols, *direct, *swapped)

    own, both, *outgoing = call(
        combine_kernel,
        "combine",
        [f32(part, extent), f32(2 * length, extent)] + [bf16(part + 2 * length, extent)] * (spans - 1),
        [smem, vmem, vmem, vmem],
        [vmem] * (spans + 1),
    )(place, keep, other_core(send), first_cols)
    arrived = [
        moved(value, lambda zz, xx, yy, cc, j=j: (zz, xx, (yy + j) % spans, cc)) for j, value in enumerate(outgoing, 1)
    ]
    return call(
        back_kernel,
        "back",
        f32(*sources.shape),
        [smem] + [vmem] * (2 + spans),
        vmem,
        blocks=blocks,
        owners=owners,
    )(place, own, both, firsts, *arrived)


def solution(mesh):
    return jax.shard_map(
        local,
        mesh=mesh,
        in_specs=(
            P("col", "row"),
            P("row", "col", None, None, None),
            P("row", "col", None),
            P("row", "col", None),
            P("row", "col"),
        ),
        out_specs=P("col", "row"),
        check_vma=False,
    )
```

```python
import functools
import math

import jax
import jax.numpy as jnp
from jax import lax
from jax.experimental import pallas as pl
from jax.experimental.pallas import tpu as pltpu
from jax.sharding import PartitionSpec as P

ROOT_HALF = 1.0 / math.sqrt(2.0)
SIDE_ROWS = 16
UNROLL = 4
AHEAD = 12
LANES = 128
MIB = 2**20


def haar_parts(extent, transposed):
    k = lax.broadcasted_iota(jnp.int32, (extent, extent), 1 if transposed else 0)
    n = lax.broadcasted_iota(jnp.int32, (extent, extent), 0 if transposed else 1)
    stride = jnp.where(n == 0, extent, n & -n)
    signs = jnp.where((k ^ n) < 2 * stride, jnp.where((k & stride) == 0, 1.0, -1.0), 0.0)
    n = lax.broadcasted_iota(jnp.int32, (1, extent), 1)
    scale = jnp.full((1, extent), 1.0 / math.sqrt(extent), jnp.float32)
    level = 1
    while level < extent:
        scale = jnp.where((n & -n) == level, 1.0 / math.sqrt(2 * level), scale)
        level *= 2
    return signs.astype(jnp.bfloat16), scale


def three_terms(value):
    high = value.astype(jnp.bfloat16)
    rest = value - high.astype(jnp.float32)
    middle = rest.astype(jnp.bfloat16)
    low = (rest - middle.astype(jnp.float32)).astype(jnp.bfloat16)
    return high, middle, low


def exact_dot(value, signs, terms=3):
    return sum(jnp.dot(term, signs, preferred_element_type=jnp.float32) for term in three_terms(value)[:terms])


def block_forward(columns):
    columns = list(columns)
    stride = 1
    while stride < len(columns):
        for p in range(0, len(columns), 2 * stride):
            u, v = columns[p], columns[p + stride]
            columns[p], columns[p + stride] = (u + v) * ROOT_HALF, (u - v) * ROOT_HALF
        stride *= 2
    return columns


def block_inverse(columns):
    columns = list(columns)
    stride = len(columns) // 2
    while stride >= 1:
        for p in range(0, len(columns), 2 * stride):
            u, v = columns[p], columns[p + stride]
            columns[p], columns[p + stride] = (u + v) * ROOT_HALF, (u - v) * ROOT_HALF
        stride //= 2
    return columns


def packed_place(core, span, x, z):
    return (core + 2 * span + 256 * x + 65536 * z).astype(jnp.int32).reshape(1)


def core_of(place_ref):
    return place_ref[0] & 1


def span_of(place_ref):
    return (place_ref[0] >> 1) & 127


def x_of(place_ref):
    return (place_ref[0] >> 8) & 255


def z_of(place_ref):
    return place_ref[0] >> 16


def source_span(place_ref, m, spans):
    return (z_of(place_ref) ^ m ^ (spans - 1)) & (spans - 1)


def prepare_kernel(sources_ref, mine_ref, walk_ref, rest_ref, sem):
    copy = pltpu.make_async_copy(sources_ref, mine_ref, sem)
    copy.start()
    walk_ref[...] = jnp.zeros_like(walk_ref)
    rest_ref[...] = jnp.zeros_like(rest_ref)
    copy.wait()


def front_kernel(place_ref, mine_ref, other_ref, out_ref, first_ref, *, blocks, extent):
    height = mine_ref.shape[0]
    pair = 2 * height
    signs, scale = haar_parts(extent, False)
    mine, other = mine_ref[...], other_ref[...]
    first_core = core_of(place_ref) == 0
    both = jnp.concatenate([jnp.where(first_core, mine, other), jnp.where(first_core, other, mine)], axis=0)
    parts = [both[:, b * extent : (b + 1) * extent] for b in range(blocks)]
    coef = exact_dot(jnp.concatenate(parts, axis=0), signs) * scale
    columns = block_forward([coef[b * pair : (b + 1) * pair, 0:1] for b in range(blocks)])
    lane = lax.broadcasted_iota(jnp.int32, (pair, extent), 1)
    for b in range(blocks):
        column = jnp.zeros_like(columns[0]) if b == 0 else columns[b]
        block = jnp.where(lane == 0, column, coef[b * pair : (b + 1) * pair, :])
        out_ref[b * pair : (b + 1) * pair, :] = block.astype(jnp.bfloat16)
    total = functools.reduce(jnp.add, parts)
    ones = jnp.ones((SIDE_ROWS, extent), jnp.bfloat16)
    first = sum(
        lax.dot_general(ones, term, (((1,), (1,)), ((), ())), preferred_element_type=jnp.float32)
        for term in three_terms(total)
    )
    first_ref[...] = jnp.zeros_like(first_ref)
    first_ref[:, 0:pair] = first[0:8, :] * (1.0 / math.sqrt(blocks * extent))


def list_kernel(place_ref, rows_ref, cols_ref, count_ref, order_ref, sizes_ref, *, blocks, owners):
    x = x_of(place_ref)

    def visit(slot, sizes):
        row, col = rows_ref[slot], cols_ref[slot]
        owner, block = col // blocks, lax.rem(col, blocks)
        behind = lax.rem(x - owner + owners, owners)
        near = behind == 0
        side = jnp.where(near, block, (behind - 1) * blocks + block)
        entry = (slot << 16) + (side << 8) + row
        plain = (slot << 16) + (col << 8) + row
        near_size, far_size, row_size, col_size = sizes
        order_ref[jnp.where(near, 0, 1), jnp.where(near, near_size, far_size)] = entry
        order_ref[2, row_size] = plain
        order_ref[3, col_size] = plain
        one = near.astype(jnp.int32)
        return (
            near_size + one,
            far_size + 1 - one,
            row_size + (row == 0).astype(jnp.int32),
            col_size + (block == 0).astype(jnp.int32),
        )

    sizes = lax.fori_loop(0, count_ref[0], visit, (jnp.int32(0),) * 4)
    for which in range(4):
        sizes_ref[which] = sizes[which]
    for which in range(2):
        for k in range(UNROLL - 1):
            order_ref[which, sizes[which] + k] = blocks


def edge_kernel(
    place_ref,
    _,
    order_ref,
    sizes_ref,
    tiles_ref,
    first_ref,
    cols_ref,
    line_ref,
    strips,
    columns,
    summed,
    strip_sems,
    column_sems,
    *,
    owners,
):
    def strip_copy(index):
        slot = order_ref[3, index] >> 16
        return pltpu.make_async_copy(tiles_ref.at[slot, 0:SIDE_ROWS, :], strips.at[index], strip_sems.at[index])

    def column_copy(index):
        slot = order_ref[2, index] >> 16
        return pltpu.make_async_copy(tiles_ref.at[slot, :, 0:LANES], columns.at[index], column_sems.at[index])

    lax.fori_loop(0, sizes_ref[2], lambda i, _: (column_copy(i).start(), 0)[1], 0)
    lax.fori_loop(0, sizes_ref[3], lambda i, _: (strip_copy(i).start(), 0)[1], 0)
    cols_ref[...] = jnp.zeros_like(cols_ref)
    summed[...] = jnp.zeros_like(summed)
    lane = lax.broadcasted_iota(jnp.int32, summed.shape, 1)

    def add_strip(index, _):
        entry = order_ref[3, index]
        strip_copy(index).wait()
        at = pl.ds(((entry >> 8) & 255) + (entry & 255), 1)
        cols_ref[at, :] += strips[index].astype(jnp.float32)[0:1, :]
        return 0

    def add_column(index, _):
        column_copy(index).wait()
        column = columns[index].astype(jnp.float32)[:, 0:1]
        summed[...] += jnp.where(lane == ((order_ref[2, index] >> 8) & 255), column, 0.0)
        return 0

    lax.fori_loop(0, sizes_ref[3], add_strip, 0)
    lax.fori_loop(0, sizes_ref[2], add_column, 0)
    length = cols_ref.shape[0]
    line_ref[0:length, :] = jnp.transpose(summed[...])[0:length, :]
    index = lax.broadcasted_iota(jnp.int32, (line_ref.shape[0] - length, line_ref.shape[1]), 0)
    own = z_of(place_ref) * owners + x_of(place_ref)
    line_ref[length:, :] = jnp.where(index == own, first_ref[0:1, :], 0.0)


def butterfly(value, partner, index, bit):
    active = lax.rem(index, 2**bit) == 0
    upper = ((index >> bit) & 1) == 1
    return jnp.where(active, jnp.where(upper, partner - value, partner + value) * ROOT_HALF, value)


def arrange_kernel(place_ref, cols_ref, *refs):
    *behind, walk_ref, rest_ref = refs
    owners = len(behind)
    length = cols_ref.shape[0]
    x = x_of(place_ref)
    rest_ref[0:length, :] = cols_ref[...]
    gathered = behind[0][length:, :]
    for j in range(1, owners):
        gathered = gathered + behind[j][length:, :]
    walk_ref[length:, :] = gathered
    for i in range(owners):
        value = behind[0][0:length, :]
        for j in range(1, owners):
            value = jnp.where(lax.rem(x - i + owners, owners) == j, behind[j][0:length, :], value)
        if i == 0:
            walk_ref[0:length, :] = value
        else:
            rest_ref[i * length : (i + 1) * length, :] = value


def z_level_kernel(place_ref, walk_ref, partner_ref, _, out_ref, *, bit, length):
    walk, partner = walk_ref[...], partner_ref[...]
    row = lax.broadcasted_iota(jnp.int32, walk.shape, 0)
    out_ref[...] = jnp.where(row < length, butterfly(walk, partner, z_of(place_ref), bit), walk + partner)


def coarse_kernel(place_ref, walk_ref, rest_ref, row_ref, cols_ref, firsts_ref, *, blocks, rows):
    x = x_of(place_ref)
    length = row_ref.shape[0]
    owners = length // blocks
    by_x = [walk_ref[0:length, :]] + [rest_ref[i * length : (i + 1) * length, :] for i in range(1, owners)]
    by_x = block_inverse(by_x)
    value = by_x[0]
    for i in range(1, owners):
        value = jnp.where(x == i, by_x[i], value)
    row_ref[...] = value
    cols = rest_ref[0:length, :]
    index = lax.broadcasted_iota(jnp.int32, cols.shape, 0)
    lane = lax.broadcasted_iota(jnp.int32, cols.shape, 1)
    cols_ref[...] = jnp.where((lax.rem(index, blocks) == 0) & (lane == 0), value, cols)
    firsts_ref[...] = jnp.zeros_like(firsts_ref)
    for i, first in enumerate(block_forward([walk_ref[length + i : length + i + 1, :] for i in range(rows)])):
        firsts_ref[i : i + 1, :] = first


def fill_sides(sides, messages, place_ref, blocks, spans):
    pair = sides.shape[1] // spans
    for index, message in enumerate(messages):
        behind, m = index // spans, index % spans
        rows = pl.ds(pl.multiple_of(source_span(place_ref, m, spans) * pair, pair), pair)
        for b in range(blocks):
            sides[behind * blocks + b, rows, :] = message[b * pair : (b + 1) * pair, :]


def groups_of(sizes_ref, which):
    return (sizes_ref[which] + UNROLL - 1) // UNROLL


def tile_copy(order_ref, which, index, tiles_ref, held, sems, at):
    slot = order_ref[which, index] >> 16
    return pltpu.make_async_copy(tiles_ref.at[slot], held.at[at], sems.at[at])


def add_group(order_ref, which, index, held, sides, acc):
    for k in range(UNROLL):
        entry = order_ref[which, index * UNROLL + k]
        side, row = (entry >> 8) & 255, entry & 255
        acc[row] += jnp.dot(sides[side], held[index * UNROLL + k], preferred_element_type=jnp.float32)


def blank_kernel(_, sum_ref, ahead_ref):
    sum_ref[0] = jnp.zeros(sum_ref.shape[1:], jnp.float32)
    ahead_ref[0] = jnp.zeros(ahead_ref.shape[1:], jnp.bfloat16)


def near_kernel(place_ref, _, order_ref, sizes_ref, tiles_ref, *refs, blocks, spans):
    *messages, acc_ref, ahead_ref, sides, held, sems, ahead_sems = refs
    groups = groups_of(sizes_ref, 0)
    ahead = jnp.minimum(groups_of(sizes_ref, 1) * UNROLL, AHEAD)

    def own(i):
        return tile_copy(order_ref, 0, i, tiles_ref, held, sems, i)

    def other(i):
        return tile_copy(order_ref, 1, i, tiles_ref, ahead_ref, ahead_sems, i)

    lax.fori_loop(0, groups * UNROLL, lambda i, _: (own(i).start(), 0)[1], 0)
    lax.fori_loop(0, ahead, lambda i, _: (other(i).start(), 0)[1], 0)
    fill_sides(sides, messages, place_ref, blocks, spans)
    acc_ref[...] = jnp.zeros_like(acc_ref)

    def group(index, _):
        for k in range(UNROLL):
            own(index * UNROLL + k).wait()
        add_group(order_ref, 0, index, held, sides, acc_ref)
        return 0

    lax.fori_loop(0, groups, group, 0)
    lax.fori_loop(0, ahead, lambda i, _: (other(i).wait(), 0)[1], 0)


def far_kernel(
    place_ref, order_ref, sizes_ref, tiles_ref, _, ahead_ref, row_ref, cols_ref, *refs, blocks, owners, spans
):
    messages = refs[: owners * spans]
    keep_ref, send_ref, acc, sides, held, sems, near_sides, near_sems = refs[owners * spans :]
    copies = [
        pltpu.make_async_copy(messages[m], near_sides.at[m], near_sems.at[m]) for m in range(spans)
    ]
    for copy in copies:
        copy.start()
    groups = groups_of(sizes_ref, 1)
    ahead = jnp.minimum(groups, AHEAD // UNROLL)

    def fetch(i):
        return tile_copy(order_ref, 1, i, tiles_ref, held, sems, i)

    lax.fori_loop(ahead * UNROLL, groups * UNROLL, lambda i, _: (fetch(i).start(), 0)[1], 0)
    extent = tiles_ref.shape[-1]
    pair = sides.shape[1] // spans
    height = pair // 2
    x = x_of(place_ref)
    fill_sides(sides, messages[spans:], place_ref, blocks, spans)

    def ready(index, _):
        add_group(order_ref, 1, index, ahead_ref, sides, acc)
        return 0

    def group(index, _):
        for k in range(UNROLL):
            fetch(index * UNROLL + k).wait()
        add_group(order_ref, 1, index, held, sides, acc)
        return 0

    lax.fori_loop(0, ahead, ready, 0)
    lax.fori_loop(ahead, groups, group, 0)

    for copy in copies:
        copy.wait()
    messages = (*(near_sides.at[m] for m in range(spans)), *messages[spans:])
    lane = lax.broadcasted_iota(jnp.int32, (pair, extent), 1)
    for m in range(spans):
        rows = pl.ds(pl.multiple_of(source_span(place_ref, m, spans) * pair, pair), pair)
        total = jnp.zeros((pair, extent), jnp.float32)
        for behind in range(owners):
            owner = lax.rem(x - behind + owners, owners)
            message = messages[behind * spans + m]
            for b in range(blocks):
                line = row_ref[pl.ds(owner * blocks + b, 1), :]
                total += message[b * pair : (b + 1) * pair, :].astype(jnp.float32) * line
        top = jnp.sum(total, axis=1, keepdims=True)
        acc[0, rows, :] = jnp.where(lane == 0, top, acc[0, rows, :])
    first_core = core_of(place_ref) == 0
    for i in range(blocks):
        value = acc[i]
        for y in range(spans):
            one = value[y * pair : y * pair + height, :]
            two = value[y * pair + height : (y + 1) * pair, :]
            at = (y * blocks + i) * height
            keep_ref[at : at + height, :] = jnp.where(first_core, one, two)
            send_ref[at : at + height, :] = jnp.where(first_core, two, one).astype(jnp.bfloat16)
    send_ref[spans * blocks * height :, :] = cols_ref[...].astype(jnp.bfloat16)


def combine_kernel(place_ref, keep_ref, arrived_ref, cols_ref, own_ref, both_ref, *out_refs):
    spans = len(out_refs) + 1
    span = span_of(place_ref)
    rows = own_ref.shape[0]
    length = cols_ref.shape[0]
    first_core = core_of(place_ref) == 0
    mine, other = cols_ref[...], arrived_ref[spans * rows :, :].astype(jnp.float32)
    both_ref[0:length, :] = jnp.where(first_core, mine, other)
    both_ref[length:, :] = jnp.where(first_core, other, mine)
    at = pl.ds(pl.multiple_of(span * rows, rows), rows)
    own_ref[...] = keep_ref[at, :] + arrived_ref[at, :].astype(jnp.float32)
    both = both_ref[...].astype(jnp.bfloat16)
    for j, out_ref in enumerate(out_refs, 1):
        at = pl.ds(pl.multiple_of(lax.rem(span + j, spans) * rows, rows), rows)
        out_ref[0:rows, :] = (keep_ref[at, :] + arrived_ref[at, :].astype(jnp.float32)).astype(jnp.bfloat16)
        out_ref[rows:, :] = both


def back_kernel(place_ref, own_ref, both_ref, firsts_ref, *refs, blocks, owners):
    *arrived, out_ref = refs
    spans = len(arrived) + 1
    extent = own_ref.shape[1]
    rows = own_ref.shape[0]
    height = rows // blocks
    span = span_of(place_ref)
    total = own_ref[...]
    for part in arrived:
        total = total + part[0:rows, :].astype(jnp.float32)
    tables, picked = [both_ref[...]], []
    for part in arrived:
        tables.append(part[rows:, :].astype(jnp.float32))
    for j in range(spans):
        source = lax.rem(span - j + spans, spans)
        for k in range(2 * owners):
            picked.append(firsts_ref[pl.ds(source * 2 * owners + k, 1), :])
    picked += [jnp.zeros_like(picked[0])] * (-len(picked) % 16)
    columns = jnp.transpose(jnp.concatenate(picked, axis=0))
    columns = jnp.where(core_of(place_ref) == 0, columns[0:height, :], columns[height : 2 * height, :])
    blocks_of = []
    for b in range(blocks):
        value = total[b * height : (b + 1) * height, :]
        for j, table in enumerate(tables):
            for k in range(2 * owners):
                at = k * blocks + b
                index = j * 2 * owners + k
                value = value + columns[:, index : index + 1] * table[at : at + 1, :]
        blocks_of.append(value)
    columns = block_inverse([value[:, 0:1] for value in blocks_of])
    lane = lax.broadcasted_iota(jnp.int32, (height, extent), 1)
    fixed = jnp.concatenate([jnp.where(lane == 0, columns[b], blocks_of[b]) for b in range(blocks)], axis=0)
    signs, scale = haar_parts(extent, True)
    result = exact_dot(fixed * scale, signs, 2)
    for b in range(blocks):
        out_ref[:, b * extent : (b + 1) * extent] = result[b * height : (b + 1) * height, :]


def local(sources, tiles, tile_row, tile_col, tile_count):
    n_row, n_col = lax.axis_size("row"), lax.axis_size("col")
    owners = n_row // n_col
    spans = n_col // 2
    extent = tiles.shape[-1]
    slots = tiles.shape[2]
    height = sources.shape[0]
    blocks = sources.shape[1] // extent
    pair = 2 * height
    row_index, col_index = lax.axis_index("row"), lax.axis_index("col")
    z, x = row_index // owners, row_index % owners
    span, core = col_index // 2, col_index % 2

    def moved(value, to):
        pairs = []
        for a in range(n_row):
            for b in range(n_col):
                zz, xx, yy, cc = to(a // owners, a % owners, b // 2, b % 2)
                pairs.append((a * n_col + b, (zz * owners + xx) * n_col + yy * 2 + cc))
        return lax.ppermute(value, ("row", "col"), pairs)

    def other_core(value):
        return moved(value, lambda zz, xx, yy, cc: (zz, xx, yy, 1 - cc))

    def along_x(value, j):
        return moved(value, lambda zz, xx, yy, cc: (zz, (xx + j) % owners, yy, cc))

    smem = pl.BlockSpec(memory_space=pltpu.SMEM)
    vmem = pl.BlockSpec(memory_space=pltpu.VMEM)
    hbm = pl.BlockSpec(memory_space=pltpu.HBM)
    unread = pl.BlockSpec(memory_space=pl.ANY)

    def call(kernel, name, out_shape, in_specs, out_specs, limit=16, scratch=(), aliases=None, **sizes):
        return pl.pallas_call(
            functools.partial(kernel, **sizes) if sizes else kernel,
            out_shape=out_shape,
            in_specs=in_specs,
            out_specs=out_specs,
            scratch_shapes=scratch,
            input_output_aliases=aliases or {},
            name=name,
            compiler_params=pltpu.CompilerParams(vmem_limit_bytes=int(limit * MIB)),
            cost_estimate=pl.CostEstimate(flops=0, bytes_accessed=MIB, transcendentals=0),
        )

    def in_hbm(value):
        return pltpu.with_memory_space_constraint(value, pltpu.HBM)

    def f32(*dims):
        return jax.ShapeDtypeStruct(dims, jnp.float32)

    def kept(*dims):
        return pltpu.VMEM(dims, jnp.float32)

    def bf16(*dims):
        return jax.ShapeDtypeStruct(dims, jnp.bfloat16)

    place = packed_place(core, span, x, z)

    def after(value, *others):
        return lax.optimization_barrier((value, *others))[0]

    def apart(body, *state):
        return lax.fori_loop(0, jnp.minimum(tile_count.reshape(()), 1), body, state if len(state) > 1 else state[0])

    length = owners * blocks
    stack = in_hbm(tiles.reshape(slots, extent, extent))
    from_core = other_core(sources)
    gathered = -(-n_row // 8) * 8
    every = (spans * pair, extent)
    mine, blank_walk, blank_rest = call(
        prepare_kernel,
        "prepare",
        [kept(*sources.shape), kept(length + gathered, extent), kept(owners * length, extent)],
        [hbm],
        [vmem] * 3,
        scratch=[pltpu.SemaphoreType.DMA],
    )(in_hbm(sources))
    message, first = call(
        front_kernel,
        "front",
        [bf16(blocks * pair, extent), f32(8, extent)],
        [smem, vmem, vmem],
        [vmem] * 2,
        blocks=blocks,
        extent=extent,
    )(place, mine, from_core)
    order, sizes = call(
        list_kernel,
        "lists",
        [pltpu.SMEM((4, slots + UNROLL), jnp.int32), pltpu.SMEM((4,), jnp.int32)],
        [smem] * 4,
        [smem] * 2,
        blocks=blocks,
        owners=owners,
    )(place, in_hbm(tile_row.reshape(-1)), in_hbm(tile_col.reshape(-1)), tile_count.reshape(1))

    direct = [
        moved(message, lambda zz, xx, yy, cc, m=m: (cc * spans + (yy ^ m ^ (spans - 1)), xx, zz // 2, zz % 2))
        for m in range(spans)
    ]

    def early(trip, _):
        cols, line = call(
            edge_kernel,
            "edges",
            [f32(length, extent), f32(length + gathered, extent)],
            [smem] * 4 + [hbm, vmem],
            [vmem] * 2,
            scratch=[
                pltpu.VMEM((slots, SIDE_ROWS, extent), jnp.bfloat16),
                pltpu.VMEM((slots, extent, LANES), jnp.bfloat16),
                pltpu.VMEM((extent, LANES), jnp.float32),
                pltpu.SemaphoreType.DMA((slots,)),
                pltpu.SemaphoreType.DMA((slots,)),
            ],
            owners=owners,
        )(place, trip.reshape(1), order, sizes, stack, first)
        behind = [along_x(line, j) for j in range(1, owners)]
        return call(
            arrange_kernel,
            "arrange",
            [kept(*blank_walk.shape), kept(*blank_rest.shape)],
            [smem] + [vmem] * (1 + owners),
            [vmem] * 2,
        )(place, cols, line, *behind)

    walk, rest = apart(early, blank_walk, blank_rest)
    swapped = [along_x(after(piece, walk), j) for j in range(1, owners) for piece in direct]

    held_tiles = [
        pltpu.VMEM((slots + UNROLL, extent, extent), jnp.bfloat16),
        pltpu.SemaphoreType.DMA((slots + UNROLL,)),
    ]

    sum_shape, ahead_shape = (blocks + 1, *every), (AHEAD, extent, extent)
    later = [kept(*sum_shape), pltpu.VMEM(ahead_shape, jnp.bfloat16)]
    blank_sum, blank_ahead = call(blank_kernel, "blank", later, [unread], [vmem] * 2)(walk)

    def late(trip, state):
        walk, *_ = state
        near, ahead = call(
            near_kernel,
            "near",
            later,
            [smem] * 4 + [hbm] + [vmem] * len(direct),
            [vmem] * 2,
            scratch=[pltpu.VMEM((blocks, *every), jnp.bfloat16), *held_tiles, pltpu.SemaphoreType.DMA((AHEAD,))],
            blocks=blocks,
            spans=spans,
        )(place, trip.reshape(1), order, sizes, stack, *direct)
        for bit in reversed(range((n_row // owners).bit_length() - 1)):
            partner = moved(walk, lambda zz, xx, yy, cc, bit=bit: (zz ^ 2**bit, xx, yy, cc))
            walk = call(
                z_level_kernel, "z_level", kept(*walk.shape), [smem, vmem, vmem, unread], vmem, bit=bit, length=length
            )(place, walk, partner, near)
        return walk, near, ahead

    walk, near, ahead = apart(late, after(walk, *direct), blank_sum, blank_ahead)
    first_row, first_cols, firsts = call(
        coarse_kernel,
        "coarse",
        [f32(length, extent), f32(length, extent), f32(gathered, extent)],
        [smem, vmem, vmem],
        [vmem] * 3,
        blocks=blocks,
        rows=n_row,
    )(place, walk, rest)

    part = blocks * height
    keep, send, _ = call(
        far_kernel,
        "far",
        [f32(spans * part, extent), bf16(spans * part + length, extent), kept(*sum_shape)],
        [smem] * 3 + [hbm] + [vmem] * 4 + [unread] * len(direct) + [vmem] * len(swapped),
        [vmem] * 3,
        aliases={4: 2},
        scratch=[
            pltpu.VMEM(((owners - 1) * blocks, *every), jnp.bfloat16),
            *held_tiles,
            pltpu.VMEM((spans, blocks * pair, extent), jnp.bfloat16),
            pltpu.SemaphoreType.DMA((spans,)),
        ],
        blocks=blocks,
        owners=owners,
        spans=spans,
    )(place, order, sizes, stack, near, ahead, first_row, first_cols, *direct, *swapped)

    own, both, *outgoing = call(
        combine_kernel,
        "combine",
        [f32(part, extent), f32(2 * length, extent)] + [bf16(part + 2 * length, extent)] * (spans - 1),
        [smem, vmem, vmem, vmem],
        [vmem] * (spans + 1),
    )(place, keep, other_core(send), first_cols)
    arrived = [
        moved(value, lambda zz, xx, yy, cc, j=j: (zz, xx, (yy + j) % spans, cc)) for j, value in enumerate(outgoing, 1)
    ]
    return call(
        back_kernel,
        "back",
        f32(*sources.shape),
        [smem] + [vmem] * (2 + spans),
        vmem,
        blocks=blocks,
        owners=owners,
    )(place, own, both, firsts, *arrived)


def solution(mesh):
    return jax.shard_map(
        local,
        mesh=mesh,
        in_specs=(
            P("col", "row"),
            P("row", "col", None, None, None),
            P("row", "col", None),
            P("row", "col", None),
            P("row", "col"),
        ),
        out_specs=P("col", "row"),
        check_vma=False,
    )
```
